32 devices in a mesh: dp: 8 (over z, y), row: 2 (over core), col: 2 (over x).
Axes of the slice: x: 2, y: 2, z: 4, core: 2. Of those that a mesh axis runs over, the one named last changes fastest.
Arguments:
- layer_in: bfloat16 [8192, 1024], P('dp', ('row', 'col')), may hold values from -6 to 6
- lengths: int32 [8, 4], P('dp'), may hold values from 1 to 512, 1024 in all within a row
- placing: int32 [8, 1024], P('dp'), may hold values from 0 to 1023, each once within a row
- routes: int32 [8192, 2], P('dp'), may hold values from 0 to 3, all different within a row; in each aligned block of 1024 rows (0 to 1023, 1024 to 2047, ...) at most 640 rows name the same one
- cotangent: bfloat16 [8192, 1024], P('dp', ('row', 'col')), may hold values from -6 to 6
- norm_gains: float32 [2, 1024], P(None, ('row', 'col')), may hold values from 0.28 to 2.6, as said below
- gain_first: float32 [2, 1024], P(None, ('row', 'col')), may hold values from -512 to 512
- gain_second: float32 [2, 1024], P(None, ('row', 'col')), may hold values from 4096 to 65536
- rel_bias: float32 [32, 16], P(None, ('row', 'col')), may hold values from -6 to 6
- bias_first: float32 [32, 16], P(None, ('row', 'col')), may hold values from -256 to 256
- bias_second: float32 [32, 16], P(None, ('row', 'col')), may hold values from 1024 to 16384
- router: float32 [1024, 4], P(('row', 'col')), may hold values from -0.125 to 0.125
- router_first: float32 [1024, 4], P(('row', 'col')), may hold values from -5120 to 5120
- router_second: float32 [1024, 4], P(('row', 'col')), may hold values from 409600 to 6553600
- qkv_weight: float32 [2, 8, 64, 2, 3, 512], P('row', 'dp', None, None, None, 'col'), may hold values from -0.1875 to 0.1875
- qkv_first: float32 [2, 8, 64, 2, 3, 512], P('row', 'dp', None, None, None, 'col'), may hold values from -512 to 512
- qkv_second: float32 [2, 8, 64, 2, 3, 512], P('row', 'dp', None, None, None, 'col'), may hold values from 4096 to 65536
- proj_weight: float32 [2, 512, 2, 8, 64], P(None, 'col', 'row', 'dp'), may hold values from -0.5 to 0.5
- proj_first: float32 [2, 512, 2, 8, 64], P(None, 'col', 'row', 'dp'), may hold values from -160 to 160
- proj_second: float32 [2, 512, 2, 8, 64], P(None, 'col', 'row', 'dp'), may hold values from 368.64 to 5898.24
- expert_up: float32 [8, 1024, 2, 1408], P('dp', 'row', None, 'col'), may hold values from -0.1875 to 0.1875
- up_first: float32 [8, 1024, 2, 1408], P('dp', 'row', None, 'col'), may hold values from -192 to 192
- up_second: float32 [8, 1024, 2, 1408], P('dp', 'row', None, 'col'), may hold values from 512 to 8192
- expert_down: float32 [8, 1408, 1024], P('dp', 'col', 'row'), may hold values from -0.15625 to 0.15625
- down_first: float32 [8, 1408, 1024], P('dp', 'col', 'row'), may hold values from -96 to 96
- down_second: float32 [8, 1408, 1024], P('dp', 'col', 'row'), may hold values from 128 to 2048
Outputs:
- layer_out: bfloat16 [8192, 1024], P('dp', ('row', 'col'))
- input_grad: bfloat16 [8192, 1024], P('dp', ('row', 'col'))
- gains_new: float32 [2, 1024], P(None, ('row', 'col'))
- gains_moment: float32 [2, 1024], P(None, ('row', 'col'))
- gains_square: float32 [2, 1024], P(None, ('row', 'col'))
- bias_new: float32 [32, 16], P(None, ('row', 'col'))
- bias_moment: float32 [32, 16], P(None, ('row', 'col'))
- bias_square: float32 [32, 16], P(None, ('row', 'col'))
- router_new: float32 [1024, 4], P(('row', 'col'))
- router_moment: float32 [1024, 4], P(('row', 'col'))
- router_square: float32 [1024, 4], P(('row', 'col'))
- qkv_new: float32 [2, 8, 64, 2, 3, 512], P('row', 'dp', None, None, None, 'col')
- qkv_moment: float32 [2, 8, 64, 2, 3, 512], P('row', 'dp', None, None, None, 'col')
- qkv_square: float32 [2, 8, 64, 2, 3, 512], P('row', 'dp', None, None, None, 'col')
- qkv_copy: bfloat16 [2, 8, 64, 2, 3, 512], P('row', 'dp', None, None, None, 'col')
- proj_new: float32 [2, 512, 2, 8, 64], P(None, 'col', 'row', 'dp')
- proj_moment: float32 [2, 512, 2, 8, 64], P(None, 'col', 'row', 'dp')
- proj_square: float32 [2, 512, 2, 8, 64], P(None, 'col', 'row', 'dp')
- proj_copy: bfloat16 [2, 512, 2, 8, 64], P(None, 'col', 'row', 'dp')
- up_new: float32 [8, 1024, 2, 1408], P('dp', 'row', None, 'col')
- up_moment: float32 [8, 1024, 2, 1408], P('dp', 'row', None, 'col')
- up_square: float32 [8, 1024, 2, 1408], P('dp', 'row', None, 'col')
- up_copy: bfloat16 [8, 1024, 2, 1408], P('dp', 'row', None, 'col')
- down_new: float32 [8, 1408, 1024], P('dp', 'col', 'row')
- down_moment: float32 [8, 1408, 1024], P('dp', 'col', 'row')
- down_square: float32 [8, 1408, 1024], P('dp', 'col', 'row')
- down_copy: bfloat16 [8, 1408, 1024], P('dp', 'col', 'row')
The draws below stay inside these ranges and needn't reach their ends.
Inputs may be any that keep to these rules, and one draw needn't show every extreme that they name: `lengths`: each row sums to 1024; its largest entry is 512. `placing`: each row is a permutation. `routes`: each token names 2 different experts; among the tokens of one index of dp no expert is named more than 640 times, and in some index one expert is named exactly 640 times. `norm_gains`: positive gains.
All inputs are finite; a program needn't handle non-finite values.
Results may differ from the reference program's by a relative error of at most 0.025.
Values may be sent and summed in bfloat16 or wider, within the bound.
A program may use at most 256 MiB of HBM per device.

```python
import math
import jax
import jax.numpy as jnp
import numpy as np
from jax import lax

D = 1024
HEADS = 16
HD = 64
FF = 2816
TOP = 2
BUCKETS = 32
SEQS_DEV = 4
STEP = 5
TOK_DEV = 1024
LONGEST = 512
EXPERTS = 4
CAP = 640
TOKENS = 8192
N_DP = 8
N_ROW = 2


def draw_norm_gains(key, part):
    key = jax.random.fold_in(key, 7)
    along = jnp.arange(D, dtype=jnp.float32) / (D - 1)
    ramp = 0.6 + 1.2 * along
    rough = jax.random.uniform(key, (2, D), jnp.float32, 0.8, 1.2)
    return ramp[None, :] * rough


def level_of(key, extent, split, least, top_value):
    factor_of = 1.0
    for dim, parts in split:
        steps = jax.random.uniform(jax.random.fold_in(jax.random.fold_in(key, 6), dim), (parts,), jnp.float32, least / len(split), top_value / len(split))
        factor_of = factor_of * jnp.repeat(jnp.exp(steps), extent[dim] // parts).reshape((-1,) + (1,) * (len(extent) - 1 - dim))
    return factor_of


def profile(amount, total, bound, lean):
    weights = [(1 << 20) // math.isqrt(grade ** lean) + 1 for grade in range(2, amount + 1)]
    rest, holding = total - bound - (amount - 1), [1] * (amount - 1)
    while rest > 0:
        movable = [i for i in range(amount - 1) if holding[i] < bound]
        pool, left = sum([weights[i] for i in movable]), rest
        for i in movable:
            addition = min(bound - holding[i], max(1, left * weights[i] // pool), rest)
            holding[i] = holding[i] + addition
            rest = rest - addition
    return np.array([bound] + holding)


def ragged(rng, amount, total, limit, skew):
    if amount == 2:
        one = jax.random.randint(rng, (), max(1, total - limit), min(limit, total - 1) + 1)
        return jnp.stack([one, total - one])
    tallies = jnp.asarray(profile(amount, total, limit, skew), jnp.int32)
    twos = (amount - 1) // 2
    source_of, sink = tallies[1:1 + 2 * twos:2], tallies[2:2 + 2 * twos:2]
    slack = jnp.minimum(source_of - 1, limit - sink)
    shifted = jax.random.randint(jax.random.fold_in(rng, 1), (twos,), 0, 1 << 20) % (slack + 1)
    tallies = tallies.at[1:1 + 2 * twos:2].set(source_of - shifted).at[2:2 + 2 * twos:2].set(sink + shifted)
    return tallies[jax.random.permutation(jax.random.fold_in(rng, 2), amount)]


def routed_block(key, own, number, rows, amount, top, bound, skew):
    order = jax.random.permutation(key, amount)
    heavy_load, usual = load_shares(amount, rows * top, bound, skew, True), load_shares(amount, rows * top, bound, skew, False)
    places = jnp.arange(amount)

    def named(tallies, rotation):
        used = int((tallies > 0).sum())
        fixed = max(1, used // 4)
        moved = fixed + (places - fixed + rotation * (used - fixed)) % max(1, amount - fixed)
        return jnp.zeros((amount,), jnp.int32).at[order[jnp.where(places < fixed, places, moved)]].set(jnp.asarray(tallies, jnp.int32))

    tallies = jnp.where(number % 4 == 0, named(heavy_load, number // 4), named(usual, number - number // 4 - 1))
    mixed = jax.random.permutation(jax.random.fold_in(own, 3), amount)
    giver, sink = mixed[0:amount // 2 * 2:2], mixed[1:amount // 2 * 2:2]
    room = jnp.minimum(tallies[giver] - 1, bound - tallies[sink]) // 2
    room = jnp.where((giver == order[0]) | (sink == order[0]) | (tallies[sink] == 0), 0, jnp.maximum(room, 0))
    moved = jax.random.randint(jax.random.fold_in(own, 4), (amount // 2,), 0, 1 << 20) % (room + 1)
    tallies = tallies.at[giver].add(-moved).at[sink].add(moved)
    members = jnp.searchsorted(jnp.cumsum(tallies), jnp.arange(rows * top), side="right").astype(jnp.int32)
    table = members.reshape(top, rows).T
    table = table[jax.random.permutation(jax.random.fold_in(own, 1), rows)]
    rotation = jax.random.randint(jax.random.fold_in(own, 2), (rows, 1), 0, top)
    return jnp.take_along_axis(table, (jnp.arange(top)[None, :] + rotation) % top, axis=1)


def load_shares(amount, total, reach, skew, full):
    weights = [(1 << 20) // math.isqrt(standing ** skew) + 1 for standing in range(1, amount + 1)]
    largest = reach if full else min(reach, max(-(-total // amount), total * weights[0] // sum(weights)))
    least = 1 if total - largest >= amount - 1 else 0
    given, surplus = [largest] + [least] * (amount - 1), total - largest - least * (amount - 1)
    while surplus > 0:
        free = [i for i in range(1, amount) if given[i] < largest] or [i for i in range(1, amount) if given[i] < reach]
        whole, left = sum([weights[i] for i in free]), surplus
        for i in free:
            addition = min(reach - given[i], max(1, left * weights[i] // whole), surplus)
            given[i] = given[i] + addition
            surplus = surplus - addition
    return np.array(given)


def normal_values(stream_key, shape, deviation, most, cuts=(), kind=jnp.bfloat16):
    array = jax.random.normal(stream_key, shape, jnp.float32) * deviation
    if len(cuts) > 0:
        array = level_of(stream_key, shape, cuts, -0.22, 0.18) * array
    return jnp.clip(array, min=-most, max=most).astype(kind)


def setup_inputs(seed: int = 0) -> dict:
    seeds = jax.random.split(jax.random.key(seed), 27)
    layer_in = normal_values(seeds[0], (TOKENS, D), 1.0, 6.0, ((0, 8), (1, 4)))
    lengths = jax.vmap(lambda own: ragged(own, SEQS_DEV, TOK_DEV, LONGEST, 2))(jax.random.split(seeds[1], N_DP)).reshape((N_DP, SEQS_DEV)).astype(jnp.int32)
    placing = jax.vmap(lambda own: jax.random.permutation(own, TOK_DEV))(jax.random.split(seeds[2], N_DP)).reshape((N_DP, TOK_DEV)).astype(jnp.int32)
    routes_keys = jax.random.split(jax.random.fold_in(seeds[3], 1), TOKENS // TOK_DEV)
    routes_turns = jax.random.permutation(jax.random.fold_in(seeds[3], 3), TOKENS // TOK_DEV)
    routes = jax.vmap(lambda own, number: routed_block(jax.random.fold_in(seeds[3], 2), own, number, TOK_DEV, EXPERTS, TOP, CAP, 1))(routes_keys, routes_turns).reshape((TOKENS, TOP))
    cotangent = normal_values(seeds[4], (TOKENS, D), 1.0, 6.0, ((0, 8), (1, 4)))
    norm_gains = draw_norm_gains(jax.random.fold_in(seeds[26], 71), 0)
    gain_first = normal_values(seeds[6], (2, D), (TOKENS ** 0.5), 512.0, ((1, 4),), jnp.float32)
    gain_second = jnp.clip(jnp.exp(math.log(65536.0) - 2.7725887 * jax.random.uniform(seeds[7], (2, D), jnp.float32) ** level_of(seeds[7], (2, D), ((1, 4),), -0.2, 0.2)), 4096.0, 65536.0)
    rel_bias = normal_values(seeds[8], (BUCKETS, HEADS), 1.0, 6.0, ((1, 4),), jnp.float32)
    bias_first = normal_values(seeds[9], (BUCKETS, HEADS), (0.5 * TOKENS ** 0.5), 256.0, ((1, 4),), jnp.float32)
    bias_second = jnp.clip(jnp.exp(math.log(16384.0) - 2.7725887 * jax.random.uniform(seeds[10], (BUCKETS, HEADS), jnp.float32) ** level_of(seeds[10], (BUCKETS, HEADS), ((1, 4),), -0.2, 0.2)), 1024.0, 16384.0)
    router = normal_values(seeds[11], (D, EXPERTS), (2 * D) ** -0.5, 0.125, ((0, 4),), jnp.float32)
    router_first = normal_values(seeds[12], (D, EXPERTS), (10 * TOKENS ** 0.5), 5120.0, ((0, 4),), jnp.float32)
    router_second = jnp.clip(jnp.exp(math.log(6553600) - 2.7725887 * jax.random.uniform(seeds[13], (D, EXPERTS), jnp.float32) ** level_of(seeds[13], (D, EXPERTS), ((0, 4),), -0.2, 0.2)), 409600.0, 6553600)
    qkv_weight = normal_values(seeds[14], (N_ROW, N_DP, D // (N_ROW * N_DP), N_ROW, 3, HEADS * HD // N_ROW), D ** -0.5, 0.1875, ((0, 2), (1, 8), (5, 2)), jnp.float32)
    qkv_first = normal_values(seeds[15], (N_ROW, N_DP, D // (N_ROW * N_DP), N_ROW, 3, HEADS * HD // N_ROW), (TOKENS ** 0.5), 512.0, ((0, 2), (1, 8), (5, 2)), jnp.float32)
    qkv_second = jnp.clip(jnp.exp(math.log(65536.0) - 2.7725887 * jax.random.uniform(seeds[16], (N_ROW, N_DP, D // (N_ROW * N_DP), N_ROW, 3, HEADS * HD // N_ROW), jnp.float32) ** level_of(seeds[16], (N_ROW, N_DP, D // (N_ROW * N_DP), N_ROW, 3, HEADS * HD // N_ROW), ((0, 2), (1, 8), (5, 2)), -0.2, 0.2)), 4096.0, 65536.0)
    proj_weight = normal_values(seeds[17], (N_ROW, HEADS * HD // N_ROW, N_ROW, N_DP, D // (N_ROW * N_DP)), (HEADS * HD // 8) ** -0.5, 0.5, ((1, 2), (2, 2), (3, 8)), jnp.float32)
    proj_first = normal_values(seeds[18], (N_ROW, HEADS * HD // N_ROW, N_ROW, N_DP, D // (N_ROW * N_DP)), (0.3 * TOKENS ** 0.5), 160.0, ((1, 2), (2, 2), (3, 8)), jnp.float32)
    proj_second = jnp.clip(jnp.exp(math.log(5898.24) - 2.7725887 * jax.random.uniform(seeds[19], (N_ROW, HEADS * HD // N_ROW, N_ROW, N_DP, D // (N_ROW * N_DP)), jnp.float32) ** level_of(seeds[19], (N_ROW, HEADS * HD // N_ROW, N_ROW, N_DP, D // (N_ROW * N_DP)), ((1, 2), (2, 2), (3, 8)), -0.2, 0.2)), 368.64, 5898.24)
    expert_up = normal_values(seeds[20], (N_DP, D, 2, FF // 2), D ** -0.5, 0.1875, ((0, 8), (1, 2), (3, 2)), jnp.float32)
    up_first = normal_values(seeds[21], (N_DP, D, 2, FF // 2), (TOK_DEV ** 0.5), 192.0, ((0, 8), (1, 2), (3, 2)), jnp.float32)
    up_second = jnp.clip(jnp.exp(math.log(8192.0) - 2.7725887 * jax.random.uniform(seeds[22], (N_DP, D, 2, FF // 2), jnp.float32) ** level_of(seeds[22], (N_DP, D, 2, FF // 2), ((0, 8), (1, 2), (3, 2)), -0.2, 0.2)), 512.0, 8192.0)
    expert_down = normal_values(seeds[23], (N_DP, FF // 2, D), (FF // 2) ** -0.5, 0.15625, ((0, 8), (1, 2), (2, 2)), jnp.float32)
    down_first = normal_values(seeds[24], (N_DP, FF // 2, D), (0.5 * TOK_DEV ** 0.5), 96.0, ((0, 8), (1, 2), (2, 2)), jnp.float32)
    down_second = jnp.clip(jnp.exp(math.log(2048.0) - 2.7725887 * jax.random.uniform(seeds[25], (N_DP, FF // 2, D), jnp.float32) ** level_of(seeds[25], (N_DP, FF // 2, D), ((0, 8), (1, 2), (2, 2)), -0.2, 0.2)), 128.0, 2048.0)
    return dict(layer_in=layer_in, lengths=lengths, placing=placing, routes=routes, cotangent=cotangent, norm_gains=norm_gains, gain_first=gain_first, gain_second=gain_second, rel_bias=rel_bias, bias_first=bias_first, bias_second=bias_second, router=router, router_first=router_first, router_second=router_second, qkv_weight=qkv_weight, qkv_first=qkv_first, qkv_second=qkv_second, proj_weight=proj_weight, proj_first=proj_first, proj_second=proj_second, expert_up=expert_up, up_first=up_first, up_second=up_second, expert_down=expert_down, down_first=down_first, down_second=down_second)


@jax.custom_vjp
def low(v):
    return lax.optimization_barrier(v.astype(jnp.bfloat16)).astype(jnp.float32)

@jax.custom_vjp
def low_back(v):
    return v

def low_keep(v):
    return (low(v), None)

def low_pass(kept, grad):
    return (grad,)

def back_keep(v):
    return (v, None)

def back_low(kept, grad):
    return (low(grad),)
low.defvjp(low_keep, low_pass)
low_back.defvjp(back_keep, back_low)
bucket_edges = np.floor(16.0 * 2.0 ** (np.arange(16) * 0.375)).astype(np.int32)
norm_epsilon = 1e-06
beta_first = 0.5
beta_second = 0.5
adam_epsilon = 1e-08
weight_decay = 0.01
highest = lax.Precision.HIGHEST

def bucket_of(distance):
    counted = jnp.zeros_like(distance)
    for edge_value in bucket_edges:
        counted = counted + (distance >= int(edge_value)).astype(jnp.int32)
    return jnp.where(distance < 16, distance, 15 + counted)

def rms_norm(resid, gain):
    inverse = lax.rsqrt(lax.optimization_barrier(jnp.mean(resid * resid, axis=-1, keepdims=True)) + norm_epsilon)
    return resid * inverse * gain

def sequence_ids(seq_lengths, length_all):
    ends = jnp.cumsum(seq_lengths)
    places = jnp.arange(length_all, dtype=jnp.int32)
    return lax.optimization_barrier(jnp.sum((places[:, None] >= ends[None, :]).astype(jnp.int32), axis=1))

def attend_device(resid, seq_lengths, qkv_matrix, proj_matrix, bias_table, gain_rows):
    length_all = resid.shape[0]
    features = low(rms_norm(resid, gain_rows[0]))
    qkv_all = jnp.einsum('td,dnkh->tnkh', features, qkv_matrix, precision=highest)
    qkv_all = low(low_back(qkv_all))
    heads_all = qkv_all.reshape(length_all, N_ROW, 3, HEADS // N_ROW, HD)
    queries = heads_all[:, :, 0].reshape(length_all, HEADS, HD)
    key_rows = heads_all[:, :, 1].reshape(length_all, HEADS, HD)
    value_rows = heads_all[:, :, 2].reshape(length_all, HEADS, HD)
    places = jnp.arange(length_all, dtype=jnp.int32)
    distance = places[:, None] - places[None, :]
    rel_terms = jnp.transpose(bias_table[bucket_of(jnp.maximum(distance, 0))], (2, 0, 1))
    scores = jnp.einsum('qhd,khd->hqk', queries, key_rows, precision=highest) * HD ** (-0.5) + rel_terms
    scores = low_back(scores)
    sequence = sequence_ids(seq_lengths, length_all)
    visible = (sequence[:, None] == sequence[None, :]) & (distance >= 0)
    attn_probs = jax.nn.softmax(jnp.where(visible[None], scores, -1e+30), axis=-1)
    attended = jnp.einsum('hqk,khd->qhd', low(attn_probs), value_rows, precision=highest)
    attended = low(low_back(attended.reshape(length_all, N_ROW, HEADS * HD // N_ROW)))
    branch = low_back(jnp.einsum('tnh,nhd->td', attended, proj_matrix, precision=highest))
    second = resid + branch
    return (second, low(rms_norm(second, gain_rows[1])))

def expert_pair(slot_rows, up_pair, down_pair):
    summed = jnp.zeros((slot_rows.shape[0], D), jnp.float32)
    for half_index in range(2):
        entering = low_back(slot_rows)
        hidden = low_back(jnp.einsum('sd,dgf->sgf', entering, up_pair[half_index], precision=highest))
        active = low(jax.nn.gelu(hidden[:, 0], approximate=True) * hidden[:, 1])
        summed = summed + low(low_back(jnp.dot(active, down_pair[half_index], precision=highest)))
    return summed

def slot_table(routes):
    per_device = routes.reshape(N_DP, TOK_DEV * TOP)
    route_hits = (per_device[:, :, None] == jnp.arange(EXPERTS, dtype=jnp.int32)[None, None, :]).astype(jnp.int32)
    before = jnp.cumsum(route_hits, axis=1) - route_hits
    position = lax.optimization_barrier(jnp.sum(before * route_hits, axis=2))
    slot_ids = jnp.arange(N_DP, dtype=jnp.int32)[:, None] * CAP + position
    token_ids = jnp.arange(TOKENS * TOP, dtype=jnp.int32).reshape(N_DP, TOK_DEV * TOP) // TOP
    slot_lookup = jnp.full((EXPERTS, N_DP * CAP), TOKENS, jnp.int32)
    slot_lookup = slot_lookup.at[per_device.reshape(-1), slot_ids.reshape(-1)].set(token_ids.reshape(-1))
    target = (per_device * (N_DP * CAP) + slot_ids).reshape(TOKENS, TOP)
    return (slot_lookup, target)

def adamw_step(weight, grad, first, second, rate):
    first_new = beta_first * first + (1.0 - beta_first) * grad
    second_new = beta_second * second + (1.0 - beta_second) * grad * grad
    moment = first_new / (1.0 - beta_first ** STEP)
    spread = second_new / (1.0 - beta_second ** STEP)
    weight_new = weight - rate * (moment / (jnp.sqrt(spread) + adam_epsilon) + weight_decay * weight)
    return (weight_new, first_new, second_new)

def reference(layer_in, lengths, placing, routes, cotangent, norm_gains, gain_first, gain_second, rel_bias, bias_first, bias_second, router, router_first, router_second, qkv_weight, qkv_first, qkv_second, proj_weight, proj_first, proj_second, expert_up, up_first, up_second, expert_down, down_first, down_second):
    qkv_matrix = qkv_weight.astype(jnp.bfloat16).astype(jnp.float32).reshape(D, N_ROW, 3, HEADS * HD // N_ROW)
    proj_matrix = proj_weight.astype(jnp.bfloat16).astype(jnp.float32).reshape(N_ROW, HEADS * HD // N_ROW, D)
    up_matrix = expert_up.astype(jnp.bfloat16).astype(jnp.float32)
    down_matrix = expert_down.astype(jnp.bfloat16).astype(jnp.float32)
    inputs_all = layer_in.astype(jnp.float32).reshape(N_DP, TOK_DEV, D)
    placed = jnp.take_along_axis(inputs_all, placing[:, :, None], axis=1).reshape(TOKENS, D)
    grads_all = cotangent.astype(jnp.float32).reshape(N_DP, TOK_DEV, D)
    grad_out = jnp.take_along_axis(grads_all, placing[:, :, None], axis=1).reshape(TOKENS, D)
    slot_lookup, target = slot_table(routes)

    def layer(placed_rows, qkv_mat, proj_mat, router_matrix, bias_table, gain_rows, up_mat, down_mat):
        step_attend = jax.checkpoint(attend_device)
        second, mixed_in = lax.map(lambda both_args: step_attend(both_args[0], both_args[1], qkv_mat, proj_mat, bias_table, gain_rows), (placed_rows.reshape(N_DP, TOK_DEV, D), lengths))
        second = second.reshape(TOKENS, D)
        mixed_in = mixed_in.reshape(TOKENS, D)
        logits = jnp.dot(mixed_in, router_matrix, precision=highest)
        gate_values = jax.nn.softmax(jnp.take_along_axis(logits, routes, axis=1), axis=1)
        padded = jnp.concatenate([mixed_in, jnp.zeros((1, D), jnp.float32)], axis=0)

        def one_expert(number):
            slot_rows = padded[slot_lookup[number]]
            up_pair = lax.dynamic_slice_in_dim(up_mat, 2 * number, 2, 0)
            down_pair = lax.dynamic_slice_in_dim(down_mat, 2 * number, 2, 0)
            return expert_pair(slot_rows, up_pair, down_pair)
        outputs = lax.map(jax.checkpoint(one_expert), jnp.arange(EXPERTS, dtype=jnp.int32))
        picked = outputs.reshape(-1, D)[target]
        return second + lax.optimization_barrier(jnp.sum(gate_values[:, :, None] * picked, axis=1))
    third, pull = jax.vjp(layer, placed, qkv_matrix, proj_matrix, router, rel_bias, norm_gains, up_matrix, down_matrix)
    grad_placed, grad_qkv, grad_proj, grad_router, grad_bias, grad_gains, grad_up, grad_down = pull(grad_out)
    unplace = jax.vmap(lambda rows_here, perm_here: jnp.zeros_like(rows_here).at[perm_here].set(rows_here))
    layer_out = unplace(third.astype(jnp.bfloat16).reshape(N_DP, TOK_DEV, D), placing).reshape(TOKENS, D)
    input_grad = unplace(grad_placed.astype(jnp.bfloat16).reshape(N_DP, TOK_DEV, D), placing).reshape(TOKENS, D)
    gains_new, gains_moment, gains_square = adamw_step(norm_gains, grad_gains, gain_first, gain_second, 0.5)
    bias_new, bias_moment, bias_square = adamw_step(rel_bias, grad_bias, bias_first, bias_second, 1.0)
    router_new, router_moment, router_square = adamw_step(router, grad_router, router_first, router_second, 2.0 * (2 * D) ** (-0.5))
    qkv_new, qkv_moment, qkv_square = adamw_step(qkv_weight, grad_qkv.reshape(qkv_weight.shape), qkv_first, qkv_second, 2.0 * D ** (-0.5))
    proj_new, proj_moment, proj_square = adamw_step(proj_weight, grad_proj.reshape(proj_weight.shape), proj_first, proj_second, 2.0 * (HEADS * HD / 8) ** (-0.5))
    up_new, up_moment, up_square = adamw_step(expert_up, grad_up, up_first, up_second, 2.0 * D ** (-0.5))
    down_new, down_moment, down_square = adamw_step(expert_down, grad_down, down_first, down_second, 2.0 * (FF / 2) ** (-0.5))
    return (layer_out, input_grad, gains_new, gains_moment, gains_square, bias_new, bias_moment, bias_square, router_new, router_moment, router_square, qkv_new, qkv_moment, qkv_square, qkv_new.astype(jnp.bfloat16), proj_new, proj_moment, proj_square, proj_new.astype(jnp.bfloat16), up_new, up_moment, up_square, up_new.astype(jnp.bfloat16), down_new, down_moment, down_square, down_new.astype(jnp.bfloat16))
```

```python
import functools

import jax
import jax.numpy as jnp
import numpy as np
from jax import lax
from jax.experimental import pallas as pl
from jax.experimental.pallas import tpu as pltpu
from jax.sharding import Mesh, PartitionSpec as P

D = 1024
HEADS = 16
FF = 2816
TOP = 2
STEP = 5
beta_first = 0.5
beta_second = 0.5
adam_epsilon = 1e-08
weight_decay = 0.01
highest = lax.Precision.HIGHEST
EXTRA = 16
HD = 64
BUCKETS = 32
LONGEST = 512
TILE = 256
norm_epsilon = 1e-06
hidden_score = -1e30
bucket_edges = np.floor(16.0 * 2.0 ** (np.arange(16) * 0.375)).astype(np.int32)
f32 = jnp.float32
bf16 = jnp.bfloat16
MIB = 1 << 20


def dot_nn(a, b):
    return lax.dot_general(a, b, (((1,), (0,)), ((), ())), preferred_element_type=f32)


def dot_nt(a, b):
    return lax.dot_general(a, b, (((1,), (1,)), ((), ())), preferred_element_type=f32)


def dot_tn(a, b):
    return lax.dot_general(a, b, (((0,), (0,)), ((), ())), preferred_element_type=f32)


def tile_reach(tokens):
    return min(tokens // TILE, (LONGEST - 1 + TILE - 1) // TILE + 1)


def toeplitz_places(tokens):
    reach = tile_reach(tokens)
    m = np.arange(2 * TILE)
    base = np.where(m < TILE, -m, 2 * TILE - m)
    distance = np.arange(reach)[:, None] * TILE + base[None, :]
    clipped = np.maximum(distance, 0)
    buckets = np.where(
        clipped < 16, clipped, 15 + (clipped[..., None] >= bucket_edges).sum(-1)
    )
    return (distance, buckets)


def bias_vectors(rel_bias, tokens):
    distance, buckets = toeplitz_places(tokens)
    table = jnp.asarray((buckets[..., None] == np.arange(BUCKETS)).astype(np.float32))
    values = jnp.einsum("dmb,bh->hdm", table, rel_bias, precision=lax.Precision.HIGHEST)
    values = jnp.where(jnp.asarray(distance < 0)[None], hidden_score, values)
    return values.reshape(-1, 2 * TILE)


def bias_gradient(vectors, head_count, tokens):
    distance, buckets = toeplitz_places(tokens)
    table = ((buckets[..., None] == np.arange(BUCKETS)) & (distance >= 0)[..., None]).astype(np.float32)
    return jnp.einsum(
        "dmb,hdm->bh",
        jnp.asarray(table),
        vectors.reshape(head_count, distance.shape[0], 2 * TILE),
        precision=lax.Precision.HIGHEST,
    )


def fill_bias(vector_ref, bias):
    for i in range(bias.shape[0]):
        wide = jnp.broadcast_to(vector_ref[i : i + 1, :], (TILE, 2 * TILE))
        bias[i] = pltpu.roll(wide, 0, 1, stride=1, stride_axis=0)[:, :TILE]


def head_lanes(shape, head):
    return lax.broadcasted_iota(jnp.int32, shape, 1) // HD == head


def attention_forward_kernel(
    x_ref, gain_ref, weight_ref, place_row, place_col, start_ref, vector_ref,
    first_ref, qkv_ref, attended_ref, lse_ref, bias, placed_out,
):
    quarters, tokens, part = x_ref.shape
    width = quarters * part
    hc = weight_ref.shape[1] // 3
    head_count = hc // HD
    reach = bias.shape[0] // head_count
    fill_bias(vector_ref, bias)
    squares = jnp.zeros((tokens, 1), f32)
    for q in range(quarters):
        v = x_ref[q].astype(f32)
        squares = squares + jnp.sum(v * v, axis=1, keepdims=True)
    inverse = lax.rsqrt(squares / width + norm_epsilon)
    total = jnp.zeros((tokens, 3 * hc), f32)
    for q in range(quarters):
        first = (x_ref[q].astype(f32) * inverse * gain_ref[q]).astype(bf16)
        first_ref[q] = first
        total = total + dot_nn(first, weight_ref[q * part : (q + 1) * part, :])
    to_placed = jnp.where(
        place_col[...] == lax.broadcasted_iota(jnp.int32, (tokens, tokens), 1), 1.0, 0.0
    ).astype(bf16)
    scale = jnp.where(
        lax.broadcasted_iota(jnp.int32, (1, 3 * hc), 1) < hc, HD ** (-0.5), 1.0
    )
    qkv_ref[...] = dot_nn(to_placed, (total * scale).astype(bf16)).astype(bf16)
    for a in range(tokens // TILE):
        rows = slice(a * TILE, (a + 1) * TILE)
        blocks = range(max(0, a - reach + 1), a + 1)
        starts = start_ref[rows, :]
        visible = [
            b * TILE + lax.broadcasted_iota(jnp.int32, (TILE, TILE), 1) >= starts for b in blocks
        ]

        def one_head(head, carry):
            out, lse = carry
            mine = head_lanes((TILE, hc), head)
            query = jnp.where(mine, qkv_ref[rows, :hc], 0)
            scores = []
            for b, seen in zip(blocks, visible):
                s = dot_nt(query, qkv_ref[b * TILE : (b + 1) * TILE, hc : 2 * hc])
                scores.append(jnp.where(seen, s + bias[head * reach + a - b], hidden_score))
            top = functools.reduce(jnp.maximum, [jnp.max(s, axis=1, keepdims=True) for s in scores])
            exps = [jnp.exp(s - top) for s in scores]
            denominator = functools.reduce(jnp.add, [jnp.sum(e, axis=1, keepdims=True) for e in exps])
            share = 1.0 / denominator
            value = jnp.zeros((TILE, hc), f32)
            for b, e in zip(blocks, exps):
                value = value + dot_nn(
                    (e * share).astype(bf16), qkv_ref[b * TILE : (b + 1) * TILE, 2 * hc :]
                )
            lane = lax.broadcasted_iota(jnp.int32, (TILE, 128), 1)
            return (
                jnp.where(mine, value, out),
                jnp.where(lane == head, top + jnp.log(denominator), lse),
            )

        out, lse = lax.fori_loop(
            0, head_count, one_head, (jnp.zeros((TILE, hc), f32), jnp.zeros((TILE, 128), f32))
        )
        placed_out[rows, :] = out.astype(bf16)
        lse_ref[rows, :] = lse
    to_given = jnp.where(
        place_row[...] == lax.broadcasted_iota(jnp.int32, (tokens, tokens), 0), 1.0, 0.0
    ).astype(bf16)
    attended_ref[...] = dot_nn(to_given, placed_out[...]).astype(bf16)


def vmem():
    return pl.BlockSpec(memory_space=pltpu.VMEM)


def attention_forward(x, gain, weight, place_row, place_col, starts, vectors):
    quarters, tokens, part = x.shape
    hc = weight.shape[1] // 3
    return pl.pallas_call(
        attention_forward_kernel,
        out_shape=(
            jax.ShapeDtypeStruct(x.shape, bf16),
            jax.ShapeDtypeStruct((tokens, 3 * hc), bf16),
            jax.ShapeDtypeStruct((tokens, hc), bf16),
            jax.ShapeDtypeStruct((tokens, 128), f32),
        ),
        in_specs=[vmem()] * 7,
        out_specs=(vmem(),) * 4,
        scratch_shapes=[
            pltpu.VMEM((vectors.shape[0], TILE, TILE), f32),
            pltpu.VMEM((tokens, hc), bf16),
        ],
        compiler_params=pltpu.CompilerParams(vmem_limit_bytes=48 * MIB),
        name="attention_forward",
    )(x, gain, weight, place_row, place_col, starts, vectors)


def attention_backward_kernel(
    branch_ref, proj_ref, qkv_ref, lse_ref, attended_ref, first_ref, weight_ref,
    place_row, place_col, start_ref, vector_ref,
    dfirst_ref, dweight_ref, dproj_ref, dvector_ref,
    bias, dbias, grad_ref, dqkv, dkv,
):
    quarters, tokens, part = branch_ref.shape
    hc = weight_ref.shape[1] // 3
    head_count = hc // HD
    reach = bias.shape[0] // head_count
    fill_bias(vector_ref, bias)
    dbias[...] = jnp.zeros_like(dbias)
    dkv[...] = jnp.zeros_like(dkv)
    total = jnp.zeros((tokens, hc), f32)
    for q in range(quarters):
        total = total + dot_nn(branch_ref[q], proj_ref[q * part : (q + 1) * part, :])
        dproj_ref[q * part : (q + 1) * part, :] = dot_tn(branch_ref[q], attended_ref[...]).astype(bf16)
    to_placed = jnp.where(
        place_col[...] == lax.broadcasted_iota(jnp.int32, (tokens, tokens), 1), 1.0, 0.0
    ).astype(bf16)
    grad_ref[...] = dot_nn(to_placed, total.astype(bf16)).astype(bf16)
    for a in range(tokens // TILE):
        rows = slice(a * TILE, (a + 1) * TILE)
        blocks = range(max(0, a - reach + 1), a + 1)
        starts = start_ref[rows, :]
        visible = [
            b * TILE + lax.broadcasted_iota(jnp.int32, (TILE, TILE), 1) >= starts for b in blocks
        ]

        def one_head(head, dquery):
            mine = head_lanes((TILE, hc), head)
            query = jnp.where(mine, qkv_ref[rows, :hc], 0)
            grad = jnp.where(mine, grad_ref[rows, :], 0)
            lane = lax.broadcasted_iota(jnp.int32, (TILE, 128), 1)
            lse = jnp.sum(jnp.where(lane == head, lse_ref[rows, :], 0.0), axis=1, keepdims=True)
            probs, dprobs = [], []
            inner = jnp.zeros((TILE, 1), f32)
            for b, seen in zip(blocks, visible):
                keys = slice(b * TILE, (b + 1) * TILE)
                s = dot_nt(query, qkv_ref[keys, hc : 2 * hc]) + bias[head * reach + a - b]
                p = jnp.where(seen, jnp.exp(s - lse), 0.0)
                d = dot_nt(grad, qkv_ref[keys, 2 * hc :])
                inner = inner + jnp.sum(p * d, axis=1, keepdims=True)
                probs.append(p)
                dprobs.append(d)
            for b, p, d in zip(blocks, probs, dprobs):
                keys = slice(b * TILE, (b + 1) * TILE)
                ds = p * (d - inner)
                place = head * reach + a - b
                dbias[place] = dbias[place] + ds
                low = ds.astype(bf16)
                dquery = dquery + dot_nn(low, jnp.where(mine, qkv_ref[keys, hc : 2 * hc], 0))
                dkv[keys, :hc] = dkv[keys, :hc] + dot_tn(low, query)
                dkv[keys, hc:] = dkv[keys, hc:] + dot_tn(p.astype(bf16), grad)
            return dquery

        dquery = lax.fori_loop(0, head_count, one_head, jnp.zeros((TILE, hc), f32))
        dqkv[rows, :hc] = (dquery * HD ** (-0.5)).astype(bf16)
    dqkv[:, hc:] = dkv[...].astype(bf16)
    for i in range(dbias.shape[0]):
        wide = jnp.concatenate([dbias[i], jnp.zeros((TILE, TILE), f32)], axis=1)
        level = wide[:8]
        for g in range(8, TILE, 8):
            level = level + pltpu.roll(wide[g : g + 8], 2 * TILE - g, 1)
        row = level[:1]
        for s in range(1, 8):
            row = row + pltpu.roll(level[s : s + 1], 2 * TILE - s, 1)
        dvector_ref[i : i + 1, :] = row
    to_given = jnp.where(
        place_row[...] == lax.broadcasted_iota(jnp.int32, (tokens, tokens), 0), 1.0, 0.0
    ).astype(bf16)
    given = dot_nn(to_given, dqkv[...]).astype(bf16)
    for q in range(quarters):
        dims = slice(q * part, (q + 1) * part)
        dfirst_ref[q] = dot_nt(given, weight_ref[dims, :]).astype(bf16)
        dweight_ref[dims, :] = dot_tn(first_ref[q], given).astype(bf16)


def attention_backward(branch, proj, qkv, lse, attended, first, weight, place_row, place_col, starts, vectors):
    quarters, tokens, part = branch.shape
    hc = weight.shape[1] // 3
    return pl.pallas_call(
        attention_backward_kernel,
        out_shape=(
            jax.ShapeDtypeStruct(branch.shape, bf16),
            jax.ShapeDtypeStruct(weight.shape, bf16),
            jax.ShapeDtypeStruct(proj.shape, bf16),
            jax.ShapeDtypeStruct(vectors.shape, f32),
        ),
        in_specs=[vmem()] * 11,
        out_specs=(vmem(),) * 4,
        scratch_shapes=[
            pltpu.VMEM((vectors.shape[0], TILE, TILE), f32),
            pltpu.VMEM((vectors.shape[0], TILE, TILE), f32),
            pltpu.VMEM((tokens, hc), bf16),
            pltpu.VMEM((tokens, 3 * hc), bf16),
            pltpu.VMEM((tokens, 2 * hc), f32),
        ],
        compiler_params=pltpu.CompilerParams(vmem_limit_bytes=56 * MIB),
        name="attention_backward",
    )(branch, proj, qkv, lse, attended, first, weight, place_row, place_col, starts, vectors)


def half_places(rows, part):
    row = lax.broadcasted_iota(jnp.int32, (rows, EXTRA), 0) // part
    high = lax.broadcasted_iota(jnp.int32, (rows, EXTRA), 1)
    column = lax.broadcasted_iota(jnp.int32, (rows, part), 0) % part
    return (row, high, column == lax.broadcasted_iota(jnp.int32, (rows, part), 1))


def write_extra(values, part):
    row, high, column = half_places(values.shape[0], part)
    near = values.astype(bf16)
    left = (values - near.astype(f32)).astype(bf16)
    near_rows = jnp.where(row == high, 1.0, 0.0).astype(bf16)
    left_rows = jnp.where(row + 8 == high, 1.0, 0.0).astype(bf16)
    near_values = jnp.where(column, near.astype(f32), 0.0).astype(bf16)
    left_values = jnp.where(column, left.astype(f32), 0.0).astype(bf16)
    return dot_tn(near_rows, near_values) + dot_tn(left_rows, left_values)


def read_extra(extra, rows):
    part = extra.shape[1]
    row, high, column = half_places(rows, part)
    pick = jnp.where(row == high % 8, 1.0, 0.0).astype(bf16)
    return jnp.sum(jnp.where(column, dot_nn(pick, extra), 0.0), axis=1, keepdims=True)


GELU_A = 0.7978845608028654
GELU_B = 0.044715


def expert_kernel(x_ref, g_ref, up_ref, down_ref, dx_ref, y_ref, dup_ref, ddown_ref):
    quarters, _, cap, part = g_ref.shape
    x = jnp.concatenate([x_ref[q, 0, :cap] for q in range(quarters)], axis=1)
    grad = jnp.concatenate([g_ref[q, 0] for q in range(quarters)], axis=1)
    gate = read_extra(x_ref[0, 0, cap:], cap)
    a = dot_nn(x, up_ref[0])
    b = dot_nn(x, up_ref[1])
    t = jnp.tanh(GELU_A * (a + GELU_B * (a * a * a)))
    smooth = 0.5 * a * (1.0 + t)
    slope = 0.5 * (1.0 + t) + (0.5 * GELU_A) * a * (1.0 - t * t) * (1.0 + (3.0 * GELU_B) * (a * a))
    active = smooth * b
    dact = dot_nt(grad, down_ref[...]) * gate
    da = (dact * b * slope).astype(bf16)
    db = (dact * smooth).astype(bf16)
    low = active.astype(bf16)
    dx = dot_nt(da, up_ref[0]) + dot_nt(db, up_ref[1])
    extra = write_extra(jnp.sum(dact * active, axis=1, keepdims=True), part)
    y = dot_nn(low, down_ref[...])
    for q in range(quarters):
        dims = slice(q * part, (q + 1) * part)
        dx_ref[q, 0, :cap] = dx[:, dims].astype(bf16)
        dx_ref[q, 0, cap:] = extra.astype(bf16)
        y_ref[q, 0] = y[:, dims].astype(bf16)
    scaled = (active * gate).astype(bf16)

    @pl.when(pl.program_id(0) == 0)
    def _():
        dup_ref[0] = dot_tn(x, da)
        dup_ref[1] = dot_tn(x, db)
        ddown_ref[...] = dot_tn(scaled, grad)

    @pl.when(pl.program_id(0) > 0)
    def _():
        dup_ref[0] = dup_ref[0] + dot_tn(x, da)
        dup_ref[1] = dup_ref[1] + dot_tn(x, db)
        ddown_ref[...] = ddown_ref[...] + dot_tn(scaled, grad)


def expert_block(x, grads, up, down):
    quarters, sources, cap, part = grads.shape
    ext = x.shape[2]
    ff = down.shape[0]
    whole = lambda shape: pl.BlockSpec(shape, lambda i: (0,) * len(shape))
    rows = lambda n: pl.BlockSpec((quarters, 1, n, part), lambda i: (0, i, 0, 0))
    return pl.pallas_call(
        expert_kernel,
        grid=(sources,),
        out_shape=(
            jax.ShapeDtypeStruct(x.shape, bf16),
            jax.ShapeDtypeStruct(grads.shape, bf16),
            jax.ShapeDtypeStruct(up.shape, f32),
            jax.ShapeDtypeStruct(down.shape, f32),
        ),
        in_specs=[rows(ext), rows(cap), whole(up.shape), whole(down.shape)],
        out_specs=(rows(ext), rows(cap), whole(up.shape), whole(down.shape)),
        compiler_params=pltpu.CompilerParams(vmem_limit_bytes=60 * MIB),
        name="expert_block",
    )(x, grads, up, down)


def adamw_step(weight, grad, first, second, rate):
    first_new = beta_first * first + (1.0 - beta_first) * grad
    second_new = beta_second * second + (1.0 - beta_second) * grad * grad
    moment = first_new / (1.0 - beta_first**STEP)
    spread = second_new / (1.0 - beta_second**STEP)
    weight_new = weight - rate * (
        moment / (jnp.sqrt(spread) + adam_epsilon) + weight_decay * weight
    )
    return (weight_new, first_new, second_new)


def swap_rows(values):
    return lax.ppermute(values, "row", [(0, 1), (1, 0)])


def gather_quarters(values):
    return lax.all_gather(values, ("row", "col"), axis=0)


def sum_quarters(values):
    return lax.psum_scatter(values, ("row", "col"), scatter_dimension=0, tiled=False)


def cross(values, near):
    perm = [(h * 2 + r, (r if near else 1 - r) * 2 + h) for h in range(2) for r in range(2)]
    return lax.ppermute(values, ("half", "row"), perm)


def cross_back(values, near):
    perm = [((r if near else 1 - r) * 2 + h, h * 2 + r) for h in range(2) for r in range(2)]
    return lax.ppermute(values, ("half", "row"), perm)


def in_order(index, own, other):
    return jnp.where(index == 0, jnp.stack([own, other]), jnp.stack([other, own]))


def pick(values, index):
    return lax.dynamic_index_in_dim(values, index, 0, keepdims=False)


def local(
    layer_in, lengths, placing, routes, cotangent,
    norm_gains, gain_first, gain_second, rel_bias, bias_first, bias_second,
    router, router_first, router_second, qkv_weight, qkv_first, qkv_second,
    proj_weight, proj_first, proj_second, expert_up, up_first, up_second,
    expert_down, down_first, down_second,
):
    tokens, part = layer_in.shape
    experts = lax.axis_size("ex")
    dp_count = 2 * experts
    both = ("ex", "half")
    quarters = lax.axis_size("row") * lax.axis_size("col")
    row, half = lax.axis_index("row"), lax.axis_index("half")
    cap = min(tokens, 5 * TOP * tokens // (4 * experts))
    hc = qkv_weight.shape[5]
    head_count = hc // HD

    x_all = gather_quarters(layer_in)
    gains_all = gather_quarters(norm_gains)

    qkv_low = jnp.moveaxis(qkv_weight[0, 0].astype(bf16), 1, 0).reshape(2, -1, 3 * hc)
    qkv_both = in_order(row, pick(qkv_low, row), swap_rows(pick(qkv_low, 1 - row)))
    weight = lax.all_gather(qkv_both, both, axis=1).reshape(D, 3 * hc)
    proj_low = jnp.swapaxes(proj_weight[:, :, 0, 0].astype(bf16), 1, 2)
    proj_both = in_order(row, pick(proj_low, row), swap_rows(pick(proj_low, 1 - row)))
    proj = lax.all_gather(proj_both, both, axis=1).reshape(D, hc)

    up_low = jnp.swapaxes(expert_up[0].astype(bf16), 0, 1)
    down_low = expert_down[0].astype(bf16)
    up = in_order(half, cross(up_low, True), cross(up_low, False))
    up = jnp.moveaxis(up, 0, 1).reshape(2, D, -1)
    down = in_order(half, cross(down_low, True), cross(down_low, False))
    down = jnp.moveaxis(down, 0, 1).reshape(-1, D)

    places = placing[0]
    given_routes = jnp.zeros_like(routes).at[places].set(routes)
    flat = given_routes.reshape(-1)
    numbers = jnp.arange(experts, dtype=jnp.int32)
    hits = (flat[:, None] == numbers[None, :]).astype(jnp.int32)
    before = jnp.cumsum(hits, axis=0) - hits
    table = hits.astype(f32).reshape(tokens, TOP, experts)
    slot_of = jnp.sum((jnp.where(hits > 0, before + 1, 0)).reshape(tokens, TOP, experts), axis=1) - 1
    one_hot = (slot_of.T[:, None, :] == jnp.arange(cap, dtype=jnp.int32)[None, :, None]).astype(bf16)

    def to_slots(values):
        return jnp.einsum("est,tf->esf", one_hot, values, preferred_element_type=f32).astype(bf16)

    def from_slots(values):
        return jnp.einsum("est,esf->tf", one_hot, values, preferred_element_type=f32)

    def exchange(values):
        return lax.all_to_all(values, "ex", split_axis=0, concat_axis=0, tiled=True)

    slot_grads = gather_quarters(exchange(to_slots(cotangent)))

    ends = jnp.cumsum(lengths[0])
    at = jnp.arange(tokens, dtype=jnp.int32)
    starts = jnp.max(jnp.where(ends[None, :] <= at[:, None], ends[None, :], 0), axis=1).astype(jnp.int32)
    vectors = bias_vectors(rel_bias, tokens)
    first, qkv, attended, lse = attention_forward(
        x_all, gains_all[:, :1], weight, places[None, :], places[:, None], starts[:, None], vectors
    )
    partial = dot_nt(attended, proj).astype(bf16).reshape(tokens, quarters, part)
    resid_one = layer_in.astype(f32)
    second = resid_one + sum_quarters(jnp.moveaxis(partial, 1, 0)).astype(f32)

    scaled_router = norm_gains[1][:, None] * router
    sums = lax.psum(
        jnp.concatenate(
            [jnp.sum(second * second, axis=1)[None], jnp.dot(second, scaled_router, precision=highest).T]
        ),
        ("row", "col"),
    )
    inverse_two = lax.rsqrt(sums[0] / D + norm_epsilon)
    mixed = (second * inverse_two[:, None] * norm_gains[1]).astype(bf16)
    logits = sums[1:].T * inverse_two[:, None]
    chosen = jnp.sum(table * logits[:, None, :], axis=2)
    gates = jax.nn.softmax(chosen, axis=1)
    gate_of = jnp.sum(table * gates[:, :, None], axis=1)

    gate_slots = jnp.einsum("est,te->es", one_hot.astype(f32), gate_of, precision=highest)
    padded = jnp.pad(gate_slots, ((0, 0), (0, 8 * part - cap))).reshape(experts, 8, part)
    near = padded.astype(bf16)
    left = (padded - near.astype(f32)).astype(bf16)
    slots = jnp.concatenate([to_slots(mixed), near, left], axis=1)
    slot_x = gather_quarters(exchange(slots))
    dx, y, dup, ddown = expert_block(slot_x, slot_grads, up, down)
    dx_home = exchange(sum_quarters(dx))
    y_home = exchange(sum_quarters(y))

    token_y = jnp.einsum("est,esf->etf", one_hot, y_home, preferred_element_type=f32)
    layer_out = (second + jnp.einsum("etf,te->tf", token_y, gate_of, precision=highest)).astype(bf16)

    extra = dx_home[:, cap:].astype(f32)
    gate_grad_slots = (extra[:, :8] + extra[:, 8:]).reshape(experts, -1)[:, :cap]
    gate_dgate = jnp.einsum("est,es->te", one_hot.astype(f32), gate_grad_slots, precision=highest)
    grad_logits = gate_dgate - gate_of * jnp.sum(gate_dgate, axis=1, keepdims=True)
    grad_router = jnp.dot(mixed.astype(f32).T, grad_logits, precision=highest)
    grad_mixed = from_slots(dx_home[:, :cap]) + jnp.dot(grad_logits, router.T, precision=highest)
    scaled = grad_mixed * norm_gains[1]
    row_total = lax.psum(jnp.sum(second * scaled, axis=1), ("row", "col"))
    grad_two = cotangent.astype(f32) + (
        scaled * inverse_two[:, None] - second * (inverse_two**3 * row_total / D)[:, None]
    )
    grad_gain_two = jnp.sum(grad_mixed * second * inverse_two[:, None], axis=0)

    branch = gather_quarters(grad_two.astype(bf16))
    dfirst, dweight, dproj, dvectors = attention_backward(
        branch, proj, qkv, lse, attended, first, weight, places[None, :], places[:, None], starts[:, None], vectors
    )
    grad_norm_one = sum_quarters(dfirst).astype(f32)
    square_sum = jnp.sum(x_all.astype(f32) ** 2, axis=(0, 2))
    inverse_one = lax.rsqrt(square_sum / D + norm_epsilon)
    scaled = grad_norm_one * norm_gains[0]
    row_total = lax.psum(jnp.sum(resid_one * scaled, axis=1), ("row", "col"))
    back_one = scaled * inverse_one[:, None] - resid_one * (inverse_one**3 * row_total / D)[:, None]
    input_grad = (grad_two + back_one).astype(bf16)
    grad_gain_one = jnp.sum(grad_norm_one * resid_one * inverse_one[:, None], axis=0)

    grad_bias = bias_gradient(dvectors, head_count, tokens)
    grad_gains, grad_bias, grad_router = lax.psum(
        (jnp.stack([grad_gain_one, grad_gain_two]), grad_bias, grad_router), both
    )
    qkv_part = lax.psum_scatter(
        dweight.reshape(2, dp_count, -1, 3 * hc), both, scatter_dimension=1, tiled=False
    )
    qkv_part = in_order(row, pick(qkv_part, row), swap_rows(pick(qkv_part, 1 - row)))
    grad_qkv = jnp.moveaxis(qkv_part, 0, 1).reshape(qkv_weight.shape).astype(f32)
    proj_part = lax.psum_scatter(
        dproj.reshape(2, dp_count, -1, hc), both, scatter_dimension=1, tiled=False
    )
    proj_part = in_order(row, pick(proj_part, row), swap_rows(pick(proj_part, 1 - row)))
    grad_proj = jnp.swapaxes(proj_part, 1, 2).reshape(proj_weight.shape).astype(f32)
    dup = jnp.moveaxis(dup.astype(bf16).reshape(2, 2, D // 2, -1), 1, 0)
    grad_up = cross_back(pick(dup, half), True).astype(f32) + cross_back(pick(dup, 1 - half), False).astype(f32)
    grad_up = jnp.swapaxes(grad_up, 0, 1)[None]
    ddown = jnp.moveaxis(ddown.astype(bf16).reshape(-1, 2, D // 2), 1, 0)
    grad_down = cross_back(pick(ddown, half), True).astype(f32) + cross_back(pick(ddown, 1 - half), False).astype(f32)
    grad_down = grad_down[None]

    gains = adamw_step(norm_gains, grad_gains, gain_first, gain_second, 0.5)
    bias = adamw_step(rel_bias, grad_bias, bias_first, bias_second, 1.0)
    routers = adamw_step(router, grad_router, router_first, router_second, 2.0 * (2 * D) ** (-0.5))
    qkvs = adamw_step(qkv_weight, grad_qkv, qkv_first, qkv_second, 2.0 * D ** (-0.5))
    projs = adamw_step(proj_weight, grad_proj, proj_first, proj_second, 2.0 * (HEADS * HD / 8) ** (-0.5))
    ups = adamw_step(expert_up, grad_up, up_first, up_second, 2.0 * D ** (-0.5))
    downs = adamw_step(expert_down, grad_down, down_first, down_second, 2.0 * (FF / 2) ** (-0.5))
    out = (layer_out, input_grad) + gains + bias + routers
    for group in (qkvs, projs, ups, downs):
        out = out + group + (group[0].astype(bf16),)
    return out


def solution(mesh):
    shape = mesh.devices.shape
    fine = Mesh(
        mesh.devices.reshape((shape[0] // 2, 2) + shape[1:]), ("ex", "half", "row", "col")
    )
    dp, grid = ("ex", "half"), ("row", "col")
    tokens, own = P(dp, grid), P(dp, None)
    gain, router = P(None, grid), P(grid, None)
    qkv, proj = P("row", dp, None, None, None, "col"), P(None, "col", "row", dp, None)
    up, down = P(dp, "row", None, "col"), P(dp, "col", "row")
    in_specs = (
        (tokens, own, own, own, tokens) + (gain,) * 6 + (router,) * 3
        + (qkv,) * 3 + (proj,) * 3 + (up,) * 3 + (down,) * 3
    )
    out_specs = (
        (tokens, tokens) + (gain,) * 6 + (router,) * 3
        + (qkv,) * 4 + (proj,) * 4 + (up,) * 4 + (down,) * 4
    )
    return jax.shard_map(local, mesh=fine, in_specs=in_specs, out_specs=out_specs, check_vma=False)
```

```python
import functools

import jax
import jax.numpy as jnp
import numpy as np
from jax import lax
from jax.experimental import pallas as pl
from jax.experimental.layout import Layout, with_layout_constraint
from jax.experimental.pallas import tpu as pltpu
from jax.sharding import Mesh, PartitionSpec as P

D = 1024
HEADS = 16
FF = 2816
TOP = 2
STEP = 5
beta_first = 0.5
beta_second = 0.5
adam_epsilon = 1e-08
weight_decay = 0.01
highest = lax.Precision.HIGHEST
EXTRA = 16
HD = 64
BUCKETS = 32
LONGEST = 512
TILE = 256
norm_epsilon = 1e-06
hidden_score = -1e30
bucket_edges = np.floor(16.0 * 2.0 ** (np.arange(16) * 0.375)).astype(np.int32)
f32 = jnp.float32
bf16 = jnp.bfloat16
MIB = 1 << 20


def dot_nn(a, b):
    return lax.dot_general(a, b, (((1,), (0,)), ((), ())), preferred_element_type=f32)


def dot_nt(a, b):
    return lax.dot_general(a, b, (((1,), (1,)), ((), ())), preferred_element_type=f32)


def dot_tn(a, b):
    return lax.dot_general(a, b, (((0,), (0,)), ((), ())), preferred_element_type=f32)


def tile_reach(tokens):
    return min(tokens // TILE, (LONGEST - 1 + TILE - 1) // TILE + 1)


def toeplitz_places(tokens):
    reach = tile_reach(tokens)
    m = np.arange(2 * TILE)
    base = np.where(m < TILE, -m, 2 * TILE - m)
    distance = np.arange(reach)[:, None] * TILE + base[None, :]
    clipped = np.maximum(distance, 0)
    buckets = np.where(
        clipped < 16, clipped, 15 + (clipped[..., None] >= bucket_edges).sum(-1)
    )
    return (distance, buckets)


def bias_vectors(rel_bias, tokens):
    distance, buckets = toeplitz_places(tokens)
    table = jnp.asarray((buckets[..., None] == np.arange(BUCKETS)).astype(np.float32))
    values = jnp.einsum("dmb,bh->hdm", table, rel_bias, precision=lax.Precision.HIGHEST)
    values = jnp.where(jnp.asarray(distance < 0)[None], hidden_score, values)
    return values.reshape(-1, 2 * TILE)


def bias_gradient(vectors, head_count, tokens):
    distance, buckets = toeplitz_places(tokens)
    table = ((buckets[..., None] == np.arange(BUCKETS)) & (distance >= 0)[..., None]).astype(np.float32)
    return jnp.einsum(
        "dmb,hdm->bh",
        jnp.asarray(table),
        vectors.reshape(head_count, distance.shape[0], 2 * TILE),
        precision=lax.Precision.HIGHEST,
    )


def fill_bias(vector_ref, bias):
    for i in range(bias.shape[0]):
        wide = jnp.broadcast_to(vector_ref[i : i + 1, :], (TILE, 2 * TILE))
        bias[i] = pltpu.roll(wide, 0, 1, stride=1, stride_axis=0)[:, :TILE]


def head_lanes(shape, head):
    return lax.broadcasted_iota(jnp.int32, shape, 1) // HD == head


def attention_forward_kernel(
    x_ref, gain_ref, weight_ref, place_row, place_col, start_ref, vector_ref,
    first_ref, qkv_ref, attended_ref, lse_ref, bias, placed_out,
):
    quarters, tokens, part = x_ref.shape
    width = quarters * part
    hc = weight_ref.shape[1] // 4
    head_count = hc // HD
    reach = bias.shape[0] // head_count
    fill_bias(vector_ref, bias)
    squares = jnp.zeros((tokens, 1), f32)
    for q in range(quarters):
        v = x_ref[q].astype(f32)
        squares = squares + jnp.sum(v * v, axis=1, keepdims=True)
    inverse = lax.rsqrt(squares / width + norm_epsilon)
    total = jnp.zeros((tokens, 3 * hc), f32)
    for q in range(quarters):
        first = (x_ref[q].astype(f32) * inverse * gain_ref[q, :1]).astype(bf16)
        first_ref[q] = first
        total = total + dot_nn(first, weight_ref[q * part : (q + 1) * part, : 3 * hc])
    to_placed = jnp.where(
        place_col[...] == lax.broadcasted_iota(jnp.int32, (tokens, tokens), 1), 1.0, 0.0
    ).astype(bf16)
    scale = jnp.where(
        lax.broadcasted_iota(jnp.int32, (1, 3 * hc), 1) < hc, HD ** (-0.5), 1.0
    )
    qkv_ref[...] = dot_nn(to_placed, (total * scale).astype(bf16)).astype(bf16)
    for a in range(tokens // TILE):
        rows = slice(a * TILE, (a + 1) * TILE)
        blocks = range(max(0, a - reach + 1), a + 1)
        starts = start_ref[rows, :]
        visible = [
            b * TILE + lax.broadcasted_iota(jnp.int32, (TILE, TILE), 1) >= starts for b in blocks
        ]

        def one_head(head, carry):
            out, lse = carry
            mine = head_lanes((TILE, hc), head)
            query = jnp.where(mine, qkv_ref[rows, :hc], 0)
            scores = []
            for b, seen in zip(blocks, visible):
                s = dot_nt(query, qkv_ref[b * TILE : (b + 1) * TILE, hc : 2 * hc])
                scores.append(jnp.where(seen, s + bias[head * reach + a - b], hidden_score))
            top = functools.reduce(jnp.maximum, [jnp.max(s, axis=1, keepdims=True) for s in scores])
            exps = [jnp.exp(s - top) for s in scores]
            denominator = functools.reduce(jnp.add, [jnp.sum(e, axis=1, keepdims=True) for e in exps])
            share = 1.0 / denominator
            value = jnp.zeros((TILE, hc), f32)
            for b, e in zip(blocks, exps):
                value = value + dot_nn(
                    (e * share).astype(bf16), qkv_ref[b * TILE : (b + 1) * TILE, 2 * hc :]
                )
            lane = lax.broadcasted_iota(jnp.int32, (TILE, 128), 1)
            return (
                jnp.where(mine, value, out),
                jnp.where(lane == head, top + jnp.log(denominator), lse),
            )

        out, lse = lax.fori_loop(
            0, head_count, one_head, (jnp.zeros((TILE, hc), f32), jnp.zeros((TILE, 128), f32))
        )
        placed_out[rows, :] = out.astype(bf16)
        lse_ref[rows, :] = lse
    lane = lax.broadcasted_iota(jnp.int32, (tokens, 128), 1)
    lse_ref[...] = jnp.where(lane == 127, inverse, lse_ref[...])
    to_given = jnp.where(
        place_row[...] == lax.broadcasted_iota(jnp.int32, (tokens, tokens), 0), 1.0, 0.0
    ).astype(bf16)
    attended_ref[...] = dot_nn(to_given, placed_out[...]).astype(bf16)


def microseconds(time):
    return pl.CostEstimate(flops=0, bytes_accessed=int(time * 3.5e6), transcendentals=0)


def vmem():
    return pl.BlockSpec(memory_space=pltpu.VMEM)


def attention_forward(x, gain, weight, place_row, place_col, starts, vectors):
    quarters, tokens, part = x.shape
    hc = weight.shape[1] // 4
    return pl.pallas_call(
        attention_forward_kernel,
        out_shape=(
            jax.ShapeDtypeStruct(x.shape, bf16),
            jax.ShapeDtypeStruct((tokens, 3 * hc), bf16),
            jax.ShapeDtypeStruct((tokens, hc), bf16),
            jax.ShapeDtypeStruct((tokens, 128), f32),
        ),
        in_specs=[vmem()] * 7,
        out_specs=(vmem(),) * 4,
        scratch_shapes=[
            pltpu.VMEM((vectors.shape[0], TILE, TILE), f32),
            pltpu.VMEM((tokens, hc), bf16),
        ],
        compiler_params=pltpu.CompilerParams(vmem_limit_bytes=16 * MIB),
        cost_estimate=microseconds(20),
        name="attention_forward",
    )(x, gain, weight, place_row, place_col, starts, vectors)


def attention_backward_kernel(
    branch_ref, qkv_ref, lse_ref, attended_ref, first_ref, weight_ref,
    place_row, place_col, start_ref, vector_ref,
    dfirst_ref, dweight_ref, dvector_ref,
    bias, dbias, grad_ref, dqkv, dkv,
):
    quarters, tokens, part = branch_ref.shape
    hc = weight_ref.shape[1] // 4
    head_count = hc // HD
    reach = bias.shape[0] // head_count
    fill_bias(vector_ref, bias)
    dbias[...] = jnp.zeros_like(dbias)
    dkv[...] = jnp.zeros_like(dkv)
    total = jnp.zeros((tokens, hc), f32)
    for q in range(quarters):
        dims = slice(q * part, (q + 1) * part)
        total = total + dot_nn(branch_ref[q], weight_ref[dims, 3 * hc :])
        dweight_ref[dims, 3 * hc :] = dot_tn(branch_ref[q], attended_ref[...]).astype(bf16)
    to_placed = jnp.where(
        place_col[...] == lax.broadcasted_iota(jnp.int32, (tokens, tokens), 1), 1.0, 0.0
    ).astype(bf16)
    grad_ref[...] = dot_nn(to_placed, total.astype(bf16)).astype(bf16)
    for a in range(tokens // TILE):
        rows = slice(a * TILE, (a + 1) * TILE)
        blocks = range(max(0, a - reach + 1), a + 1)
        starts = start_ref[rows, :]
        visible = [
            b * TILE + lax.broadcasted_iota(jnp.int32, (TILE, TILE), 1) >= starts for b in blocks
        ]

        def one_head(head, dquery):
            mine = head_lanes((TILE, hc), head)
            query = jnp.where(mine, qkv_ref[rows, :hc], 0)
            grad = jnp.where(mine, grad_ref[rows, :], 0)
            lane = lax.broadcasted_iota(jnp.int32, (TILE, 128), 1)
            lse = jnp.sum(jnp.where(lane == head, lse_ref[rows, :], 0.0), axis=1, keepdims=True)
            probs, dprobs = [], []
            inner = jnp.zeros((TILE, 1), f32)
            for b, seen in zip(blocks, visible):
                keys = slice(b * TILE, (b + 1) * TILE)
                s = dot_nt(query, qkv_ref[keys, hc : 2 * hc]) + bias[head * reach + a - b]
                p = jnp.where(seen, jnp.exp(s - lse), 0.0)
                d = dot_nt(grad, qkv_ref[keys, 2 * hc :])
                inner = inner + jnp.sum(p * d, axis=1, keepdims=True)
                probs.append(p)
                dprobs.append(d)
            for b, p, d in zip(blocks, probs, dprobs):
                keys = slice(b * TILE, (b + 1) * TILE)
                ds = p * (d - inner)
                place = head * reach + a - b
                dbias[place] = dbias[place] + ds
                low = ds.astype(bf16)
                dquery = dquery + dot_nn(low, jnp.where(mine, qkv_ref[keys, hc : 2 * hc], 0))
                dkv[keys, :hc] = dkv[keys, :hc] + dot_tn(low, query)
                dkv[keys, hc:] = dkv[keys, hc:] + dot_tn(p.astype(bf16), grad)
            return dquery

        dquery = lax.fori_loop(0, head_count, one_head, jnp.zeros((TILE, hc), f32))
        dqkv[rows, :hc] = (dquery * HD ** (-0.5)).astype(bf16)
    dqkv[:, hc:] = dkv[...].astype(bf16)
    for i in range(dbias.shape[0]):
        wide = jnp.concatenate([dbias[i], jnp.zeros((TILE, TILE), f32)], axis=1)
        level = wide[:8]
        for g in range(8, TILE, 8):
            level = level + pltpu.roll(wide[g : g + 8], 2 * TILE - g, 1)
        row = level[:1]
        for s in range(1, 8):
            row = row + pltpu.roll(level[s : s + 1], 2 * TILE - s, 1)
        dvector_ref[i : i + 1, :] = row
    to_given = jnp.where(
        place_row[...] == lax.broadcasted_iota(jnp.int32, (tokens, tokens), 0), 1.0, 0.0
    ).astype(bf16)
    given = dot_nn(to_given, dqkv[...]).astype(bf16)
    for q in range(quarters):
        dims = slice(q * part, (q + 1) * part)
        dfirst_ref[q] = dot_nt(given, weight_ref[dims, : 3 * hc]).astype(bf16)
        dweight_ref[dims, : 3 * hc] = dot_tn(first_ref[q], given).astype(bf16)


def attention_backward(branch, qkv, lse, attended, first, weight, place_row, place_col, starts, vectors):
    quarters, tokens, part = branch.shape
    hc = weight.shape[1] // 4
    return pl.pallas_call(
        attention_backward_kernel,
        out_shape=(
            jax.ShapeDtypeStruct(branch.shape, bf16),
            jax.ShapeDtypeStruct(weight.shape, bf16),
            jax.ShapeDtypeStruct(vectors.shape, f32),
        ),
        in_specs=[vmem()] * 10,
        out_specs=(vmem(),) * 3,
        scratch_shapes=[
            pltpu.VMEM((vectors.shape[0], TILE, TILE), f32),
            pltpu.VMEM((vectors.shape[0], TILE, TILE), f32),
            pltpu.VMEM((tokens, hc), bf16),
            pltpu.VMEM((tokens, 3 * hc), bf16),
            pltpu.VMEM((tokens, 2 * hc), f32),
        ],
        compiler_params=pltpu.CompilerParams(vmem_limit_bytes=24 * MIB),
        cost_estimate=microseconds(28),
        name="attention_backward",
    )(branch, qkv, lse, attended, first, weight, place_row, place_col, starts, vectors)


def half_places(rows, part):
    row = lax.broadcasted_iota(jnp.int32, (rows, EXTRA), 0) // part
    high = lax.broadcasted_iota(jnp.int32, (rows, EXTRA), 1)
    column = lax.broadcasted_iota(jnp.int32, (rows, part), 0) % part
    return (row, high, column == lax.broadcasted_iota(jnp.int32, (rows, part), 1))


def write_extra(values, part):
    row, high, column = half_places(values.shape[0], part)
    near = values.astype(bf16)
    left = (values - near.astype(f32)).astype(bf16)
    near_rows = jnp.where(row == high, 1.0, 0.0).astype(bf16)
    left_rows = jnp.where(row + 8 == high, 1.0, 0.0).astype(bf16)
    near_values = jnp.where(column, near.astype(f32), 0.0).astype(bf16)
    left_values = jnp.where(column, left.astype(f32), 0.0).astype(bf16)
    return dot_tn(near_rows, near_values) + dot_tn(left_rows, left_values)


def read_extra(extra, rows):
    part = extra.shape[1]
    row, high, column = half_places(rows, part)
    pick = jnp.where(row == high % 8, 1.0, 0.0).astype(bf16)
    return jnp.sum(jnp.where(column, dot_nn(pick, extra), 0.0), axis=1, keepdims=True)


GELU_A = 0.7978845608028654
GELU_B = 0.044715


MESH = pl.DeviceIdType.MESH


def remote(src, dst, send, recv, where):
    return pltpu.make_async_remote_copy(
        src_ref=src, dst_ref=dst, send_sem=send, recv_sem=recv, device_id=where, device_id_type=MESH
    )


def greet(wheres):
    barrier = pltpu.get_barrier_semaphore()
    for where in wheres:
        pl.semaphore_signal(barrier, inc=1, device_id=where, device_id_type=MESH)
    pl.semaphore_wait(barrier, len(wheres))


def dot_exact(a, b, dims):
    return lax.dot_general(a, b, ((dims, ((), ()))), precision=highest, preferred_element_type=f32)


def grid_peers(columns):
    row, col = lax.axis_index("row"), lax.axis_index("col")
    return [
        {"row": (row + i) % 2, "col": (col + j) % columns}
        for i in range(2)
        for j in range(columns)
        if i + j > 0
    ]


def sum_of_peers(mine, got, send, recv, columns):
    copies = [
        remote(mine, got.at[i], send.at[i], recv.at[i], where)
        for i, where in enumerate(grid_peers(columns))
    ]
    for copy in copies:
        copy.start()
    for copy in copies:
        copy.wait_recv()
    total = mine[...]
    for i in range(len(copies)):
        total = total + got[i]
    for copy in copies:
        copy.wait_send()
    return total


PIECES = 4


def project_kernel(
    columns, experts,
    attended_ref, weight_ref, layer_ref, gain_ref, router_ref, slot_ref,
    second_ref, mixed_ref, gate_ref, column_ref,
    core_out, core_in, keep, col_out, col_in, stat, stat_in,
    core_send, core_recv, col_send, col_recv, stat_send, stat_recv,
):
    row, col = lax.axis_index("row"), lax.axis_index("col")
    tokens, part = layer_ref.shape
    wide = columns * part
    size = tokens // PIECES
    greet(grid_peers(columns))
    heads = slice(3 * weight_ref.shape[1] // 4, weight_ref.shape[1])
    own_rows = pl.ds(pl.multiple_of(row * wide, wide), wide)
    other_rows = pl.ds(pl.multiple_of((1 - row) * wide, wide), wide)
    cores = []
    for i in range(PIECES):
        at = slice(i * size, (i + 1) * size)
        core_out[i] = dot_nt(attended_ref[at, :], weight_ref[other_rows, heads]).astype(bf16)
        copy = remote(core_out.at[i], core_in.at[i], core_send.at[i], core_recv.at[i], {"row": 1 - row})
        copy.start()
        cores.append(copy)
        keep[i] = dot_nt(attended_ref[at, :], weight_ref[own_rows, heads])
    own_columns = pl.ds(pl.multiple_of(col * part, part), part)
    crossing = []
    for i in range(PIECES):
        cores[i].wait_recv()
        keep[i] = keep[i] + core_in[i].astype(f32)
        for k in range(1, columns):
            to = (col + k) % columns
            col_out[i, k - 1] = keep[i, :, pl.ds(pl.multiple_of(to * part, part), part)].astype(bf16)
            copy = remote(
                col_out.at[i, k - 1], col_in.at[i, k - 1], col_send.at[i, k - 1], col_recv.at[i, k - 1], {"col": to}
            )
            copy.start()
            crossing.append(copy)
    ones = jnp.where(lax.broadcasted_iota(jnp.int32, router_ref.shape, 0) == experts, 1.0, 0.0)
    for i in range(PIECES):
        at = slice(i * size, (i + 1) * size)
        total = layer_ref[at, :].astype(f32) + keep[i, :, own_columns]
        for k in range(1, columns):
            crossing[i * (columns - 1) + k - 1].wait_recv()
            total = total + col_in[i, k - 1].astype(f32)
        second_ref[at, :] = total
        stat[:, at] = dot_exact(router_ref[...], total, ((1,), (1,))) + dot_exact(
            ones, total * total, ((1,), (1,))
        )
    total = sum_of_peers(stat, stat_in, stat_send, stat_recv, columns)
    inverse = lax.rsqrt(total[experts : experts + 1] / D + norm_epsilon)
    routed = slot_ref[...] >= 0
    logits = jnp.where(routed, total * inverse, hidden_score)
    shares = jnp.where(routed, jnp.exp(logits - jnp.max(logits, axis=0, keepdims=True)), 0.0)
    gates = shares / jnp.sum(shares, axis=0, keepdims=True)
    gate_ref[...] = gates
    number = lax.broadcasted_iota(jnp.int32, gates.shape, 0)
    lanes = (gates.shape[0], 128)
    eye = jnp.where(
        lax.broadcasted_iota(jnp.int32, lanes, 0) == lax.broadcasted_iota(jnp.int32, lanes, 1), 1.0, 0.0
    )
    table = dot_exact(jnp.where(number == experts, inverse, gates), eye, ((0,), (0,)))
    column_ref[...] = table
    mixed_ref[...] = (second_ref[...] * table[:, experts : experts + 1] * gain_ref[...]).astype(bf16)
    for copy in cores + crossing:
        copy.wait_send()


def project(attended, weight, layer_in, gain, router_rows, slots, experts, columns):
    tokens, part = layer_in.shape
    size = tokens // PIECES
    rows = router_rows.shape[0]
    dma = pltpu.SemaphoreType.DMA
    return pl.pallas_call(
        functools.partial(project_kernel, columns, experts),
        out_shape=(
            jax.ShapeDtypeStruct((tokens, part), f32),
            jax.ShapeDtypeStruct((tokens, part), bf16),
            jax.ShapeDtypeStruct((rows, tokens), f32),
            jax.ShapeDtypeStruct((tokens, 128), f32),
        ),
        in_specs=[vmem()] * 6,
        out_specs=(vmem(),) * 4,
        scratch_shapes=[
            pltpu.VMEM((PIECES, size, columns * part), bf16),
            pltpu.VMEM((PIECES, size, columns * part), bf16),
            pltpu.VMEM((PIECES, size, columns * part), f32),
            pltpu.VMEM((PIECES, columns - 1, size, part), bf16),
            pltpu.VMEM((PIECES, columns - 1, size, part), bf16),
            pltpu.VMEM((rows, tokens), f32),
            pltpu.VMEM((2 * columns - 1, rows, tokens), f32),
            dma((PIECES,)), dma((PIECES,)),
            dma((PIECES, columns - 1)), dma((PIECES, columns - 1)),
            dma((2 * columns - 1,)), dma((2 * columns - 1,)),
        ],
        compiler_params=pltpu.CompilerParams(
            collective_id=1, has_side_effects=True, vmem_limit_bytes=40 * MIB
        ),
        cost_estimate=microseconds(22),
        name="project",
    )(attended, weight, layer_in, gain, router_rows, slots)


def gather_kernel(
    columns, experts,
    layer_ref, gain_ref, shard_ref,
    x_ref, gains_ref, weight_ref,
    x_send, x_recv, own_send, own_recv, pass_send, pass_recv, gain_send, gain_recv,
    swap_send, swap_recv, z_send, z_recv, y_send, y_recv, place,
):
    ex, half = lax.axis_index("ex"), lax.axis_index("half")
    row, col = lax.axis_index("row"), lax.axis_index("col")
    mine = row * columns + col
    greet(
        grid_peers(columns)
        + [{"ex": (ex + s) % experts} for s in range(1, experts)]
        + [{"half": 1 - half}]
    )
    spread = Spread(
        x_ref, layer_ref, columns, x_send, x_recv, own_send, own_recv, pass_send, pass_recv
    )
    member = 2 * ex + half
    swap = remote(
        shard_ref.at[1 - row], weight_ref.at[row, member], swap_send.at[0], swap_recv.at[0], {"row": 1 - row}
    )
    swap.start()
    arrived = remote(
        shard_ref.at[1 - row], weight_ref.at[1 - row, member], swap_send.at[0], swap_recv.at[0], {"row": 1 - row}
    )
    place_shard = pltpu.make_async_copy(shard_ref.at[row], weight_ref.at[row, member], place.at[0])
    place_shard.start()
    spread.start()
    gains_ref[mine] = gain_ref[...]
    gain_copies = [
        remote(gain_ref, gains_ref.at[mine], gain_send.at[i], gain_recv.at[i], where)
        for i, where in enumerate(grid_peers(columns))
    ]
    for copy in gain_copies:
        copy.start()

    def z_copy(s, a):
        block = weight_ref.at[a, member]
        return remote(block, block, z_send.at[s, a], z_recv.at[s, a], {"ex": (ex + s) % experts})

    def z_arrival(s, a):
        block = weight_ref.at[a, 2 * ((ex - s + experts) % experts) + half]
        return remote(block, block, z_send.at[s, a], z_recv.at[s, a], {"ex": (ex + s) % experts})

    def y_copy(s, a):
        block = weight_ref.at[a, 2 * ((ex - s + experts) % experts) + half]
        return remote(block, block, y_send.at[s, a], y_recv.at[s, a], {"half": 1 - half})

    def y_arrival(s, a):
        block = weight_ref.at[a, 2 * ((ex - s + experts) % experts) + 1 - half]
        return remote(block, block, y_send.at[s, a], y_recv.at[s, a], {"half": 1 - half})

    place_shard.wait()
    for a in (row, 1 - row):
        if a is not row:
            arrived.wait_recv()
        for s in range(1, experts):
            z_copy(s, a).start()
        y_copy(0, a).start()
    spread.hand_on()
    for s in range(1, experts):
        for a in (row, 1 - row):
            z_arrival(s, a).wait_recv()
            y_copy(s, a).start()
    spread.finish()
    for i, copy in enumerate(gain_copies):
        copy.wait()
    swap.wait_send()
    for s in range(experts):
        for a in range(2):
            y_arrival(s, a).wait_recv()
            y_copy(s, a).wait_send()
            if s > 0:
                z_copy(s, a).wait_send()


class Spread:
    def __init__(self, out, source, columns, x_send, x_recv, own_send, own_recv, pass_send, pass_recv):
        row, col = lax.axis_index("row"), lax.axis_index("col")
        mine = row * columns + col
        size = source.shape[0] // PIECES
        self.out, self.source, self.mine = out, source, mine
        self.across, self.own, self.passed = [], [], []
        for i in range(PIECES):
            at = pl.ds(i * size, size)
            for k in range(1, columns):
                self.across.append(
                    remote(
                        source.at[at], out.at[mine, at], x_send.at[i, k - 1], x_recv.at[i, k - 1],
                        {"col": (col + k) % columns},
                    )
                )
                block = out.at[row * columns + (col - k + columns) % columns, at]
                self.passed.append(
                    remote(block, block, pass_send.at[i, k - 1], pass_recv.at[i, k - 1], {"row": 1 - row})
                )
            self.own.append(
                remote(source.at[at], out.at[mine, at], own_send.at[i], own_recv.at[i], {"row": 1 - row})
            )

    def start(self):
        for copy in self.across + self.own:
            copy.start()
        self.out[self.mine] = self.source[...]

    def hand_on(self):
        for across, passed in zip(self.across, self.passed):
            across.wait_recv()
            passed.start()

    def finish(self):
        for copy in self.own + self.passed:
            copy.wait_recv()
        for copy in self.across + self.own + self.passed:
            copy.wait_send()


def spread_semaphores(columns):
    dma = pltpu.SemaphoreType.DMA
    return [dma((PIECES, columns - 1))] * 2 + [dma((PIECES,))] * 2 + [dma((PIECES, columns - 1))] * 2


def gather(layer_in, gains, shard, experts, columns):
    tokens, part = layer_in.shape
    _, rows, width = shard.shape
    quarters = 2 * columns
    dma = pltpu.SemaphoreType.DMA
    return pl.pallas_call(
        functools.partial(gather_kernel, columns, experts),
        out_shape=(
            jax.ShapeDtypeStruct((quarters, tokens, part), bf16),
            jax.ShapeDtypeStruct((quarters,) + gains.shape, f32),
            jax.ShapeDtypeStruct((2, 2 * experts, rows, width), bf16),
        ),
        in_specs=[vmem()] * 3,
        out_specs=(vmem(),) * 3,
        scratch_shapes=spread_semaphores(columns)
        + [
            dma((quarters - 1,)), dma((quarters - 1,)), dma((1,)), dma((1,)),
            dma((experts, 2)), dma((experts, 2)), dma((experts, 2)), dma((experts, 2)), dma((1,)),
        ],
        compiler_params=pltpu.CompilerParams(
            collective_id=0, has_side_effects=True, vmem_limit_bytes=40 * MIB
        ),
        cost_estimate=microseconds(30),
        name="gather",
    )(layer_in, gains, shard)


def expert_kernel(
    columns, experts,
    *refs,
):
    grad_count = columns * experts
    mixed_ref, slot_ref, gate_ref, up_hbm, down_hbm = refs[:5]
    grad_hbm = refs[5 : 5 + grad_count]
    (
    home_ref, y_hbm, dup_hbm, ddown_hbm,
    x, xs, grads, up, down, da, db, scaled, core_out, core_in, keep, col_out, col_in,
    load, grad_load, grad_send, grad_recv, z_send, z_recv, own_send, own_recv, col_send, col_recv, pass_send, pass_recv,
    core_send, core_recv, back_send, back_recv, home_send, home_recv, y_sem, store, far_send, far_recv,
    ) = refs[5 + grad_count :]
    ex, half = lax.axis_index("ex"), lax.axis_index("half")
    row, col = lax.axis_index("row"), lax.axis_index("col")
    tokens, part = mixed_ref.shape
    ext = x.shape[2]
    cap = ext - EXTRA
    quarters = 2 * columns
    wide = columns * part
    mine = row * columns + col
    last = experts - 1
    greet(
        [{"ex": (ex + s) % experts} for s in range(1, experts)]
        + [{"col": (col + k) % columns} for k in range(1, columns)]
        + [{"row": 1 - row}]
    )

    own_rows = pl.ds(pl.multiple_of(row * wide, wide), wide)
    other_rows = pl.ds(pl.multiple_of((1 - row) * wide, wide), wide)
    loads = [
        pltpu.make_async_copy(up_hbm.at[row], up.at[:, own_rows], load.at[0]),
        pltpu.make_async_copy(down_hbm.at[row], down.at[:, own_rows], load.at[1]),
    ]
    handed = [
        remote(up_hbm.at[1 - row], up.at[:, own_rows], load.at[2], load.at[3], {"row": 1 - row}),
        remote(down_hbm.at[1 - row], down.at[:, own_rows], load.at[4], load.at[5], {"row": 1 - row}),
    ]
    for s in range(experts):
        for k in range(columns):
            at = (s, k)
            place = row * columns + (col - k + columns) % columns
            block = grad_hbm[s * columns + k]
            loads.append(pltpu.make_async_copy(block, grads.at[place, s], grad_load.at[at]))
            handed.append(
                remote(block, grads.at[place, s], grad_send.at[at], grad_recv.at[at], {"row": 1 - row})
            )
    for copy in loads + handed:
        copy.start()

    def z_copy(s):
        return remote(
            xs.at[s], x.at[mine, s], z_send.at[s], z_recv.at[s], {"ex": (ex + s) % experts}
        )

    def own_copy(s):
        block = x.at[mine, s]
        return remote(block, block, own_send.at[s], own_recv.at[s], {"row": 1 - row})

    def col_copy(s, k):
        block = x.at[mine, s]
        return remote(
            block, block, col_send.at[s, k - 1], col_recv.at[s, k - 1], {"col": (col + k) % columns}
        )

    def pass_copy(s, k):
        block = x.at[row * columns + (col - k + columns) % columns, s]
        return remote(
            block, block, pass_send.at[s, k - 1], pass_recv.at[s, k - 1], {"row": 1 - row}
        )

    def spread(s):
        own_copy(s).start()
        for k in range(1, columns):
            col_copy(s, k).start()

    def hand_on(s):
        for k in range(1, columns):
            col_copy(s, k).wait_recv()
            pass_copy(s, k).start()

    def slots_of(e):
        hit = slot_ref[pl.ds(e, 1), :] == lax.broadcasted_iota(jnp.int32, (cap, tokens), 0)
        values = dot_nn(jnp.where(hit, 1.0, 0.0).astype(bf16), mixed_ref[...]).astype(bf16)
        gate = jnp.sum(jnp.where(hit, gate_ref[pl.ds(e, 1), :], 0.0), axis=1, keepdims=True)
        return values, write_extra(gate, part).astype(bf16)

    def build(s):
        values, extra = slots_of((ex + s) % experts)
        xs[s, :cap] = values
        xs[s, cap:] = extra

    def nth(p):
        far = experts // 2
        return jnp.where(p == 1, far, jnp.where((p > 1) & (p <= far), p - 1, p))

    build(nth(1))
    z_copy(nth(1)).start()
    values, extra = slots_of(ex)
    x[mine, 0, :cap] = values
    x[mine, 0, cap:] = extra
    spread(0)

    @pl.loop(2, experts)
    def _(p):
        build(nth(p))

    for copy in loads:
        copy.wait()
    for copy in handed:
        copy.wait()
    hand_on(0)
    z_copy(nth(1)).wait_send()
    z_copy(nth(2)).start()
    z_copy(nth(1)).wait_recv()
    spread(nth(1))

    def core_copy(s):
        return remote(core_out.at[s], core_in.at[s], core_send.at[s], core_recv.at[s], {"row": 1 - row})

    def back_copy(s, k):
        return remote(
            col_out.at[s, k - 1], col_in.at[s, k - 1], back_send.at[s, k - 1], back_recv.at[s, k - 1],
            {"col": (col + k) % columns},
        )

    def home_copy(s):
        return remote(
            xs.at[s], home_ref.at[s], home_send.at[s], home_recv.at[s], {"ex": (ex - s + experts) % experts}
        )

    def up_store(g):
        return pltpu.make_async_copy(up.at[g, own_rows], dup_hbm.at[row, g], store.at[g])

    def up_far(g):
        return remote(up.at[g, other_rows], dup_hbm.at[row, g], far_send.at[g], far_recv.at[g], {"row": 1 - row})

    def down_store():
        return pltpu.make_async_copy(down.at[:, own_rows], ddown_hbm.at[row], store.at[2])

    def down_far():
        return remote(down.at[:, other_rows], ddown_hbm.at[row], far_send.at[2], far_recv.at[2], {"row": 1 - row})

    def y_copy(s, slot):
        return pltpu.make_async_copy(core_in.at[pl.ds(2 * slot, 2)], y_hbm.at[:, :, s], y_sem.at[slot])

    def after_core(s, slot):
        core_copy(s).wait_recv()
        keep[slot] = keep[slot] + core_in[s].astype(f32)
        for k in range(1, columns):
            to = (col + k) % columns
            col_out[s, k - 1] = keep[slot, to].astype(bf16)
            back_copy(s, k).start()

    def after_columns(s, slot):
        total = keep[slot, col]
        for k in range(1, columns):
            back_copy(s, k).wait_recv()
            total = total + col_in[s, k - 1].astype(f32)
        return total.astype(bf16)

    def send_home(s, slot):
        xs[s] = after_columns(s, slot)
        home_copy(s).start()

    @pl.loop(0, experts)
    def _(p):
        s = nth(p)
        slot = jnp.where(p == 0, 2, p % 2)
        grad = jnp.concatenate([grads[q, s] for q in range(quarters)], axis=1)
        d = dot_nt(grad, down[...])
        own_copy(s).wait_recv()
        for k in range(1, columns):
            pass_copy(s, k).wait_recv()

        @pl.when(p > 1)
        def _():
            after_core(nth(p - 1), (p - 1) % 2)

        @pl.when(p > 2)
        def _():
            send_home(nth(p - 2), p % 2)

        rows = jnp.concatenate([x[q, s] for q in range(quarters)], axis=1)
        gate = read_extra(x[mine, s, cap:], ext)
        a = dot_nn(rows, up[0])
        b = dot_nn(rows, up[1])
        d = d * gate
        square = a * a
        t = jnp.tanh(a * (GELU_A + (GELU_A * GELU_B) * square))
        part_on = 0.5 + 0.5 * t
        smooth = a * part_on
        slope = part_on + (a * (0.5 - 0.5 * t * t)) * (GELU_A + (3 * GELU_A * GELU_B) * square)
        active = smooth * b
        da[s] = (d * b * slope).astype(bf16)
        db[s] = (d * smooth).astype(bf16)
        scaled[s] = (active * gate).astype(bf16)
        extra = write_extra(jnp.sum(d * active, axis=1, keepdims=True), part)

        @pl.when((p > 0) & (p + 2 < experts))
        def _():
            z_copy(nth(p + 2)).wait_recv()
            spread(nth(p + 2))

        @pl.when((p > 0) & (p + 1 < experts))
        def _():
            hand_on(nth(p + 1))

        @pl.when((p > 0) & (p + 3 < experts))
        def _():
            z_copy(nth(p + 2)).wait_send()
            z_copy(nth(p + 3)).start()

        for j in range(columns):
            dims = pl.ds(pl.multiple_of(((1 - row) * columns + j) * part, part), part)
            value = dot_nt(da[s], up[0, dims]) + dot_nt(db[s], up[1, dims])
            core_out[s, j] = value.astype(bf16)
            core_out[s, j, cap:] = extra.astype(bf16)
        core_copy(s).start()
        for j in range(columns):
            dims = pl.ds(pl.multiple_of((row * columns + j) * part, part), part)
            keep[slot, j] = dot_nt(da[s], up[0, dims]) + dot_nt(db[s], up[1, dims])
            keep[slot, j, cap:] = extra

        @pl.when(p == 0)
        def _():
            hand_on(nth(1))
            z_copy(nth(2)).wait_send()
            z_copy(nth(3)).start()
            z_copy(nth(2)).wait_recv()
            spread(nth(2))

    def flat(ref, *at):
        block = ref[at] if at else ref[...]
        return block.reshape(experts * ext, block.shape[-1])

    before, final = nth(last - 1), nth(last)
    z_copy(final).wait_send()
    after_core(final, last % 2)
    after_core(0, 2)
    send_home(before, (last - 1) % 2)
    @pl.loop(0, experts)
    def _(s):
        slot = s % 2

        @pl.when(s > 1)
        def _():
            y_copy(s - 2, slot).wait()

        for i in range(2):
            for j in range(columns):
                dims = slice((i * columns + j) * part, (i * columns + j + 1) * part)
                core_in[2 * slot + i, j] = dot_nn(scaled[s], down[:, dims]).astype(bf16)
        y_copy(s, slot).start()

    send_home(final, last % 2)
    low = flat(scaled)
    for q in range(quarters):
        down[:, q * part : (q + 1) * part] = dot_tn(low, flat(grads, q)).astype(bf16)
    down_store().start()
    down_far().start()
    for g, hidden in enumerate((da, db)):
        low = flat(hidden)
        for q in range(quarters):
            up[g, q * part : (q + 1) * part] = dot_tn(flat(x, q), low).astype(bf16)
        up_store(g).start()
        up_far(g).start()
    home_ref[0] = after_columns(0, 2)
    for s in range(max(0, experts - 2), experts):
        y_copy(s, s % 2).wait()
    down_store().wait()
    down_far().wait()
    for g in range(2):
        up_store(g).wait()
        up_far(g).wait()

    @pl.loop(1, experts)
    def _(s):
        home_copy(s).wait_recv()
        home_copy(s).wait_send()

    @pl.loop(0, experts)
    def _(s):
        own_copy(s).wait_send()
        core_copy(s).wait_send()
        for k in range(1, columns):
            col_copy(s, k).wait_send()
            pass_copy(s, k).wait_send()
            back_copy(s, k).wait_send()


def expert_block(mixed, slots, gates, grads, up, down, columns):
    tokens, part = mixed.shape
    quarters, experts = 2 * columns, len(grads) // columns
    ext = grads[0].shape[0]
    ff = down.shape[1]
    wide = D // 2
    dma = pltpu.SemaphoreType.DMA
    hbm = pl.BlockSpec(memory_space=pl.ANY)
    others = columns - 1
    return pl.pallas_call(
        functools.partial(expert_kernel, columns, experts),
        out_shape=(
            jax.ShapeDtypeStruct((experts, ext, part), bf16),
            jax.ShapeDtypeStruct((2, columns, experts, ext, part), bf16),
            jax.ShapeDtypeStruct((2, 2, wide, ff), bf16),
            jax.ShapeDtypeStruct((2, ff, wide), bf16),
        ),
        in_specs=[vmem()] * 3 + [hbm] * (2 + len(grads)),
        out_specs=(vmem(), hbm, hbm, hbm),
        scratch_shapes=[
            pltpu.VMEM((quarters, experts, ext, part), bf16),
            pltpu.VMEM((experts, ext, part), bf16),
            pltpu.VMEM((quarters, experts, ext, part), bf16),
            pltpu.VMEM((2, D, ff), bf16),
            pltpu.VMEM((ff, D), bf16),
            pltpu.VMEM((experts, ext, ff), bf16),
            pltpu.VMEM((experts, ext, ff), bf16),
            pltpu.VMEM((experts, ext, ff), bf16),
            pltpu.VMEM((experts, columns, ext, part), bf16),
            pltpu.VMEM((experts, columns, ext, part), bf16),
            pltpu.VMEM((3, columns, ext, part), f32),
            pltpu.VMEM((experts, others, ext, part), bf16),
            pltpu.VMEM((experts, others, ext, part), bf16),
            dma((6,)), dma((experts, columns)), dma((experts, columns)), dma((experts, columns)),
            dma((experts,)), dma((experts,)), dma((experts,)), dma((experts,)),
            dma((experts, others)), dma((experts, others)), dma((experts, others)), dma((experts, others)),
            dma((experts,)), dma((experts,)), dma((experts, others)), dma((experts, others)),
            dma((experts,)), dma((experts,)), dma((2,)), dma((3,)), dma((3,)), dma((3,)),
        ],
        compiler_params=pltpu.CompilerParams(
            collective_id=2, has_side_effects=True, vmem_limit_bytes=56 * MIB
        ),
        cost_estimate=microseconds(80),
        name="expert_block",
    )(mixed, slots, gates, up, down, *grads)


def settle_kernel(
    columns, experts,
    home_ref, slot_ref, column_ref, second_ref, mixed_ref, cotangent_ref, gain_ref, router_ref,
    branch_ref, two_ref, drouter_ref, dgain_ref,
    low, stat, stat_in, stat_send, stat_recv, *spread_sems,
):
    ex = lax.axis_index("ex")
    tokens, part = second_ref.shape
    ext = home_ref.shape[1]
    cap = ext - EXTRA
    greet(grid_peers(columns))
    lane = lax.broadcasted_iota(jnp.int32, (tokens, 128), 1)
    dmixed = jnp.zeros((tokens, part), f32)
    gate_grads = jnp.zeros((tokens, 128), f32)
    for s in range(experts):
        e = (ex + s) % experts
        place = jnp.sum(jnp.where(lane == e, slot_ref[...], 0.0), axis=1, keepdims=True)
        hit = place == lax.broadcasted_iota(jnp.int32, (tokens, ext), 1).astype(f32)
        pick_rows = jnp.where(hit, 1.0, 0.0).astype(bf16)
        dmixed = dmixed + dot_nn(pick_rows, home_ref[s])
        values = read_extra(home_ref[s, cap:], ext)
        near = values.astype(bf16)
        left = (values - near.astype(f32)).astype(bf16)
        both = jnp.concatenate(
            [jnp.broadcast_to(near, (ext, 128)), jnp.broadcast_to(left, (ext, 128))], axis=1
        )
        found = dot_nn(pick_rows, both)
        gate_grads = jnp.where(lane == e, found[:, :128] + found[:, 128:], gate_grads)
    gates = jnp.where(lane < experts, column_ref[...], 0.0)
    dlogits = gate_grads - gates * jnp.sum(gate_grads, axis=1, keepdims=True)
    rows = drouter_ref.shape[0]
    drouter_ref[...] = dot_exact(dlogits, mixed_ref[...].astype(f32), ((0,), (0,)))[:rows]
    dmixed = dmixed + dot_exact(dlogits, router_ref[...], ((1,), (0,)))
    scaled = dmixed * gain_ref[...]
    stat[...] = dot_exact(jnp.ones((8, part), f32), second_ref[...] * scaled, ((1,), (1,)))
    total = sum_of_peers(stat, stat_in, stat_send, stat_recv, columns)
    first_row = jnp.where(lax.broadcasted_iota(jnp.int32, (8, 128), 0) == 0, 1.0, 0.0)
    row_total = dot_exact(total, first_row, ((0,), (0,)))[:, :1]
    inverse = column_ref[:, experts : experts + 1]
    normed = second_ref[...] * inverse
    two = cotangent_ref[...].astype(f32) + inverse * (
        scaled - normed * (inverse * row_total / D)
    )
    two_ref[...] = two
    low[...] = two.astype(bf16)
    spread = Spread(branch_ref, low, columns, *spread_sems)
    spread.start()
    dgain_ref[...] = jnp.broadcast_to(jnp.sum(dmixed * normed, axis=0, keepdims=True), dgain_ref.shape)
    spread.hand_on()
    spread.finish()


def settle(home, slots, table, second, mixed, cotangent, gain, router_rows, rows, experts, columns):
    tokens, part = second.shape
    quarters = 2 * columns
    dma = pltpu.SemaphoreType.DMA
    return pl.pallas_call(
        functools.partial(settle_kernel, columns, experts),
        out_shape=(
            jax.ShapeDtypeStruct((quarters, tokens, part), bf16),
            jax.ShapeDtypeStruct((tokens, part), f32),
            jax.ShapeDtypeStruct((rows, part), f32),
            jax.ShapeDtypeStruct((8, part), f32),
        ),
        in_specs=[vmem()] * 8,
        out_specs=(vmem(),) * 4,
        scratch_shapes=[
            pltpu.VMEM((tokens, part), bf16),
            pltpu.VMEM((8, tokens), f32),
            pltpu.VMEM((quarters - 1, 8, tokens), f32),
            dma((quarters - 1,)), dma((quarters - 1,)),
        ]
        + spread_semaphores(columns),
        compiler_params=pltpu.CompilerParams(
            collective_id=3, has_side_effects=True, vmem_limit_bytes=40 * MIB
        ),
        cost_estimate=microseconds(25),
        name="settle",
    )(home, slots, table, second, mixed, cotangent, gain, router_rows)


def finish_kernel(
    columns, experts,
    dfirst_ref, dweight_ref, small_ref, layer_ref, two_ref, gain_ref, inverse_ref,
    input_grad_ref, grad_ref, sums_ref,
    core_in, keep, col_out, col_in, stat, stat_in, y_in, z_out, z_in, held, row_out, row_in, small, small_in,
    core_send, core_recv, col_send, col_recv, stat_send, stat_recv,
    y_send, y_recv, z_send, z_recv, row_send, row_recv, small_send, small_recv,
):
    ex, half = lax.axis_index("ex"), lax.axis_index("half")
    row, col = lax.axis_index("row"), lax.axis_index("col")
    tokens, part = layer_ref.shape
    size = tokens // PIECES
    members = 2 * experts
    others = [
        {"ex": (ex + s) % experts, "half": (half + h) % 2}
        for s in range(experts)
        for h in range(2)
        if s + h > 0
    ]
    greet(grid_peers(columns) + others)

    def core_copy(i):
        at = pl.ds(i * size, size)
        return remote(
            dfirst_ref.at[pl.ds((1 - row) * columns, columns), at], core_in.at[:, at],
            core_send.at[i], core_recv.at[i], {"row": 1 - row},
        )

    def y_copy(s):
        to = 2 * ((ex + s) % experts) + 1 - half
        return remote(dweight_ref.at[:, to], y_in.at[s], y_send.at[s], y_recv.at[s], {"half": 1 - half})

    def z_copy(s):
        return remote(z_out.at[s], z_in.at[s], z_send.at[s], z_recv.at[s], {"ex": (ex + s) % experts})

    for i in range(PIECES):
        core_copy(i).start()
    order = list(range(1, experts)) + [0]
    for s in order:
        y_copy(s).start()
    crossing = []
    for i in range(PIECES):
        at = slice(i * size, (i + 1) * size)
        core_copy(i).wait_recv()
        for j in range(columns):
            keep[j, at] = dfirst_ref[row * columns + j, at].astype(f32) + core_in[j, at].astype(f32)
        for k in range(1, columns):
            to = (col + k) % columns
            col_out[k - 1, at] = keep[to, at].astype(bf16)
            copy = remote(
                col_out.at[k - 1, pl.ds(i * size, size)], col_in.at[k - 1, pl.ds(i * size, size)],
                col_send.at[i, k - 1], col_recv.at[i, k - 1], {"col": to},
            )
            copy.start()
            crossing.append(copy)
    for s in order:
        y_copy(s).wait_recv()
        total = dweight_ref[:, 2 * ((ex + s) % experts) + half].astype(f32) + y_in[s].astype(f32)
        if s > 0:
            z_out[s] = total.astype(bf16)
            z_copy(s).start()
        else:
            held[...] = total
    for copy in crossing:
        copy.wait_recv()
    dnorm = keep[col]
    for k in range(1, columns):
        dnorm = dnorm + col_in[k - 1].astype(f32)
    v = layer_ref[...].astype(f32)
    scaled = dnorm * gain_ref[...]
    stat[...] = dot_exact(jnp.ones((8, part), f32), v * scaled, ((1,), (1,)))
    total = sum_of_peers(stat, stat_in, stat_send, stat_recv, columns)
    first_row = jnp.where(lax.broadcasted_iota(jnp.int32, (8, 128), 0) == 0, 1.0, 0.0)
    row_total = dot_exact(total, first_row, ((0,), (0,)))[:, :1]
    inverse = inverse_ref[:, 127:128]
    normed = v * inverse
    input_grad_ref[...] = (
        two_ref[...] + inverse * (scaled - normed * (inverse * row_total / D))
    ).astype(bf16)
    small[...] = small_ref[...]
    small[:8] = jnp.broadcast_to(jnp.sum(dnorm * normed, axis=0, keepdims=True), (8, part))
    smalls = [
        remote(small, small_in.at[i], small_send.at[i], small_recv.at[i], where)
        for i, where in enumerate(others)
    ]
    for copy in smalls:
        copy.start()
    for s in range(1, experts):
        z_copy(s).wait_recv()
        held[...] = held[...] + z_in[s].astype(f32)
    row_out[...] = held[1 - row].astype(bf16)
    swap = remote(row_out, row_in, row_send.at[0], row_recv.at[0], {"row": 1 - row})
    swap.start()
    grad_ref[row] = held[row]
    sums = small[...]
    for i, copy in enumerate(smalls):
        copy.wait_recv()
        sums = sums + small_in[i]
    sums_ref[...] = sums
    swap.wait_recv()
    grad_ref[1 - row] = row_in[...].astype(f32)
    swap.wait_send()
    for copy in smalls + crossing:
        copy.wait_send()
    for i in range(PIECES):
        core_copy(i).wait_send()
    for s in range(experts):
        y_copy(s).wait_send()
        if s > 0:
            z_copy(s).wait_send()


def finish(dfirst, dweight, small, layer_in, two, gain, table, experts, columns):
    quarters, tokens, part = dfirst.shape
    _, members, rows, width = dweight.shape
    dma = pltpu.SemaphoreType.DMA
    others = columns - 1
    return pl.pallas_call(
        functools.partial(finish_kernel, columns, experts),
        out_shape=(
            jax.ShapeDtypeStruct((tokens, part), bf16),
            jax.ShapeDtypeStruct((2, rows, width), f32),
            jax.ShapeDtypeStruct(small.shape, f32),
        ),
        in_specs=[vmem()] * 7,
        out_specs=(vmem(),) * 3,
        scratch_shapes=[
            pltpu.VMEM((columns, tokens, part), bf16),
            pltpu.VMEM((columns, tokens, part), f32),
            pltpu.VMEM((others, tokens, part), bf16),
            pltpu.VMEM((others, tokens, part), bf16),
            pltpu.VMEM((8, tokens), f32),
            pltpu.VMEM((quarters - 1, 8, tokens), f32),
            pltpu.VMEM((experts, 2, rows, width), bf16),
            pltpu.VMEM((experts, 2, rows, width), bf16),
            pltpu.VMEM((experts, 2, rows, width), bf16),
            pltpu.VMEM((2, rows, width), f32),
            pltpu.VMEM((rows, width), bf16),
            pltpu.VMEM((rows, width), bf16),
            pltpu.VMEM(small.shape, f32),
            pltpu.VMEM((members - 1,) + small.shape, f32),
            dma((PIECES,)), dma((PIECES,)), dma((PIECES, others)), dma((PIECES, others)),
            dma((quarters - 1,)), dma((quarters - 1,)),
            dma((experts,)), dma((experts,)), dma((experts,)), dma((experts,)),
            dma((1,)), dma((1,)), dma((members - 1,)), dma((members - 1,)),
        ],
        compiler_params=pltpu.CompilerParams(
            collective_id=4, has_side_effects=True, vmem_limit_bytes=50 * MIB
        ),
        cost_estimate=microseconds(32),
        name="finish",
    )(dfirst, dweight, small, layer_in, two, gain, table)


def adamw_step(weight, grad, first, second, rate):
    first_new = beta_first * first + (1.0 - beta_first) * grad
    second_new = beta_second * second + (1.0 - beta_second) * grad * grad
    moment = first_new / (1.0 - beta_first**STEP)
    spread = second_new / (1.0 - beta_second**STEP)
    weight_new = weight - rate * (
        moment / (jnp.sqrt(spread) + adam_epsilon) + weight_decay * weight
    )
    return (weight_new, first_new, second_new)


def pick(values, index):
    return lax.dynamic_index_in_dim(values, index, 0, keepdims=False)


def local(
    layer_in, lengths, placing, routes, cotangent,
    norm_gains, gain_first, gain_second, rel_bias, bias_first, bias_second,
    router, router_first, router_second, qkv_weight, qkv_first, qkv_second,
    proj_weight, proj_first, proj_second, expert_up, up_first, up_second,
    expert_down, down_first, down_second,
):
    tokens, part = layer_in.shape
    experts, columns = lax.axis_size("ex"), lax.axis_size("col")
    quarters = 2 * columns
    ex, half, row = lax.axis_index("ex"), lax.axis_index("half"), lax.axis_index("row")
    cap = min(tokens, 5 * TOP * tokens // (4 * experts))
    ext = cap + EXTRA
    hc = qkv_weight.shape[5]
    head_count = hc // HD
    wide = D // 2

    qkv_low = jnp.moveaxis(qkv_weight[0, 0].astype(bf16), 1, 0).reshape(2, -1, 3 * hc)
    proj_low = jnp.swapaxes(proj_weight[:, :, 0, 0].astype(bf16), 1, 2)
    shard = jnp.concatenate([qkv_low, proj_low], axis=2)
    gains_eight = jnp.pad(norm_gains, ((0, 6), (0, 0)))
    x_all, gains_all, weight = gather(layer_in, gains_eight, shard, experts, columns)
    weight = weight.reshape(D, 4 * hc)

    places = placing[0]
    given_routes = jnp.zeros_like(routes).at[places].set(routes)
    flat = given_routes.reshape(-1)
    numbers = jnp.arange(experts, dtype=jnp.int32)
    hits = (flat[:, None] == numbers[None, :]).astype(jnp.int32)
    before = jnp.cumsum(hits, axis=0)
    slot_of = jnp.sum((before * hits).reshape(tokens, TOP, experts), axis=1) - 1
    one_hot = (slot_of.T[:, None, :] == jnp.arange(ext, dtype=jnp.int32)[None, :, None]).astype(bf16)
    stat_rows = (experts + 8) // 8 * 8
    slot_rows = jnp.pad(slot_of.T, ((0, stat_rows - experts), (0, 0)), constant_values=-1)
    slot_columns = jnp.pad(slot_of.astype(f32), ((0, 0), (0, 128 - experts)), constant_values=-1.0)

    def exchange(values):
        return lax.all_to_all(values, "ex", split_axis=0, concat_axis=0, tiled=True)

    turned = (ex - numbers + experts) % experts
    slot_grads = jnp.einsum("est,tf->esf", one_hot, cotangent, preferred_element_type=f32).astype(bf16)
    up_low = jnp.swapaxes(lax.optimization_barrier(expert_up[0].astype(bf16)), 0, 1)
    down_low = expert_down[0].astype(bf16)

    x_all, slot_grads, up_low, down_low = lax.optimization_barrier((x_all, slot_grads, up_low, down_low))
    grad_rows = []
    for s in range(experts):
        block = pick(slot_grads, (ex + s) % experts)
        if s > 0:
            block = lax.ppermute(block, "ex", [(i, (i + s) % experts) for i in range(experts)])
        grad_rows.append(block)
    up_both = lax.all_gather(up_low.reshape(-1, up_low.shape[2]), "half", axis=0, tiled=True)
    up_both = up_both.reshape((2,) + up_low.shape)
    down_both = lax.all_gather(down_low, "half", axis=0, tiled=True).reshape((2,) + down_low.shape)

    ends = jnp.cumsum(lengths[0])
    at = jnp.arange(tokens, dtype=jnp.int32)
    starts = jnp.max(jnp.where(ends[None, :] <= at[:, None], ends[None, :], 0), axis=1).astype(jnp.int32)
    vectors = bias_vectors(rel_bias, tokens)
    first, qkv, attended, lse = attention_forward(
        x_all, gains_all, weight, places[None, :], places[:, None], starts[:, None], vectors
    )
    attended, *grad_rows = lax.optimization_barrier((attended, *grad_rows))
    grad_blocks = [
        lax.ppermute(block, "col", [(i, (i + k) % columns) for i in range(columns)]) if k else block
        for block in grad_rows
        for k in range(columns)
    ]
    router_rows = jnp.pad((norm_gains[1][:, None] * router).T, ((0, stat_rows - experts), (0, 0)))
    second, mixed, gates, table = project(
        attended, weight, layer_in, norm_gains[1:], router_rows, slot_rows, experts, columns
    )

    home, y, dup, ddown = expert_block(
        mixed, slot_rows, gates, grad_blocks, up_both, down_both, columns
    )
    branch, grad_two, drouter, dgain_two = settle(
        home, slot_columns, table, second, mixed, cotangent, norm_gains[1:],
        jnp.pad(router.T, ((0, 128 - experts), (0, 0))), stat_rows, experts, columns,
    )
    y_home = lax.psum_scatter(y.reshape(quarters, experts, ext, part), ("row", "col"), scatter_dimension=0, tiled=False)
    y_home = exchange(jnp.take(y_home, turned, axis=0))
    gained = jnp.einsum("est,esf->tf", one_hot, y_home, preferred_element_type=f32)
    layer_out = (second + gained).astype(bf16)

    dfirst, dweight, dvectors = attention_backward(
        branch, qkv, lse, attended, first, weight, places[None, :], places[:, None], starts[:, None], vectors
    )
    small = jnp.concatenate([jnp.zeros((8, part), f32), dgain_two, drouter, dvectors.reshape(-1, part)])
    input_grad, grad_parts, sums = finish(
        dfirst, dweight.reshape(2, 2 * experts, -1, 4 * hc), small, layer_in, grad_two, norm_gains[:1], lse,
        experts, columns,
    )
    grad_gains = jnp.stack([sums[0], sums[8]])
    grad_router = sums[16 : 16 + experts].T
    grad_bias = bias_gradient(sums[16 + stat_rows :].reshape(dvectors.shape), head_count, tokens)
    grad_qkv = jnp.moveaxis(grad_parts[:, :, : 3 * hc], 0, 1).reshape(qkv_weight.shape)
    grad_proj = jnp.swapaxes(grad_parts[:, :, 3 * hc :], 1, 2).reshape(proj_weight.shape)

    def sum_halves(parts):
        other = lax.ppermute(pick(parts, 1 - half), "half", [(0, 1), (1, 0)])
        return (pick(parts, half).astype(f32) + other.astype(f32)).astype(bf16)

    grad_up = with_layout_constraint(jnp.swapaxes(sum_halves(dup), 0, 1), Layout((0, 1, 2)))
    grad_up = grad_up[None].astype(f32)
    grad_down = sum_halves(ddown)[None].astype(f32)

    gains = adamw_step(norm_gains, grad_gains, gain_first, gain_second, 0.5)
    bias = adamw_step(rel_bias, grad_bias, bias_first, bias_second, 1.0)
    routers = adamw_step(router, grad_router, router_first, router_second, 2.0 * (2 * D) ** (-0.5))
    qkvs = adamw_step(qkv_weight, grad_qkv, qkv_first, qkv_second, 2.0 * D ** (-0.5))
    projs = adamw_step(proj_weight, grad_proj, proj_first, proj_second, 2.0 * (HEADS * HD / 8) ** (-0.5))
    ups = adamw_step(expert_up, grad_up, up_first, up_second, 2.0 * D ** (-0.5))
    downs = adamw_step(expert_down, grad_down, down_first, down_second, 2.0 * (FF / 2) ** (-0.5))
    out = (layer_out, input_grad) + gains + bias + routers
    for group in (qkvs, projs, ups, downs):
        out = out + group + (group[0].astype(bf16),)
    return out


def solution(mesh):
    shape = mesh.devices.shape
    fine = Mesh(
        mesh.devices.reshape((shape[0] // 2, 2) + shape[1:]), ("ex", "half", "row", "col")
    )
    dp, grid = ("ex", "half"), ("row", "col")
    tokens, own = P(dp, grid), P(dp, None)
    gain, router = P(None, grid), P(grid, None)
    qkv, proj = P("row", dp, None, None, None, "col"), P(None, "col", "row", dp, None)
    up, down = P(dp, "row", None, "col"), P(dp, "col", "row")
    in_specs = (
        (tokens, own, own, own, tokens) + (gain,) * 6 + (router,) * 3
        + (qkv,) * 3 + (proj,) * 3 + (up,) * 3 + (down,) * 3
    )
    out_specs = (
        (tokens, tokens) + (gain,) * 6 + (router,) * 3
        + (qkv,) * 4 + (proj,) * 4 + (up,) * 4 + (down,) * 4
    )
    return jax.shard_map(local, mesh=fine, in_specs=in_specs, out_specs=out_specs, check_vma=False)
```

```python
import functools

import jax
import jax.numpy as jnp
import numpy as np
from jax import lax
from jax.experimental import pallas as pl
from jax.experimental.pallas import tpu as pltpu
from jax.sharding import Mesh, PartitionSpec as P

D = 1024
HEADS = 16
FF = 2816
TOP = 2
STEP = 5
beta_first = 0.5
beta_second = 0.5
adam_epsilon = 1e-08
weight_decay = 0.01
highest = lax.Precision.HIGHEST
EXTRA = 16
HD = 64
BUCKETS = 32
LONGEST = 512
TILE = 256
norm_epsilon = 1e-06
hidden_score = -1e30
bucket_edges = np.floor(16.0 * 2.0 ** (np.arange(16) * 0.375)).astype(np.int32)
f32 = jnp.float32
bf16 = jnp.bfloat16
MIB = 1 << 20


def dot_nn(a, b):
    return lax.dot_general(a, b, (((1,), (0,)), ((), ())), preferred_element_type=f32)


def dot_nt(a, b):
    return lax.dot_general(a, b, (((1,), (1,)), ((), ())), preferred_element_type=f32)


def dot_tn(a, b):
    return lax.dot_general(a, b, (((0,), (0,)), ((), ())), preferred_element_type=f32)


def tile_reach(tokens):
    return min(tokens // TILE, (LONGEST - 1 + TILE - 1) // TILE + 1)


def toeplitz_places(tokens):
    reach = tile_reach(tokens)
    m = np.arange(2 * TILE)
    base = np.where(m < TILE, -m, 2 * TILE - m)
    distance = np.arange(reach)[:, None] * TILE + base[None, :]
    clipped = np.maximum(distance, 0)
    buckets = np.where(
        clipped < 16, clipped, 15 + (clipped[..., None] >= bucket_edges).sum(-1)
    )
    return (distance, buckets)


def bias_vectors(rel_bias, tokens):
    distance, buckets = toeplitz_places(tokens)
    table = jnp.asarray((buckets[..., None] == np.arange(BUCKETS)).astype(np.float32))
    values = jnp.einsum("dmb,bh->hdm", table, rel_bias, precision=lax.Precision.HIGHEST)
    values = jnp.where(jnp.asarray(distance < 0)[None], hidden_score, values)
    return values.reshape(-1, 2 * TILE)


def bias_gradient(vectors, head_count, tokens):
    distance, buckets = toeplitz_places(tokens)
    table = ((buckets[..., None] == np.arange(BUCKETS)) & (distance >= 0)[..., None]).astype(np.float32)
    return jnp.einsum(
        "dmb,hdm->bh",
        jnp.asarray(table),
        vectors.reshape(head_count, distance.shape[0], 2 * TILE),
        precision=lax.Precision.HIGHEST,
    )


def fill_bias(vector_ref, bias):
    for i in range(bias.shape[0]):
        wide = jnp.broadcast_to(vector_ref[i : i + 1, :], (TILE, 2 * TILE))
        bias[i] = pltpu.roll(wide, 0, 1, stride=1, stride_axis=0)[:, :TILE]


def head_lanes(shape, head):
    return lax.broadcasted_iota(jnp.int32, shape, 1) // HD == head


def given_table(place_row, tokens):
    return jnp.where(
        place_row[...] == lax.broadcasted_iota(jnp.int32, (tokens, tokens), 0), 1.0, 0.0
    ).astype(bf16)


def sequence_starts(length_ref, tokens):
    at = lax.broadcasted_iota(jnp.int32, (tokens, 1), 0)
    starts = jnp.zeros((tokens, 1), jnp.int32)
    end = 0
    for k in range(length_ref.shape[1]):
        end = end + length_ref[0, k]
        starts = jnp.where(at >= end, end, starts)
    return starts


def attention_forward_kernel(
    x_ref, gain_ref, weight_ref, place_row, length_ref, vector_ref,
    first_ref, qkv_ref, attended_ref, lse_ref, bias, placed_out, between,
):
    quarters, tokens, part = x_ref.shape
    width = quarters * part
    hc = weight_ref.shape[1] // 4
    head_count = hc // HD
    reach = bias.shape[0] // head_count
    fill_bias(vector_ref, bias)
    squares = jnp.zeros((tokens, 1), f32)
    for q in range(quarters):
        v = x_ref[q].astype(f32)
        squares = squares + jnp.sum(v * v, axis=1, keepdims=True)
    inverse = lax.rsqrt(squares / width + norm_epsilon)
    total = jnp.zeros((tokens, 3 * hc), f32)
    for q in range(quarters):
        first = (x_ref[q].astype(f32) * inverse * gain_ref[q, :1]).astype(bf16)
        first_ref[q] = first
        total = total + dot_nn(first, weight_ref[q * part : (q + 1) * part, : 3 * hc])
    to_given = given_table(place_row, tokens)
    all_starts = sequence_starts(length_ref, tokens)
    scale = jnp.where(
        lax.broadcasted_iota(jnp.int32, (1, 3 * hc), 1) < hc, HD ** (-0.5), 1.0
    )
    qkv_ref[...] = dot_tn(to_given, (total * scale).astype(bf16)).astype(bf16)
    between(-1)
    for a in range(tokens // TILE):
        rows = slice(a * TILE, (a + 1) * TILE)
        blocks = range(max(0, a - reach + 1), a + 1)
        starts = all_starts[rows, :]
        visible = [
            b * TILE + lax.broadcasted_iota(jnp.int32, (TILE, TILE), 1) >= starts for b in blocks
        ]

        def one_head(head, carry):
            out, lse = carry
            mine = head_lanes((TILE, hc), head)
            query = jnp.where(mine, qkv_ref[rows, :hc], 0)
            scores = []
            for b, seen in zip(blocks, visible):
                s = dot_nt(query, qkv_ref[b * TILE : (b + 1) * TILE, hc : 2 * hc])
                scores.append(jnp.where(seen, s + bias[head * reach + a - b], hidden_score))
            top = functools.reduce(jnp.maximum, [jnp.max(s, axis=1, keepdims=True) for s in scores])
            exps = [jnp.exp(s - top) for s in scores]
            denominator = functools.reduce(jnp.add, [jnp.sum(e, axis=1, keepdims=True) for e in exps])
            share = 1.0 / denominator
            value = jnp.zeros((TILE, hc), f32)
            for b, e in zip(blocks, exps):
                value = value + dot_nn(
                    (e * share).astype(bf16), qkv_ref[b * TILE : (b + 1) * TILE, 2 * hc :]
                )
            lane = lax.broadcasted_iota(jnp.int32, (TILE, 128), 1)
            return (
                jnp.where(mine, value, out),
                jnp.where(lane == head, top + jnp.log(denominator), lse),
            )

        out, lse = lax.fori_loop(
            0, head_count, one_head, (jnp.zeros((TILE, hc), f32), jnp.zeros((TILE, 128), f32))
        )
        placed_out[rows, :] = out.astype(bf16)
        lse_ref[rows, :] = lse
        between(a)
    lane = lax.broadcasted_iota(jnp.int32, (tokens, 128), 1)
    lse_ref[...] = jnp.where(lane == 127, inverse, lse_ref[...])
    attended_ref[...] = dot_nn(to_given, placed_out[...]).astype(bf16)


def microseconds(time):
    return pl.CostEstimate(flops=0, bytes_accessed=int(time * 3.5e6), transcendentals=0)


def vmem():
    return pl.BlockSpec(memory_space=pltpu.VMEM)


def hbm():
    return pl.BlockSpec(memory_space=pltpu.HBM)


def attention_backward_kernel(
    branch_ref, qkv_ref, lse_ref, attended_ref, first_ref, weight_ref,
    place_row, length_ref, vector_ref,
    dfirst_ref, dweight_ref, dvector_ref,
    bias, dbias, grad_ref, dqkv, dkv, between, after_dfirst,
):
    quarters, tokens, part = branch_ref.shape
    hc = weight_ref.shape[1] // 4
    head_count = hc // HD
    reach = bias.shape[0] // head_count
    fill_bias(vector_ref, bias)
    dbias[...] = jnp.zeros_like(dbias)
    dkv[...] = jnp.zeros_like(dkv)
    total = jnp.zeros((tokens, hc), f32)
    for q in range(quarters):
        dims = slice(q * part, (q + 1) * part)
        total = total + dot_nn(branch_ref[q], weight_ref[dims, 3 * hc :])
        dweight_ref[dims, 3 * hc :] = dot_tn(branch_ref[q], attended_ref[...]).astype(bf16)
    to_given = given_table(place_row, tokens)
    all_starts = sequence_starts(length_ref, tokens)
    grad_ref[...] = dot_tn(to_given, total.astype(bf16)).astype(bf16)
    for a in range(tokens // TILE):
        rows = slice(a * TILE, (a + 1) * TILE)
        blocks = range(max(0, a - reach + 1), a + 1)
        starts = all_starts[rows, :]
        visible = [
            b * TILE + lax.broadcasted_iota(jnp.int32, (TILE, TILE), 1) >= starts for b in blocks
        ]

        def one_head(head, dquery):
            mine = head_lanes((TILE, hc), head)
            query = jnp.where(mine, qkv_ref[rows, :hc], 0)
            grad = jnp.where(mine, grad_ref[rows, :], 0)
            lane = lax.broadcasted_iota(jnp.int32, (TILE, 128), 1)
            lse = jnp.sum(jnp.where(lane == head, lse_ref[rows, :], 0.0), axis=1, keepdims=True)
            probs, dprobs = [], []
            inner = jnp.zeros((TILE, 1), f32)
            for b, seen in zip(blocks, visible):
                keys = slice(b * TILE, (b + 1) * TILE)
                s = dot_nt(query, qkv_ref[keys, hc : 2 * hc]) + bias[head * reach + a - b]
                p = jnp.where(seen, jnp.exp(s - lse), 0.0)
                d = dot_nt(grad, qkv_ref[keys, 2 * hc :])
                inner = inner + jnp.sum(p * d, axis=1, keepdims=True)
                probs.append(p)
                dprobs.append(d)
            for b, p, d in zip(blocks, probs, dprobs):
                keys = slice(b * TILE, (b + 1) * TILE)
                ds = p * (d - inner)
                place = head * reach + a - b
                dbias[place] = dbias[place] + ds
                low = ds.astype(bf16)
                dquery = dquery + dot_nn(low, jnp.where(mine, qkv_ref[keys, hc : 2 * hc], 0))
                dkv[keys, :hc] = dkv[keys, :hc] + dot_tn(low, query)
                dkv[keys, hc:] = dkv[keys, hc:] + dot_tn(p.astype(bf16), grad)
            return dquery

        dquery = lax.fori_loop(0, head_count, one_head, jnp.zeros((TILE, hc), f32))
        dqkv[rows, :hc] = (dquery * HD ** (-0.5)).astype(bf16)
        between(a)
    dqkv[:, hc:] = dkv[...].astype(bf16)
    given = dot_nn(to_given, dqkv[...]).astype(bf16)
    for q in range(quarters):
        dfirst_ref[q] = dot_nt(given, weight_ref[q * part : (q + 1) * part, : 3 * hc]).astype(bf16)
    after_dfirst()
    for q in range(quarters):
        dims = slice(q * part, (q + 1) * part)
        dweight_ref[dims, : 3 * hc] = dot_tn(first_ref[q], given).astype(bf16)
    for i in range(dbias.shape[0]):
        wide = jnp.concatenate([dbias[i], jnp.zeros((TILE, TILE), f32)], axis=1)
        level = wide[:8]
        for g in range(8, TILE, 8):
            level = level + pltpu.roll(wide[g : g + 8], 2 * TILE - g, 1)
        row = level[:1]
        for s in range(1, 8):
            row = row + pltpu.roll(level[s : s + 1], 2 * TILE - s, 1)
        dvector_ref[i : i + 1, :] = row


def half_places(rows, part):
    row = lax.broadcasted_iota(jnp.int32, (rows, EXTRA), 0) // part
    high = lax.broadcasted_iota(jnp.int32, (rows, EXTRA), 1)
    column = lax.broadcasted_iota(jnp.int32, (rows, part), 0) % part
    return (row, high, column == lax.broadcasted_iota(jnp.int32, (rows, part), 1))


def write_extra(values, part):
    row, high, column = half_places(values.shape[0], part)
    near = values.astype(bf16)
    left = (values - near.astype(f32)).astype(bf16)
    near_rows = jnp.where(row == high, 1.0, 0.0).astype(bf16)
    left_rows = jnp.where(row + 8 == high, 1.0, 0.0).astype(bf16)
    near_values = jnp.where(column, near.astype(f32), 0.0).astype(bf16)
    left_values = jnp.where(column, left.astype(f32), 0.0).astype(bf16)
    return dot_tn(near_rows, near_values) + dot_tn(left_rows, left_values)


def read_extra(extra, rows):
    part = extra.shape[1]
    row, high, column = half_places(rows, part)
    pick = jnp.where(row == high % 8, 1.0, 0.0).astype(bf16)
    return jnp.sum(jnp.where(column, dot_nn(pick, extra), 0.0), axis=1, keepdims=True)


GELU_A = 0.7978845608028654
GELU_B = 0.044715


MESH = pl.DeviceIdType.MESH


def remote(src, dst, send, recv, where):
    return pltpu.make_async_remote_copy(
        src_ref=src, dst_ref=dst, send_sem=send, recv_sem=recv, device_id=where, device_id_type=MESH
    )


def greet(wheres):
    barrier = pltpu.get_barrier_semaphore()
    for where in wheres:
        pl.semaphore_signal(barrier, inc=1, device_id=where, device_id_type=MESH)
    pl.semaphore_wait(barrier, len(wheres))


def dot_exact(a, b, dims):
    return lax.dot_general(a, b, ((dims, ((), ()))), precision=highest, preferred_element_type=f32)


def grid_peers(columns):
    row, col = lax.axis_index("row"), lax.axis_index("col")
    return [
        {"row": (row + i) % 2, "col": (col + j) % columns}
        for i in range(2)
        for j in range(columns)
        if i + j > 0
    ]


def sum_of_peers(mine, got, send, recv, columns):
    copies = [
        remote(mine, got.at[i], send.at[i], recv.at[i], where)
        for i, where in enumerate(grid_peers(columns))
    ]
    for copy in copies:
        copy.start()
    for copy in copies:
        copy.wait_recv()
    total = mine[...]
    for i in range(len(copies)):
        total = total + got[i]
    for copy in copies:
        copy.wait_send()
    return total


PIECES = 4


def project_part(
    columns, experts,
    attended_ref, weight_ref, layer_ref, gain_ref, router_ref, slot_ref,
    second_ref, mixed_ref, gate_ref, column_ref,
    core_out, core_in, keep, col_out, col_in, stat, stat_in,
    core_send, core_recv, col_send, col_recv, stat_send, stat_recv, after_crossing,
):
    row, col = lax.axis_index("row"), lax.axis_index("col")
    tokens, part = layer_ref.shape
    wide = columns * part
    size = tokens // PIECES
    heads = slice(3 * weight_ref.shape[1] // 4, weight_ref.shape[1])
    own_rows = pl.ds(pl.multiple_of(row * wide, wide), wide)
    other_rows = pl.ds(pl.multiple_of((1 - row) * wide, wide), wide)
    cores = []
    for i in range(PIECES):
        at = slice(i * size, (i + 1) * size)
        core_out[i] = dot_nt(attended_ref[at, :], weight_ref[other_rows, heads]).astype(bf16)
        copy = remote(core_out.at[i], core_in.at[i], core_send.at[i], core_recv.at[i], {"row": 1 - row})
        copy.start()
        cores.append(copy)
        keep[i] = dot_nt(attended_ref[at, :], weight_ref[own_rows, heads])
    own_columns = pl.ds(pl.multiple_of(col * part, part), part)
    crossing = []
    for i in range(PIECES):
        cores[i].wait_recv()
        keep[i] = keep[i] + core_in[i].astype(f32)
        for k in range(1, columns):
            to = (col + k) % columns
            col_out[i, k - 1] = keep[i, :, pl.ds(pl.multiple_of(to * part, part), part)].astype(bf16)
            copy = remote(
                col_out.at[i, k - 1], col_in.at[i, k - 1], col_send.at[i, k - 1], col_recv.at[i, k - 1], {"col": to}
            )
            copy.start()
            crossing.append(copy)
    after_crossing()
    ones = jnp.where(lax.broadcasted_iota(jnp.int32, router_ref.shape, 0) == experts, 1.0, 0.0)
    for i in range(PIECES):
        at = slice(i * size, (i + 1) * size)
        total = layer_ref[at, :].astype(f32) + keep[i, :, own_columns]
        for k in range(1, columns):
            crossing[i * (columns - 1) + k - 1].wait_recv()
            total = total + col_in[i, k - 1].astype(f32)
        second_ref[at, :] = total
        stat[:, at] = dot_exact(router_ref[...] * gain_ref[...], total, ((1,), (1,))) + dot_exact(
            ones, total * total, ((1,), (1,))
        )
    total = sum_of_peers(stat, stat_in, stat_send, stat_recv, columns)
    inverse = lax.rsqrt(total[experts : experts + 1] / D + norm_epsilon)
    routed = slot_ref[...] >= 0
    logits = jnp.where(routed, total * inverse, hidden_score)
    shares = jnp.where(routed, jnp.exp(logits - jnp.max(logits, axis=0, keepdims=True)), 0.0)
    gates = shares / jnp.sum(shares, axis=0, keepdims=True)
    gate_ref[...] = gates
    number = lax.broadcasted_iota(jnp.int32, gates.shape, 0)
    lanes = (gates.shape[0], 128)
    eye = jnp.where(
        lax.broadcasted_iota(jnp.int32, lanes, 0) == lax.broadcasted_iota(jnp.int32, lanes, 1), 1.0, 0.0
    )
    table = dot_exact(jnp.where(number == experts, inverse, gates), eye, ((0,), (0,)))
    column_ref[...] = table
    mixed_ref[...] = (second_ref[...] * table[:, experts : experts + 1] * gain_ref[...]).astype(bf16)
    for copy in cores + crossing:
        copy.wait_send()


def nearest_first(experts):
    return sorted(range(1, experts), key=lambda s: min(s, experts - s))


def farthest_first(experts):
    far = experts // 2
    return [far] + [s for s in range(1, experts) if s != far]


def attend_kernel(columns, experts, *refs):
    x_hbm, gains_ref, weight_hbm, place_row, length_ref, vector_ref, layer_ref, gain_ref, router_ref, slot_ref = refs[:10]
    grad_rows = refs[10 : 10 + experts]
    (
        first_hbm, qkv_hbm, attended_hbm, lse_hbm, second_hbm, column_hbm, mixed_ref, gate_ref, came, crossed,
        first_ref, qkv_ref, attended_ref, lse_ref, second_ref, column_ref,
        bias, placed_out, core_out, core_in, keep, col_out, col_in, stat, stat_in,
        core_send, core_recv, col_send, col_recv, stat_send, stat_recv,
        z_send, z_recv, x_send, x_recv, store, x_ref, weight_ref, load,
    ) = refs[10 + experts :]
    loads = [
        pltpu.make_async_copy(x_hbm, x_ref, load.at[0]),
        pltpu.make_async_copy(weight_hbm, weight_ref, load.at[1]),
    ]
    for copy in loads:
        copy.start()
    ex, col = lax.axis_index("ex"), lax.axis_index("col")
    greet(grid_peers(columns) + [{"ex": (ex + s) % experts} for s in range(1, experts)])

    def z_copy(s):
        return remote(grad_rows[s], came.at[s], z_send.at[s], z_recv.at[s], {"ex": (ex + s) % experts})

    def x_copy(s, k):
        return remote(
            came.at[s], crossed.at[s, k - 1], x_send.at[s, k - 1], x_recv.at[s, k - 1], {"col": (col + k) % columns}
        )

    order = farthest_first(experts)
    z_copy(order[0]).start()
    done = [0]
    for copy in loads:
        copy.wait()

    def advance():
        n = done[0]
        z_copy(order[n]).wait_send()
        if n + 1 < len(order):
            z_copy(order[n + 1]).start()
        z_copy(order[n]).wait_recv()
        if n + 1 < len(order):
            for k in range(1, columns):
                x_copy(order[n], k).start()
        done[0] = n + 1

    def between(a):
        if a == 2:
            advance()

    attention_forward_kernel(
        x_ref, gains_ref, weight_ref, place_row, length_ref, vector_ref,
        first_ref, qkv_ref, attended_ref, lse_ref, bias, placed_out, between,
    )

    def stored(pairs, first):
        copies = [pltpu.make_async_copy(a, b, store.at[first + i]) for i, (a, b) in enumerate(pairs)]
        for copy in copies:
            copy.start()
        return copies

    stores = stored(
        [(first_ref, first_hbm), (qkv_ref, qkv_hbm), (attended_ref, attended_hbm), (lse_ref, lse_hbm)], 0
    )

    def after_crossing():
        while done[0] + 1 < len(order):
            advance()

    project_part(
        columns, experts,
        attended_ref, weight_ref, layer_ref, gain_ref, router_ref, slot_ref,
        second_ref, mixed_ref, gate_ref, column_ref,
        core_out, core_in, keep, col_out, col_in, stat, stat_in,
        core_send, core_recv, col_send, col_recv, stat_send, stat_recv, after_crossing,
    )
    stores = stores + stored([(second_ref, second_hbm), (column_ref, column_hbm)], 4)
    advance()
    for copy in stores:
        copy.wait()
    for s in order[:-1]:
        for k in range(1, columns):
            x_copy(s, k).wait()


def attend(x, gains, weight, placing, lengths, vectors, layer_in, gain, router_rows, slots, grad_rows, columns):
    quarters, tokens, part = x.shape
    experts = len(grad_rows)
    ext = grad_rows[0].shape[0]
    hc = weight.shape[1] // 4
    size = tokens // PIECES
    rows = router_rows.shape[0]
    dma = pltpu.SemaphoreType.DMA
    others = columns - 1
    kept = (
        jax.ShapeDtypeStruct(x.shape, bf16),
        jax.ShapeDtypeStruct((tokens, 3 * hc), bf16),
        jax.ShapeDtypeStruct((tokens, hc), bf16),
        jax.ShapeDtypeStruct((tokens, 128), f32),
        jax.ShapeDtypeStruct((tokens, part), f32),
        jax.ShapeDtypeStruct((tokens, 128), f32),
    )
    return pl.pallas_call(
        functools.partial(attend_kernel, columns, experts),
        out_shape=kept
        + (
            jax.ShapeDtypeStruct((tokens, part), bf16),
            jax.ShapeDtypeStruct((rows, tokens), f32),
            jax.ShapeDtypeStruct((experts, ext, part), bf16),
            jax.ShapeDtypeStruct((experts, others, ext, part), bf16),
        ),
        in_specs=[hbm(), vmem(), hbm(), vmem(), pl.BlockSpec(memory_space=pltpu.SMEM)]
        + [vmem()] * 5
        + [hbm()] * experts,
        out_specs=(hbm(),) * 6 + (vmem(),) * 2 + (hbm(),) * 2,
        scratch_shapes=[pltpu.VMEM(each.shape, each.dtype) for each in kept]
        + [
            pltpu.VMEM((vectors.shape[0], TILE, TILE), f32),
            pltpu.VMEM((tokens, hc), bf16),
            pltpu.VMEM((PIECES, size, columns * part), bf16),
            pltpu.VMEM((PIECES, size, columns * part), bf16),
            pltpu.VMEM((PIECES, size, columns * part), f32),
            pltpu.VMEM((PIECES, others, size, part), bf16),
            pltpu.VMEM((PIECES, others, size, part), bf16),
            pltpu.VMEM((rows, tokens), f32),
            pltpu.VMEM((quarters - 1, rows, tokens), f32),
            dma((PIECES,)), dma((PIECES,)), dma((PIECES, others)), dma((PIECES, others)),
            dma((quarters - 1,)), dma((quarters - 1,)),
            dma((experts,)), dma((experts,)), dma((experts, others)), dma((experts, others)), dma((6,)),
            pltpu.VMEM(x.shape, bf16), pltpu.VMEM(weight.shape, bf16), dma((2,)),
        ],
        compiler_params=pltpu.CompilerParams(
            collective_id=1, has_side_effects=True, vmem_limit_bytes=52 * MIB
        ),
        cost_estimate=microseconds(45),
        name="attend",
    )(x, gains, weight, placing, lengths, vectors, layer_in, gain, router_rows, slots, *grad_rows)


def gather_kernel(columns, experts, *refs):
    layer_ref, gain_ref, shard_ref, place_row, route_ref, cotangent_ref = refs[:6]
    x_ref, gains_ref, weight_ref, slot_row_ref, slot_column_ref, crossed_ref = refs[6:12]
    slot_grads = refs[12 : 12 + experts]
    (
        x_send, x_recv, own_send, own_recv, pass_send, pass_recv, gain_send, gain_recv,
        swap_send, swap_recv, z_send, z_recv, y_send, y_recv, place, cross_send, cross_recv,
        stay, slots, slot_store,
    ) = refs[12 + experts :]
    ex, half = lax.axis_index("ex"), lax.axis_index("half")
    row, col = lax.axis_index("row"), lax.axis_index("col")
    mine = row * columns + col
    tokens, part = layer_ref.shape
    greet(
        grid_peers(columns)
        + [{"ex": (ex + s) % experts} for s in range(1, experts)]
        + [{"half": 1 - half}]
    )
    spread = Spread(
        x_ref, layer_ref, columns, x_send, x_recv, own_send, own_recv, pass_send, pass_recv, stay
    )
    member = 2 * ex + half
    swap = remote(
        shard_ref.at[1 - row], weight_ref.at[row, member], swap_send.at[0], swap_recv.at[0], {"row": 1 - row}
    )
    swap.start()
    arrived = remote(
        shard_ref.at[1 - row], weight_ref.at[1 - row, member], swap_send.at[0], swap_recv.at[0], {"row": 1 - row}
    )
    place_shard = pltpu.make_async_copy(shard_ref.at[row], weight_ref.at[row, member], place.at[0])
    place_shard.start()
    spread.start()

    def z_copy(s, a):
        block = weight_ref.at[a, member]
        return remote(block, block, z_send.at[s, a], z_recv.at[s, a], {"ex": (ex + s) % experts})

    def z_arrival(s, a):
        block = weight_ref.at[a, 2 * ((ex - s + experts) % experts) + half]
        return remote(block, block, z_send.at[s, a], z_recv.at[s, a], {"ex": (ex + s) % experts})

    def y_copy(s, a):
        block = weight_ref.at[a, 2 * ((ex - s + experts) % experts) + half]
        return remote(block, block, y_send.at[s, a], y_recv.at[s, a], {"half": 1 - half})

    def y_arrival(s, a):
        block = weight_ref.at[a, 2 * ((ex - s + experts) % experts) + 1 - half]
        return remote(block, block, y_send.at[s, a], y_recv.at[s, a], {"half": 1 - half})

    queue = [(s, a) for s in nearest_first(experts) for a in (row, 1 - row)]
    place_shard.wait()
    z_copy(*queue[0]).start()
    y_copy(0, row).start()
    arrived.wait_recv()
    z_copy(*queue[1]).start()
    y_copy(0, 1 - row).start()
    gains_ref[mine] = gain_ref[...]
    gain_copies = [
        remote(gain_ref, gains_ref.at[mine], gain_send.at[i], gain_recv.at[i], where)
        for i, where in enumerate(grid_peers(columns))
    ]
    for copy in gain_copies:
        copy.start()

    lane = lax.broadcasted_iota(jnp.int32, (tokens, 128), 1)
    placed_hits = (route_ref[:, :1] == lane) | (route_ref[:, 1:2] == lane)
    to_given = given_table(place_row, tokens)
    hits = dot_nn(to_given, jnp.where(placed_hits, 1.0, 0.0).astype(bf16))
    low_hits = hits.astype(bf16)
    first_at = lax.broadcasted_iota(jnp.int32, (tokens, tokens), 0)
    second_at = lax.broadcasted_iota(jnp.int32, (tokens, tokens), 1)
    up_to = jnp.where(second_at <= first_at, 1.0, 0.0).astype(bf16)
    slot_column_ref[...] = jnp.where(hits > 0.5, dot_nn(up_to, low_hits) - 1.0, -1.0)
    from_on = jnp.where(first_at <= second_at, 1.0, 0.0).astype(bf16)
    same = jnp.where(first_at == second_at, 1.0, 0.0).astype(bf16)
    rows = slot_row_ref.shape[0]
    row_counts = dot_tn(low_hits, from_on)[:rows]
    slot_row_ref[...] = jnp.where(dot_tn(low_hits, same)[:rows] > 0.5, row_counts - 1.0, -1.0)

    def cotangent_slots(s):
        e = (ex + s) % experts
        ext = slot_grads[s].shape[0]
        hit = slot_row_ref[pl.ds(e, 1), :] == lax.broadcasted_iota(jnp.int32, (ext, tokens), 0).astype(f32)
        slots[s] = dot_nn(jnp.where(hit, 1.0, 0.0).astype(bf16), cotangent_ref[...]).astype(bf16)
        pltpu.make_async_copy(slots.at[s], slot_grads[s], slot_store.at[s]).start()

    crossing = [
        remote(
            slots.at[0], crossed_ref.at[k - 1], cross_send.at[k - 1], cross_recv.at[k - 1],
            {"col": (col + k) % columns},
        )
        for k in range(1, columns)
    ]
    cotangent_slots(0)
    for copy in crossing:
        copy.start()
    made = 1
    for i, (s, a) in enumerate(queue):
        z_copy(s, a).wait_send()
        if i + 2 < len(queue):
            z_copy(*queue[i + 2]).start()
        z_arrival(s, a).wait_recv()
        y_copy(s, a).start()
        if i == 0:
            spread.hand_on()
        while made < experts * (i + 1) // len(queue):
            cotangent_slots(made)
            made += 1
    spread.finish()
    for copy in gain_copies + crossing:
        copy.wait()
    for s in range(experts):
        pltpu.make_async_copy(slots.at[s], slot_grads[s], slot_store.at[s]).wait()
    swap.wait_send()
    for s in range(experts):
        for a in range(2):
            y_arrival(s, a).wait_recv()
            y_copy(s, a).wait_send()


class Spread:
    def __init__(
        self, out, source, columns, x_send, x_recv, own_send, own_recv, pass_send, pass_recv, stay=None
    ):
        self.stay = stay
        row, col = lax.axis_index("row"), lax.axis_index("col")
        mine = row * columns + col
        size = source.shape[0] // PIECES
        self.out, self.source, self.mine = out, source, mine
        self.across, self.own, self.passed = [], [], []
        for i in range(PIECES):
            at = pl.ds(i * size, size)
            for k in range(1, columns):
                self.across.append(
                    remote(
                        source.at[at], out.at[mine, at], x_send.at[i, k - 1], x_recv.at[i, k - 1],
                        {"col": (col + k) % columns},
                    )
                )
                block = out.at[row * columns + (col - k + columns) % columns, at]
                self.passed.append(
                    remote(block, block, pass_send.at[i, k - 1], pass_recv.at[i, k - 1], {"row": 1 - row})
                )
            self.own.append(
                remote(source.at[at], out.at[mine, at], own_send.at[i], own_recv.at[i], {"row": 1 - row})
            )

    def start(self):
        for i in range(PIECES):
            self.start_piece(i)

    def start_piece(self, i):
        others = len(self.across) // PIECES
        for copy in self.across[i * others : (i + 1) * others] + [self.own[i]]:
            copy.start()
        size = self.source.shape[0] // PIECES
        at = pl.ds(i * size, size)
        if self.stay is None:
            self.out[self.mine, at] = self.source[at]
        else:
            pltpu.make_async_copy(self.source.at[at], self.out.at[self.mine, at], self.stay.at[i]).start()

    def hand_on(self):
        for across, passed in zip(self.across, self.passed):
            across.wait_recv()
            passed.start()

    def finish(self):
        if self.stay is not None:
            size = self.source.shape[0] // PIECES
            for i in range(PIECES):
                at = pl.ds(i * size, size)
                pltpu.make_async_copy(self.source.at[at], self.out.at[self.mine, at], self.stay.at[i]).wait()
        for copy in self.own + self.passed:
            copy.wait_recv()
        for copy in self.across + self.own + self.passed:
            copy.wait_send()


def spread_semaphores(columns):
    dma = pltpu.SemaphoreType.DMA
    return [dma((PIECES, columns - 1))] * 2 + [dma((PIECES,))] * 2 + [dma((PIECES, columns - 1))] * 2


def gather(layer_in, gains, shard, place_row, routes, cotangent, stat_rows, ext, experts, columns):
    tokens, part = layer_in.shape
    _, rows, width = shard.shape
    quarters = 2 * columns
    dma = pltpu.SemaphoreType.DMA
    return pl.pallas_call(
        functools.partial(gather_kernel, columns, experts),
        out_shape=(
            jax.ShapeDtypeStruct((quarters, tokens, part), bf16),
            jax.ShapeDtypeStruct((quarters,) + gains.shape, f32),
            jax.ShapeDtypeStruct((2, 2 * experts, rows, width), bf16),
            jax.ShapeDtypeStruct((stat_rows, tokens), f32),
            jax.ShapeDtypeStruct((tokens, 128), f32),
            jax.ShapeDtypeStruct((columns - 1, ext, part), bf16),
        )
        + (jax.ShapeDtypeStruct((ext, part), bf16),) * experts,
        in_specs=[vmem()] * 6,
        out_specs=(hbm(), vmem(), hbm(), vmem(), vmem()) + (hbm(),) * (1 + experts),
        scratch_shapes=spread_semaphores(columns)
        + [
            dma((quarters - 1,)), dma((quarters - 1,)), dma((1,)), dma((1,)),
            dma((experts, 2)), dma((experts, 2)), dma((experts, 2)), dma((experts, 2)), dma((1,)),
            dma((columns - 1,)), dma((columns - 1,)), dma((PIECES,)),
            pltpu.VMEM((experts, ext, part), bf16), dma((experts,)),
        ],
        compiler_params=pltpu.CompilerParams(
            collective_id=0, has_side_effects=True, vmem_limit_bytes=52 * MIB
        ),
        cost_estimate=microseconds(30),
        name="gather",
    )(layer_in, gains, shard, place_row, routes, cotangent)


def expert_kernel(
    columns, experts,
    *refs,
):
    mixed_ref, slot_ref, gate_ref, weight_hbm, own_grads, own_crossed, came, crossed = refs[:8]
    (
        home_ref, y_hbm, y_far, keep_up, keep_down, away_up, away_down,
        x, xs, grads, weight, da, db, scaled, core_out, core_in, keep, col_out, col_in,
        load, grad_load, grad_send, grad_recv, z_send, z_recv, own_send, own_recv, col_send, col_recv, pass_send, pass_recv,
        core_send, core_recv, back_send, back_recv, home_send, home_recv, y_send, y_recv, y_sem, store, far_send, far_recv,
        free, last_send, last_recv, on_send, on_recv, y_far_send, y_far_recv,
    ) = refs[8:]
    ex, half = lax.axis_index("ex"), lax.axis_index("half")
    row, col = lax.axis_index("row"), lax.axis_index("col")
    tokens, part = mixed_ref.shape
    ext = x.shape[2]
    cap = ext - EXTRA
    quarters = 2 * columns
    wide = columns * part
    mine = row * columns + col
    last = experts - 1
    greet(
        [{"ex": (ex + s) % experts} for s in range(1, experts)]
        + [{"col": (col + k) % columns} for k in range(1, columns)]
        + [{"row": 1 - row}]
    )

    own_dims = pl.ds(pl.multiple_of(row * wide, wide), wide)
    other_dims = pl.ds(pl.multiple_of((1 - row) * wide, wide), wide)
    loads = [pltpu.make_async_copy(weight_hbm.at[row], weight.at[:, :, own_dims], load.at[0])]
    handed = [
        remote(weight_hbm.at[1 - row], weight.at[:, :, own_dims], load.at[1], load.at[2], {"row": 1 - row})
    ]
    final_chunk = farthest_first(experts)[-1]
    for s in range(experts):
        for k in range(columns):
            if k and s == final_chunk:
                continue
            at = (s, k)
            place = row * columns + (col - k + columns) % columns
            if s == 0:
                block = own_crossed.at[k - 1] if k else own_grads
            else:
                block = crossed.at[s, k - 1] if k else came.at[s]
            loads.append(pltpu.make_async_copy(block, grads.at[place, s], grad_load.at[at]))
            handed.append(
                remote(block, grads.at[place, s], grad_send.at[at], grad_recv.at[at], {"row": 1 - row})
            )
    for copy in loads + handed:
        copy.start()

    def last_copy(k):
        return remote(
            came.at[final_chunk], grads.at[mine, final_chunk], last_send.at[k - 1], last_recv.at[k - 1],
            {"col": (col + k) % columns},
        )

    def last_on(k):
        block = grads.at[row * columns + (col - k + columns) % columns, final_chunk]
        return remote(block, block, on_send.at[k - 1], on_recv.at[k - 1], {"row": 1 - row})

    def z_copy(s):
        return remote(
            xs.at[s], x.at[mine, s], z_send.at[s], z_recv.at[s], {"ex": (ex + s) % experts}
        )

    def own_copy(s):
        block = x.at[mine, s]
        return remote(block, block, own_send.at[s], own_recv.at[s], {"row": 1 - row})

    def col_copy(s, k):
        block = x.at[mine, s]
        return remote(
            block, block, col_send.at[s, k - 1], col_recv.at[s, k - 1], {"col": (col + k) % columns}
        )

    def pass_copy(s, k):
        block = x.at[row * columns + (col - k + columns) % columns, s]
        return remote(
            block, block, pass_send.at[s, k - 1], pass_recv.at[s, k - 1], {"row": 1 - row}
        )

    def spread(s):
        own_copy(s).start()
        for k in range(1, columns):
            col_copy(s, k).start()

    def hand_on(s):
        for k in range(1, columns):
            col_copy(s, k).wait_recv()
            pass_copy(s, k).start()

    def slots_of(e):
        hit = slot_ref[pl.ds(e, 1), :] == lax.broadcasted_iota(jnp.int32, (cap, tokens), 0).astype(f32)
        values = dot_nn(jnp.where(hit, 1.0, 0.0).astype(bf16), mixed_ref[...]).astype(bf16)
        gate = jnp.sum(jnp.where(hit, gate_ref[pl.ds(e, 1), :], 0.0), axis=1, keepdims=True)
        return values, write_extra(gate, part).astype(bf16)

    def build(s):
        values, extra = slots_of((ex + s) % experts)
        xs[s, :cap] = values
        xs[s, cap:] = extra

    def nth(p):
        far = experts // 2
        return jnp.where(p == 1, far, jnp.where((p > 1) & (p <= far), p - 1, p))

    build(nth(1))
    z_copy(nth(1)).start()
    values, extra = slots_of(ex)
    x[mine, 0, :cap] = values
    x[mine, 0, cap:] = extra
    spread(0)
    for k in range(1, columns):
        last_copy(k).start()

    @pl.loop(2, experts)
    def _(p):
        build(nth(p))

    for copy in loads:
        copy.wait()
    for copy in handed:
        copy.wait()
    hand_on(0)
    z_copy(nth(1)).wait_send()
    z_copy(nth(2)).start()
    z_copy(nth(1)).wait_recv()
    spread(nth(1))

    def core_copy(s):
        return remote(core_out.at[s], core_in.at[s], core_send.at[s], core_recv.at[s], {"row": 1 - row})

    def back_copy(s, k):
        return remote(
            col_out.at[s, k - 1], col_in.at[s, k - 1], back_send.at[s, k - 1], back_recv.at[s, k - 1],
            {"col": (col + k) % columns},
        )

    def home_copy(s):
        return remote(
            xs.at[s], home_ref.at[s], home_send.at[s], home_recv.at[s], {"ex": (ex - s + experts) % experts}
        )

    def stores(ups, downs):
        parts = [(weight.at[:2], ups, 0), (weight.at[2], downs, 1)]
        return [
            (
                pltpu.make_async_copy(source.at[(slice(None),) * (2 - i) + (own_dims,)], out, store.at[i]),
                remote(
                    source.at[(slice(None),) * (2 - i) + (other_dims,)], out, far_send.at[i], far_recv.at[i],
                    {"row": 1 - row},
                ),
            )
            for source, out, i in parts
        ]

    def store_gradients(i):
        for mine_here, (ups, downs) in ((True, (keep_up, keep_down)), (False, (away_up, away_down))):

            @pl.when((row == half) == mine_here)
            def _():
                for copy in stores(ups, downs)[i]:
                    copy.start()

    def wait_gradients(i):
        for copy in stores(keep_up, keep_down)[i]:
            copy.wait()

    def y_share(s):
        return remote(core_out.at[s], core_in.at[s], y_send.at[s], y_recv.at[s], {"row": 1 - row})

    def y_copy(s):
        return pltpu.make_async_copy(core_in.at[s], y_hbm.at[:, s], y_sem.at[s])

    def after_core(s, slot):
        core_copy(s).wait_recv()
        keep[slot] = keep[slot] + core_in[s].astype(f32)
        for k in range(1, columns):
            to = (col + k) % columns
            col_out[s, k - 1] = keep[slot, to].astype(bf16)
            back_copy(s, k).start()

    def after_columns(s, slot):
        total = keep[slot, col]
        for k in range(1, columns):
            back_copy(s, k).wait_recv()
            total = total + col_in[s, k - 1].astype(f32)
        return total.astype(bf16)

    def send_home(s, slot):
        xs[s] = after_columns(s, slot)
        home_copy(s).start()

    @pl.loop(0, experts)
    def _(p):
        s = nth(p)
        slot = jnp.where(p == 0, 2, p % 2)

        @pl.when(p == 1)
        def _():
            for k in range(1, columns):
                last_copy(k).wait_recv()
                last_on(k).start()

        @pl.when(p == last)
        def _():
            for k in range(1, columns):
                last_on(k).wait_recv()

        grad = jnp.concatenate([grads[q, s] for q in range(quarters)], axis=1)
        d = dot_nt(grad, weight[2])
        own_copy(s).wait_recv()
        for k in range(1, columns):
            pass_copy(s, k).wait_recv()

        @pl.when(p > 1)
        def _():
            after_core(nth(p - 1), (p - 1) % 2)

        @pl.when(p > 2)
        def _():
            send_home(nth(p - 2), p % 2)

        rows = jnp.concatenate([x[q, s] for q in range(quarters)], axis=1)
        gate = read_extra(x[mine, s, cap:], ext)
        a = dot_nt(rows, weight[0])
        b = dot_nt(rows, weight[1])
        d = d * gate
        square = a * a
        t = jnp.tanh(a * (GELU_A + (GELU_A * GELU_B) * square))
        part_on = 0.5 + 0.5 * t
        smooth = a * part_on
        slope = part_on + (a * (0.5 - 0.5 * t * t)) * (GELU_A + (3 * GELU_A * GELU_B) * square)
        active = smooth * b
        da[s] = (d * b * slope).astype(bf16)
        db[s] = (d * smooth).astype(bf16)
        scaled[s] = (active * gate).astype(bf16)
        extra = write_extra(jnp.sum(d * active, axis=1, keepdims=True), part)

        @pl.when((p > 0) & (p + 2 < experts))
        def _():
            z_copy(nth(p + 2)).wait_recv()
            spread(nth(p + 2))

        @pl.when((p > 0) & (p + 1 < experts))
        def _():
            hand_on(nth(p + 1))

        @pl.when((p > 0) & (p + 3 < experts))
        def _():
            z_copy(nth(p + 2)).wait_send()
            z_copy(nth(p + 3)).start()

        for j in range(columns):
            dims = pl.ds(pl.multiple_of(((1 - row) * columns + j) * part, part), part)
            value = dot_nn(da[s], weight[0, :, dims]) + dot_nn(db[s], weight[1, :, dims])
            core_out[s, j] = value.astype(bf16)
            core_out[s, j, cap:] = extra.astype(bf16)
        core_copy(s).start()
        for j in range(columns):
            dims = pl.ds(pl.multiple_of((row * columns + j) * part, part), part)
            keep[slot, j] = dot_nn(da[s], weight[0, :, dims]) + dot_nn(db[s], weight[1, :, dims])
            keep[slot, j, cap:] = extra

        @pl.when(p == 0)
        def _():
            hand_on(nth(1))
            z_copy(nth(2)).wait_send()
            z_copy(nth(3)).start()
            z_copy(nth(2)).wait_recv()
            spread(nth(2))

    def flat(ref, *at):
        block = ref[at] if at else ref[...]
        return block.reshape(experts * ext, block.shape[-1])

    before, final = nth(last - 1), nth(last)
    z_copy(final).wait_send()
    after_core(final, last % 2)
    after_core(0, 2)
    pl.semaphore_signal(free, inc=1, device_id={"row": 1 - row}, device_id_type=MESH)
    send_home(before, (last - 1) % 2)

    pl.semaphore_wait(free, 1)

    @pl.loop(0, experts)
    def _(s):
        core_copy(s).wait_send()
        for j in range(columns):
            dims = pl.ds(pl.multiple_of(((1 - row) * columns + j) * part, part), part)
            core_out[s, j] = dot_nn(scaled[s], weight[2, :, dims]).astype(bf16)
        y_share(s).start()

    def y_far_copy(k):
        return remote(
            core_in.at[nth(1), (col + k) % columns], y_far.at[k - 1], y_far_send.at[k - 1], y_far_recv.at[k - 1],
            {"col": (col + k) % columns},
        )

    @pl.loop(0, experts)
    def _(p):
        s = nth((p + 1) % experts)
        y_share(s).wait_recv()
        for j in range(columns):
            dims = pl.ds(pl.multiple_of((row * columns + j) * part, part), part)
            value = dot_nn(scaled[s], weight[2, :, dims]) + core_in[s, j].astype(f32)
            core_in[s, j] = value.astype(bf16)
        y_copy(s).start()

        @pl.when(p == 0)
        def _():
            for k in range(1, columns):
                y_far_copy(k).start()

    send_home(final, last % 2)
    for g, hidden in enumerate((da, db)):
        low = flat(hidden)
        for q in range(quarters):
            weight[g, :, q * part : (q + 1) * part] = dot_tn(low, flat(x, q)).astype(bf16)
    store_gradients(0)
    low = flat(scaled)
    for q in range(quarters):
        weight[2, :, q * part : (q + 1) * part] = dot_tn(low, flat(grads, q)).astype(bf16)
    store_gradients(1)
    home_ref[0] = after_columns(0, 2)
    wait_gradients(0)
    wait_gradients(1)
    for k in range(1, columns):
        y_far_copy(k).wait()
        last_copy(k).wait_send()
        last_on(k).wait_send()

    @pl.loop(1, experts)
    def _(s):
        home_copy(s).wait_recv()
        home_copy(s).wait_send()

    @pl.loop(0, experts)
    def _(s):
        own_copy(s).wait_send()
        y_share(s).wait_send()
        y_copy(s).wait()
        for k in range(1, columns):
            col_copy(s, k).wait_send()
            pass_copy(s, k).wait_send()
            back_copy(s, k).wait_send()


def expert_block(mixed, slots, gates, weights, own_grads, own_crossed, came, crossed, columns):
    tokens, part = mixed.shape
    quarters = 2 * columns
    experts, ext, _ = came.shape
    _, _, ff, wide = weights.shape
    dma = pltpu.SemaphoreType.DMA
    others = columns - 1
    return pl.pallas_call(
        functools.partial(expert_kernel, columns, experts),
        out_shape=(
            jax.ShapeDtypeStruct((experts, ext, part), bf16),
            jax.ShapeDtypeStruct((columns, experts, ext, part), bf16),
            jax.ShapeDtypeStruct((others, ext, part), bf16),
        )
        + (jax.ShapeDtypeStruct((2, ff, wide), bf16), jax.ShapeDtypeStruct((ff, wide), bf16)) * 2,
        in_specs=[vmem()] * 3 + [hbm()] * 5,
        out_specs=(vmem(),) + (hbm(),) * 6,
        scratch_shapes=[
            pltpu.VMEM((quarters, experts, ext, part), bf16),
            pltpu.VMEM((experts, ext, part), bf16),
            pltpu.VMEM((quarters, experts, ext, part), bf16),
            pltpu.VMEM((3, ff, D), bf16),
            pltpu.VMEM((experts, ext, ff), bf16),
            pltpu.VMEM((experts, ext, ff), bf16),
            pltpu.VMEM((experts, ext, ff), bf16),
            pltpu.VMEM((experts, columns, ext, part), bf16),
            pltpu.VMEM((experts, columns, ext, part), bf16),
            pltpu.VMEM((3, columns, ext, part), f32),
            pltpu.VMEM((experts, others, ext, part), bf16),
            pltpu.VMEM((experts, others, ext, part), bf16),
            dma((3,)), dma((experts, columns)), dma((experts, columns)), dma((experts, columns)),
            dma((experts,)), dma((experts,)), dma((experts,)), dma((experts,)),
            dma((experts, others)), dma((experts, others)), dma((experts, others)), dma((experts, others)),
            dma((experts,)), dma((experts,)), dma((experts, others)), dma((experts, others)),
            dma((experts,)), dma((experts,)), dma((experts,)), dma((experts,)), dma((experts,)),
            dma((2,)), dma((2,)), dma((2,)), pltpu.SemaphoreType.REGULAR,
            dma((others,)), dma((others,)), dma((others,)), dma((others,)), dma((others,)), dma((others,)),
        ],
        compiler_params=pltpu.CompilerParams(
            collective_id=2, has_side_effects=True, vmem_limit_bytes=56 * MIB
        ),
        cost_estimate=microseconds(80),
        name="expert_block",
    )(mixed, slots, gates, weights, own_grads, own_crossed, came, crossed)


def settle_part(
    columns, experts,
    home_ref, slot_ref, column_ref, second_ref, mixed_ref, cotangent_ref, gain_ref, router_ref,
    branch_ref, two_ref, drouter_ref, dgain_ref,
    low, dmixed_ref, dlogit_ref, stat, stat_in, stat_send, stat_recv, *rest,
):
    *spread_sems, after_spread = rest
    ex = lax.axis_index("ex")
    tokens, part = second_ref.shape
    ext = home_ref.shape[1]
    cap = ext - EXTRA
    size = tokens // PIECES
    lane = lax.broadcasted_iota(jnp.int32, (size, 128), 1)
    extras = []
    for s in range(experts):
        values = read_extra(home_ref[s, cap:], ext)
        near = values.astype(bf16)
        left = (values - near.astype(f32)).astype(bf16)
        extras.append(
            jnp.concatenate([jnp.broadcast_to(near, (ext, 128)), jnp.broadcast_to(left, (ext, 128))], axis=1)
        )
    peers = grid_peers(columns)
    spread = Spread(branch_ref, low, columns, *spread_sems)

    def stat_copy(i, n):
        at = pl.ds(i * size, size)
        return remote(
            stat.at[:, at], stat_in.at[n, :, at], stat_send.at[i, n], stat_recv.at[i, n], peers[n]
        )

    def combine(i):
        at = slice(i * size, (i + 1) * size)
        dmixed = jnp.zeros((size, part), f32)
        gate_grads = jnp.zeros((size, 128), f32)
        for s in range(experts):
            e = (ex + s) % experts
            place = jnp.sum(jnp.where(lane == e, slot_ref[at, :], 0.0), axis=1, keepdims=True)
            hit = place == lax.broadcasted_iota(jnp.int32, (size, ext), 1).astype(f32)
            pick_rows = jnp.where(hit, 1.0, 0.0).astype(bf16)
            dmixed = dmixed + dot_nn(pick_rows, home_ref[s])
            found = dot_nn(pick_rows, extras[s])
            gate_grads = jnp.where(lane == e, found[:, :128] + found[:, 128:], gate_grads)
        gates = jnp.where(lane < experts, column_ref[at, :], 0.0)
        dlogits = gate_grads - gates * jnp.sum(gate_grads, axis=1, keepdims=True)
        dlogit_ref[at, :] = dlogits
        dmixed = dmixed + dot_exact(dlogits[:, : router_ref.shape[0]], router_ref[...], ((1,), (0,)))
        dmixed_ref[at, :] = dmixed
        stat[:, at] = dot_exact(
            jnp.ones((8, part), f32), second_ref[at, :] * dmixed * gain_ref[...], ((1,), (1,))
        )
        for n in range(len(peers)):
            stat_copy(i, n).start()

    first_row = jnp.where(lax.broadcasted_iota(jnp.int32, (8, 128), 0) == 0, 1.0, 0.0)

    def close(i):
        at = slice(i * size, (i + 1) * size)
        total = stat[:, at]
        for n in range(len(peers)):
            stat_copy(i, n).wait_recv()
            total = total + stat_in[n, :, at]
        row_total = dot_exact(total, first_row, ((0,), (0,)))[:, :1]
        inverse = column_ref[at, experts : experts + 1]
        two = cotangent_ref[at, :].astype(f32) + inverse * (
            dmixed_ref[at, :] * gain_ref[...] - second_ref[at, :] * (inverse * inverse * row_total / D)
        )
        two_ref[at, :] = two
        low[at, :] = two.astype(bf16)
        spread.start_piece(i)

    for i in range(PIECES):
        combine(i)
        if i > 0:
            close(i - 1)
    close(PIECES - 1)
    after_spread()
    rows = drouter_ref.shape[0]
    drouter_ref[...] = dot_exact(dlogit_ref[...], mixed_ref[...].astype(f32), ((0,), (0,)))[:rows]
    normed = second_ref[...] * column_ref[:, experts : experts + 1]
    dgain_ref[...] = jnp.broadcast_to(
        jnp.sum(dmixed_ref[...] * normed, axis=0, keepdims=True), dgain_ref.shape
    )
    spread.hand_on()
    spread.finish()
    for i in range(PIECES):
        for n in range(len(peers)):
            stat_copy(i, n).wait_send()


def finish_part(
    columns, experts,
    dfirst_ref, dweight_ref, small, layer_ref, two_ref, gain_ref, inverse_ref,
    input_grad_ref, qkv_grad_ref, proj_grad_ref, sums_ref,
    core_in, keep, col_out, col_in, stat, stat_in, y_in, z_out, z_in, held, row_out, row_in, small_in,
    core_send, core_recv, col_send, col_recv, stat_send, stat_recv,
    y_send, y_recv, z_send, z_recv, row_send, row_recv, small_send, small_recv, others, while_waiting,
):
    ex, half = lax.axis_index("ex"), lax.axis_index("half")
    row, col = lax.axis_index("row"), lax.axis_index("col")
    tokens, part = layer_ref.shape
    size = tokens // PIECES
    members = 2 * experts
    rows = held.shape[1]
    hc = held.shape[2] // 4

    def core_copy(i):
        at = pl.ds(i * size, size)
        return remote(
            dfirst_ref.at[pl.ds((1 - row) * columns, columns), at], core_in.at[:, at],
            core_send.at[i], core_recv.at[i], {"row": 1 - row},
        )

    def block_of(member, a):
        return pl.ds(pl.multiple_of((a * members + member) * rows, rows), rows)

    def y_copy(s, a):
        to = 2 * ((ex + s) % experts) + 1 - half
        return remote(
            dweight_ref.at[block_of(to, a)], y_in.at[s, a], y_send.at[s, a], y_recv.at[s, a], {"half": 1 - half}
        )

    def z_copy(s, a):
        return remote(
            z_out.at[s, a], z_in.at[s, a], z_send.at[s, a], z_recv.at[s, a], {"ex": (ex + s) % experts}
        )

    queue = [(s, a) for s in nearest_first(experts)[::-1] + [0] for a in range(2)]
    crossing = []
    cell = {}

    def start():
        for i in range(PIECES):
            core_copy(i).start()

    def cross():
        for i in range(PIECES):
            at = slice(i * size, (i + 1) * size)
            core_copy(i).wait_recv()
            for j in range(columns):
                keep[j, at] = dfirst_ref[row * columns + j, at].astype(f32) + core_in[j, at].astype(f32)
            for k in range(1, columns):
                to = (col + k) % columns
                col_out[k - 1, at] = keep[to, at].astype(bf16)
                copy = remote(
                    col_out.at[k - 1, pl.ds(i * size, size)], col_in.at[k - 1, pl.ds(i * size, size)],
                    col_send.at[i, k - 1], col_recv.at[i, k - 1], {"col": to},
                )
                copy.start()
                crossing.append(copy)

    def normed():
        return layer_ref[...].astype(f32) * inverse_ref[:, 127:128]

    peers = grid_peers(columns)

    def stat_copy(n):
        return remote(stat, stat_in.at[n], stat_send.at[n], stat_recv.at[n], peers[n])

    def arrive():
        for copy in crossing:
            copy.wait_recv()
        dnorm = keep[col]
        for k in range(1, columns):
            dnorm = dnorm + col_in[k - 1].astype(f32)
        keep[col] = dnorm
        stat[...] = dot_exact(
            jnp.ones((8, part), f32), layer_ref[...].astype(f32) * (dnorm * gain_ref[...]), ((1,), (1,))
        )
        for n in range(len(peers)):
            stat_copy(n).start()
        small[:8] = jnp.broadcast_to(jnp.sum(dnorm * normed(), axis=0, keepdims=True), (8, part))
        cell["smalls"] = [
            remote(small, small_in.at[i], small_send.at[i], small_recv.at[i], where)
            for i, where in enumerate(others)
        ]
        for copy in cell["smalls"]:
            copy.start()

    def close():
        total = stat[...]
        for n in range(len(peers)):
            stat_copy(n).wait_recv()
            total = total + stat_in[n]
        first_row = jnp.where(lax.broadcasted_iota(jnp.int32, (8, 128), 0) == 0, 1.0, 0.0)
        row_total = dot_exact(total, first_row, ((0,), (0,)))[:, :1]
        inverse = inverse_ref[:, 127:128]
        input_grad_ref[...] = (
            two_ref[...] + inverse * (keep[col] * gain_ref[...] - normed() * (inverse * row_total / D))
        ).astype(bf16)

    def rest():
        for at in queue[:2]:
            y_copy(*at).start()
        cross()
        for n, (s, a) in enumerate(queue):
            y_copy(s, a).wait_send()
            if n + 2 < len(queue):
                y_copy(*queue[n + 2]).start()
            y_copy(s, a).wait_recv()
            own = dweight_ref[block_of(2 * ((ex + s) % experts) + half, a), :]
            total = own.astype(f32) + y_in[s, a].astype(f32)
            if s > 0:
                z_out[s, a] = total.astype(bf16)
                z_copy(s, a).start()
            else:
                held[a] = total
            if n == len(queue) // 2:
                arrive()
            if n == len(queue) - 2:
                close()
        while_waiting()
        for s in nearest_first(experts)[::-1]:
            for a in range(2):
                z_copy(s, a).wait_recv()
                held[a] = held[a] + z_in[s, a].astype(f32)
        row_out[...] = held[1 - row].astype(bf16)
        swap = remote(row_out, row_in, row_send.at[0], row_recv.at[0], {"row": 1 - row})
        swap.start()
        sums = small[...]
        for i, copy in enumerate(cell["smalls"]):
            copy.wait_recv()
            sums = sums + small_in[i]
        sums_ref[...] = sums
        swap.wait_recv()
        for at_row, values in ((row, held[row]), (1 - row, row_in[...].astype(f32))):
            proj_grad_ref[at_row] = values[:, 3 * hc :]
            for k in range(3):
                qkv_grad_ref[:, k, at_row, :] = values[:, k * hc : (k + 1) * hc]
        swap.wait_send()
        for copy in cell["smalls"] + crossing:
            copy.wait_send()
        for n in range(len(peers)):
            stat_copy(n).wait_send()
        for i in range(PIECES):
            core_copy(i).wait_send()
        for s, a in queue:
            if s > 0:
                z_copy(s, a).wait_send()

    return start, rest


def tail_kernel(columns, experts, *refs):
    (
        home_ref, slot_ref, column_ref, second_ref, mixed_ref, cotangent_ref, gain_two, router_ref,
        qkv_ref, lse_ref, attended_ref, first_ref, weight_ref, place_row, length_ref, vector_ref,
        layer_ref, gain_one, y_hbm, y_far, away_up, away_down,
    ) = refs[:22]
    layer_out_ref, input_grad_ref, qkv_grad_ref, proj_grad_ref, sums_ref, came_up, came_down = refs[22:29]
    scratch = list(refs[29:])

    def take(count):
        taken = scratch[:count]
        del scratch[:count]
        return taken

    branch_ref, two_ref, drouter_ref, dgain_ref, dfirst_ref, dweight_ref, dvector_ref, small = take(8)
    y_own, y_in, y_home = take(3)
    y_load, y_send, y_recv, y_away, y_came, half_send, half_recv = take(7)
    y_far_in = take(1)[0]
    settle_scratch = take(7 + 6)
    attention_scratch = take(5)
    finish_scratch = take(13 + 14)
    ex, half, col = lax.axis_index("ex"), lax.axis_index("half"), lax.axis_index("col")
    members = [
        {"ex": (ex + s) % experts, "half": (half + h) % 2}
        for s in range(experts)
        for h in range(2)
        if s + h > 0
    ]
    greet(grid_peers(columns) + members)

    halves = [
        remote(source, out, half_send.at[i], half_recv.at[i], {"half": 1 - half})
        for i, (source, out) in enumerate(((away_up, came_up), (away_down, came_down)))
    ]
    for copy in halves:
        copy.start()

    far, *near = farthest_first(experts)
    y_stay = pltpu.make_async_copy(y_hbm.at[col], y_own, y_load.at[0])
    y_stay.start()
    y_far_load = pltpu.make_async_copy(y_far, y_far_in, y_load.at[1])
    y_far_load.start()

    def y_cross(s, k):
        to = (col + k) % columns
        return remote(
            y_hbm.at[to, s], y_in.at[s, k - 1], y_send.at[s, k - 1], y_recv.at[s, k - 1], {"col": to}
        )

    def y_copy(s):
        return remote(
            y_own.at[s], y_home.at[s], y_away.at[s], y_came.at[s], {"ex": (ex - s + experts) % experts}
        )

    def y_sum(s, others):
        total = y_own[s].astype(f32)
        for other in others:
            total = total + other.astype(f32)
        if s > 0:
            y_own[s] = total.astype(bf16)
            y_copy(s).start()
        else:
            y_home[0] = total.astype(bf16)

    def y_homeward(s):
        for k in range(1, columns):
            y_cross(s, k).wait_recv()
        y_sum(s, [y_in[s, k - 1] for k in range(1, columns)])

    def after_spread():
        for s in near + [0]:
            for k in range(1, columns):
                y_cross(s, k).start()

    y_stay.wait()
    y_far_load.wait()
    y_sum(far, [y_far_in[k - 1] for k in range(1, columns)])
    settle_part(
        columns, experts,
        home_ref, slot_ref, column_ref, second_ref, mixed_ref, cotangent_ref, gain_two, router_ref,
        branch_ref, two_ref, drouter_ref, dgain_ref, *settle_scratch, after_spread,
    )
    ways = near + [0]

    def between(a):
        last = second_ref.shape[0] // TILE - 1
        if a == last:
            while ways:
                y_homeward(ways.pop(0))
        elif a > 0 and len(ways) > 1:
            y_homeward(ways.pop(0))

    def while_waiting():
        for s in range(1, experts):
            y_copy(s).wait_recv()
        tokens = second_ref.shape[0]
        ext = y_own.shape[1]
        size = tokens // PIECES
        lane = lax.broadcasted_iota(jnp.int32, (size, 128), 1)
        for i in range(PIECES):
            at = slice(i * size, (i + 1) * size)
            total = second_ref[at, :]
            for s in range(experts):
                place = jnp.sum(jnp.where(lane == (ex + s) % experts, slot_ref[at, :], 0.0), axis=1, keepdims=True)
                hit = place == lax.broadcasted_iota(jnp.int32, (size, ext), 1).astype(f32)
                total = total + dot_nn(jnp.where(hit, 1.0, 0.0).astype(bf16), y_home[s])
            layer_out_ref[at, :] = total.astype(bf16)

    start, rest = finish_part(
        columns, experts,
        dfirst_ref, dweight_ref, small, layer_ref, two_ref, gain_one, lse_ref,
        input_grad_ref, qkv_grad_ref, proj_grad_ref, sums_ref, *finish_scratch, members, while_waiting,
    )
    attention_backward_kernel(
        branch_ref, qkv_ref, lse_ref, attended_ref, first_ref, weight_ref, place_row, length_ref, vector_ref,
        dfirst_ref, dweight_ref, dvector_ref, *attention_scratch, between, start,
    )
    part = second_ref.shape[1]
    stat_rows = drouter_ref.shape[0]
    small[8:16] = dgain_ref[...]
    small[16 : 16 + stat_rows] = drouter_ref[...]
    pieces = 2 * TILE // part
    for i in range(dvector_ref.shape[0]):
        for n in range(pieces):
            at = 16 + stat_rows + i * pieces + n
            small[at : at + 1] = dvector_ref[i : i + 1, n * part : (n + 1) * part]
    rest()
    for copy in halves:
        copy.wait()
    for s in near + [0]:
        for k in range(1, columns):
            y_cross(s, k).wait_send()
    for s in range(1, experts):
        y_copy(s).wait_send()


def tail(
    home, slots, table, second, mixed, cotangent, gain_two, router_rows,
    qkv, lse, attended, first, weight, placing, lengths, vectors, layer_in, gain_one, y, y_far, away_up, away_down,
    stat_rows, experts, columns,
):
    tokens, part = second.shape
    quarters, others = 2 * columns, columns - 1
    hc = weight.shape[1] // 4
    ext = home.shape[1]
    rows, width = D // (4 * experts), 4 * hc
    small = (16 + stat_rows + vectors.size // part, part)
    dma = pltpu.SemaphoreType.DMA
    members = 2 * experts
    return pl.pallas_call(
        functools.partial(tail_kernel, columns, experts),
        out_shape=(
            jax.ShapeDtypeStruct((tokens, part), bf16),
            jax.ShapeDtypeStruct((tokens, part), bf16),
            jax.ShapeDtypeStruct((rows, 3, 2, hc), f32),
            jax.ShapeDtypeStruct((2, rows, hc), f32),
            jax.ShapeDtypeStruct(small, f32),
            jax.ShapeDtypeStruct(away_up.shape, bf16),
            jax.ShapeDtypeStruct(away_down.shape, bf16),
        ),
        in_specs=[vmem()] * 14 + [pl.BlockSpec(memory_space=pltpu.SMEM)] + [vmem()] * 3 + [hbm()] * 4,
        out_specs=(vmem(),) * 5 + (hbm(),) * 2,
        scratch_shapes=[
            pltpu.VMEM((quarters, tokens, part), bf16),
            pltpu.VMEM((tokens, part), f32),
            pltpu.VMEM((stat_rows, part), f32),
            pltpu.VMEM((8, part), f32),
            pltpu.VMEM((quarters, tokens, part), bf16),
            pltpu.VMEM((D, width), bf16),
            pltpu.VMEM(vectors.shape, f32),
            pltpu.VMEM(small, f32),
            pltpu.VMEM((experts, ext, part), bf16),
            pltpu.VMEM((experts, others, ext, part), bf16),
            pltpu.VMEM((experts, ext, part), bf16),
            dma((2,)), dma((experts, others)), dma((experts, others)), dma((experts,)), dma((experts,)), dma((2,)), dma((2,)),
            pltpu.VMEM((others, ext, part), bf16),
            pltpu.VMEM((tokens, part), bf16),
            pltpu.VMEM((tokens, part), f32),
            pltpu.VMEM((tokens, 128), f32),
            pltpu.VMEM((8, tokens), f32),
            pltpu.VMEM((quarters - 1, 8, tokens), f32),
            dma((PIECES, quarters - 1)), dma((PIECES, quarters - 1)),
        ]
        + spread_semaphores(columns)
        + [
            pltpu.VMEM((vectors.shape[0], TILE, TILE), f32),
            pltpu.VMEM((vectors.shape[0], TILE, TILE), f32),
            pltpu.VMEM((tokens, hc), bf16),
            pltpu.VMEM((tokens, 3 * hc), bf16),
            pltpu.VMEM((tokens, 2 * hc), f32),
            pltpu.VMEM((columns, tokens, part), bf16),
            pltpu.VMEM((columns, tokens, part), f32),
            pltpu.VMEM((others, tokens, part), bf16),
            pltpu.VMEM((others, tokens, part), bf16),
            pltpu.VMEM((8, tokens), f32),
            pltpu.VMEM((quarters - 1, 8, tokens), f32),
            pltpu.VMEM((experts, 2, rows, width), bf16),
            pltpu.VMEM((experts, 2, rows, width), bf16),
            pltpu.VMEM((experts, 2, rows, width), bf16),
            pltpu.VMEM((2, rows, width), f32),
            pltpu.VMEM((rows, width), bf16),
            pltpu.VMEM((rows, width), bf16),
            pltpu.VMEM((members - 1,) + small, f32),
            dma((PIECES,)), dma((PIECES,)), dma((PIECES, others)), dma((PIECES, others)),
            dma((quarters - 1,)), dma((quarters - 1,)),
            dma((experts, 2)), dma((experts, 2)), dma((experts, 2)), dma((experts, 2)),
            dma((1,)), dma((1,)), dma((members - 1,)), dma((members - 1,)),
        ],
        compiler_params=pltpu.CompilerParams(
            collective_id=3, has_side_effects=True, vmem_limit_bytes=47 * MIB
        ),
        cost_estimate=microseconds(90),
        name="tail",
    )(
        home, slots, table, second, mixed, cotangent, gain_two, router_rows,
        qkv, lse, attended, first, weight, placing, lengths, vectors, layer_in, gain_one, y, y_far, away_up, away_down,
    )


def adamw_step(weight, grad, first, second, rate):
    first_new = beta_first * first + (1.0 - beta_first) * grad
    second_new = beta_second * second + (1.0 - beta_second) * grad * grad
    moment = first_new / (1.0 - beta_first**STEP)
    spread = second_new / (1.0 - beta_second**STEP)
    weight_new = weight - rate * (
        moment / (jnp.sqrt(spread) + adam_epsilon) + weight_decay * weight
    )
    return (weight_new, first_new, second_new)


def local(
    layer_in, lengths, placing, routes, cotangent,
    norm_gains, gain_first, gain_second, rel_bias, bias_first, bias_second,
    router, router_first, router_second, qkv_weight, qkv_first, qkv_second,
    proj_weight, proj_first, proj_second, expert_up, up_first, up_second,
    expert_down, down_first, down_second,
):
    tokens, part = layer_in.shape
    experts, columns = lax.axis_size("ex"), lax.axis_size("col")
    quarters = 2 * columns
    cap = min(tokens, 5 * TOP * tokens // (4 * experts))
    ext = cap + EXTRA
    hc = qkv_weight.shape[5]
    head_count = hc // HD
    wide = D // 2

    qkv_low = jnp.moveaxis(qkv_weight[0, 0].astype(bf16), 1, 0).reshape(2, -1, 3 * hc)
    proj_low = jnp.swapaxes(proj_weight[:, :, 0, 0].astype(bf16), 1, 2)
    shard = jnp.concatenate([qkv_low, proj_low], axis=2)
    gains_eight = jnp.pad(norm_gains, ((0, 6), (0, 0)))
    stat_rows = (experts + 8) // 8 * 8
    x_all, gains_all, weight, slot_rows, slot_columns, own_crossed, *grad_rows = gather(
        layer_in, gains_eight, shard, placing, routes, cotangent, stat_rows, ext, experts, columns
    )
    weight = weight.reshape(D, 4 * hc)
    ff = expert_down.shape[1]
    weights = jnp.concatenate(
        [jnp.transpose(expert_up[0], (1, 2, 0)).reshape(2 * ff, wide).astype(bf16), expert_down[0].astype(bf16)]
    )

    x_all, weights = lax.optimization_barrier((x_all, weights))
    weights = lax.all_gather(weights, "half", axis=0, tiled=True).reshape(2, 3, ff, wide)
    vectors = bias_vectors(rel_bias, tokens)
    router_rows = jnp.pad(router.T, ((0, stat_rows - experts), (0, 0)))
    first, qkv, attended, lse, second, table, mixed, gates, came, crossed = attend(
        x_all, gains_all, weight, placing, lengths, vectors, layer_in, norm_gains[1:], router_rows, slot_rows,
        grad_rows, columns,
    )
    home, y, y_far, keep_up, keep_down, away_up, away_down = expert_block(
        mixed, slot_rows, gates, weights, grad_rows[0], own_crossed, came, crossed, columns
    )
    layer_out, input_grad, grad_qkv, grad_proj, sums, came_up, came_down = tail(
        home, slot_columns, table, second, mixed, cotangent, norm_gains[1:],
        router_rows, qkv, lse, attended, first, weight, placing, lengths, vectors, layer_in, norm_gains[:1], y, y_far, away_up, away_down,
        stat_rows, experts, columns,
    )
    grad_gains = jnp.stack([sums[0], sums[8]])
    grad_router = sums[16 : 16 + experts].T
    grad_bias = bias_gradient(sums[16 + stat_rows :].reshape(vectors.shape), head_count, tokens)
    grad_qkv = jnp.swapaxes(grad_qkv, 1, 2).reshape(qkv_weight.shape)
    grad_proj = jnp.swapaxes(grad_proj, 1, 2).reshape(proj_weight.shape)
    grad_up = jnp.transpose(keep_up.astype(f32) + came_up.astype(f32), (2, 0, 1))[None]
    grad_down = (keep_down.astype(f32) + came_down.astype(f32))[None]
    ups = adamw_step(expert_up, grad_up, up_first, up_second, 2.0 * D ** (-0.5))
    downs = adamw_step(expert_down, grad_down, down_first, down_second, 2.0 * (FF / 2) ** (-0.5))
    gains = adamw_step(norm_gains, grad_gains, gain_first, gain_second, 0.5)
    bias = adamw_step(rel_bias, grad_bias, bias_first, bias_second, 1.0)
    routers = adamw_step(router, grad_router, router_first, router_second, 2.0 * (2 * D) ** (-0.5))
    qkvs = adamw_step(qkv_weight, grad_qkv, qkv_first, qkv_second, 2.0 * D ** (-0.5))
    projs = adamw_step(proj_weight, grad_proj, proj_first, proj_second, 2.0 * (HEADS * HD / 8) ** (-0.5))
    out = (layer_out, input_grad) + gains + bias + routers
    for group in (qkvs, projs, ups, downs):
        out = out + group + (group[0].astype(bf16),)
    return out


def solution(mesh):
    shape = mesh.devices.shape
    fine = Mesh(
        mesh.devices.reshape((shape[0] // 2, 2) + shape[1:]), ("ex", "half", "row", "col")
    )
    dp, grid = ("ex", "half"), ("row", "col")
    tokens, own = P(dp, grid), P(dp, None)
    gain, router = P(None, grid), P(grid, None)
    qkv, proj = P("row", dp, None, None, None, "col"), P(None, "col", "row", dp, None)
    up, down = P(dp, "row", None, "col"), P(dp, "col", "row")
    in_specs = (
        (tokens, own, own, own, tokens) + (gain,) * 6 + (router,) * 3
        + (qkv,) * 3 + (proj,) * 3 + (up,) * 3 + (down,) * 3
    )
    out_specs = (
        (tokens, tokens) + (gain,) * 6 + (router,) * 3
        + (qkv,) * 4 + (proj,) * 4 + (up,) * 4 + (down,) * 4
    )
    return jax.shard_map(local, mesh=fine, in_specs=in_specs, out_specs=out_specs, check_vma=False)
```

```python
import functools

import jax
import jax.numpy as jnp
import numpy as np
from jax import lax
from jax.experimental import pallas as pl
from jax.experimental.pallas import tpu as pltpu
from jax.sharding import Mesh, PartitionSpec as P

D = 1024
HEADS = 16
FF = 2816
TOP = 2
STEP = 5
beta_first = 0.5
beta_second = 0.5
adam_epsilon = 1e-08
weight_decay = 0.01
highest = lax.Precision.HIGHEST
EXTRA = 16
HD = 64
BUCKETS = 32
LONGEST = 512
TILE = 256
norm_epsilon = 1e-06
hidden_score = -1e30
bucket_edges = np.floor(16.0 * 2.0 ** (np.arange(16) * 0.375)).astype(np.int32)
f32 = jnp.float32
bf16 = jnp.bfloat16
MIB = 1 << 20


def dot_nn(a, b):
    return lax.dot_general(a, b, (((1,), (0,)), ((), ())), preferred_element_type=f32)


def dot_nt(a, b):
    return lax.dot_general(a, b, (((1,), (1,)), ((), ())), preferred_element_type=f32)


def dot_tn(a, b):
    return lax.dot_general(a, b, (((0,), (0,)), ((), ())), preferred_element_type=f32)


def tile_reach(tokens):
    return min(tokens // TILE, (LONGEST - 1 + TILE - 1) // TILE + 1)


def toeplitz_places(tokens):
    reach = tile_reach(tokens)
    m = np.arange(2 * TILE)
    base = np.where(m < TILE, -m, 2 * TILE - m)
    distance = np.arange(reach)[:, None] * TILE + base[None, :]
    clipped = np.maximum(distance, 0)
    buckets = np.where(
        clipped < 16, clipped, 15 + (clipped[..., None] >= bucket_edges).sum(-1)
    )
    return (distance, buckets)


def bias_vectors(rel_bias, tokens):
    distance, buckets = toeplitz_places(tokens)
    table = jnp.asarray((buckets[..., None] == np.arange(BUCKETS)).astype(np.float32))
    values = jnp.einsum("dmb,bh->hdm", table, rel_bias, precision=lax.Precision.HIGHEST)
    values = jnp.where(jnp.asarray(distance < 0)[None], hidden_score, values)
    return values.reshape(-1, 2 * TILE)


def bias_gradient(vectors, head_count, tokens):
    distance, buckets = toeplitz_places(tokens)
    table = ((buckets[..., None] == np.arange(BUCKETS)) & (distance >= 0)[..., None]).astype(np.float32)
    return jnp.einsum(
        "dmb,hdm->bh",
        jnp.asarray(table),
        vectors.reshape(head_count, distance.shape[0], 2 * TILE),
        precision=lax.Precision.HIGHEST,
    )


def fill_bias(vector_ref, bias):
    for i in range(bias.shape[0]):
        wide = jnp.broadcast_to(vector_ref[i : i + 1, :], (TILE, 2 * TILE))
        bias[i] = pltpu.roll(wide, 0, 1, stride=1, stride_axis=0)[:, :TILE]


def head_lanes(shape, head):
    return lax.broadcasted_iota(jnp.int32, shape, 1) // HD == head


def given_table(place_row, tokens):
    return jnp.where(
        place_row[...] == lax.broadcasted_iota(jnp.int32, (tokens, tokens), 0), 1.0, 0.0
    ).astype(bf16)


def sequence_starts(length_ref, tokens):
    at = lax.broadcasted_iota(jnp.int32, (tokens, 1), 0)
    starts = jnp.zeros((tokens, 1), jnp.int32)
    end = 0
    for k in range(length_ref.shape[1]):
        end = end + length_ref[0, k]
        starts = jnp.where(at >= end, end, starts)
    return starts


def attention_forward_kernel(
    x_ref, gain_ref, weight_ref, length_ref, vector_ref,
    first_ref, qkv_ref, attended_ref, lse_ref, bias, between,
):
    quarters, tokens, part = x_ref.shape
    width = quarters * part
    hc = weight_ref.shape[1] // 4
    head_count = hc // HD
    reach = bias.shape[0] // head_count
    fill_bias(vector_ref, bias)
    squares = jnp.zeros((tokens, 1), f32)
    for q in range(quarters):
        v = x_ref[q].astype(f32)
        squares = squares + jnp.sum(v * v, axis=1, keepdims=True)
    inverse = lax.rsqrt(squares / width + norm_epsilon)
    total = jnp.zeros((tokens, 3 * hc), f32)
    for q in range(quarters):
        first = (x_ref[q].astype(f32) * inverse * gain_ref[q, :1]).astype(bf16)
        first_ref[q] = first
        total = total + dot_nn(first, weight_ref[q * part : (q + 1) * part, : 3 * hc])
    all_starts = sequence_starts(length_ref, tokens)
    scale = jnp.where(
        lax.broadcasted_iota(jnp.int32, (1, 3 * hc), 1) < hc, HD ** (-0.5), 1.0
    )
    qkv_ref[...] = (total * scale).astype(bf16)
    between(-1)
    for a in range(tokens // TILE):
        rows = slice(a * TILE, (a + 1) * TILE)
        blocks = range(max(0, a - reach + 1), a + 1)
        starts = all_starts[rows, :]
        visible = [
            b * TILE + lax.broadcasted_iota(jnp.int32, (TILE, TILE), 1) >= starts for b in blocks
        ]

        def one_head(head, carry):
            out, lse = carry
            mine = head_lanes((TILE, hc), head)
            query = jnp.where(mine, qkv_ref[rows, :hc], 0)
            scores = []
            for b, seen in zip(blocks, visible):
                s = dot_nt(query, qkv_ref[b * TILE : (b + 1) * TILE, hc : 2 * hc])
                scores.append(jnp.where(seen, s + bias[head * reach + a - b], hidden_score))
            top = functools.reduce(jnp.maximum, [jnp.max(s, axis=1, keepdims=True) for s in scores])
            exps = [jnp.exp(s - top) for s in scores]
            denominator = functools.reduce(jnp.add, [jnp.sum(e, axis=1, keepdims=True) for e in exps])
            share = 1.0 / denominator
            value = jnp.zeros((TILE, hc), f32)
            for b, e in zip(blocks, exps):
                value = value + dot_nn(
                    (e * share).astype(bf16), qkv_ref[b * TILE : (b + 1) * TILE, 2 * hc :]
                )
            lane = lax.broadcasted_iota(jnp.int32, (TILE, 128), 1)
            return (
                jnp.where(mine, value, out),
                jnp.where(lane == head, top + jnp.log(denominator), lse),
            )

        out, lse = lax.fori_loop(
            0, head_count, one_head, (jnp.zeros((TILE, hc), f32), jnp.zeros((TILE, 128), f32))
        )
        attended_ref[rows, :] = out.astype(bf16)
        lane = lax.broadcasted_iota(jnp.int32, (TILE, 128), 1)
        lse_ref[rows, :] = jnp.where(lane == 127, inverse[rows], lse)
        between(a)


def microseconds(time):
    return pl.CostEstimate(flops=0, bytes_accessed=int(time * 3.5e6), transcendentals=0)


def vmem():
    return pl.BlockSpec(memory_space=pltpu.VMEM)


def hbm():
    return pl.BlockSpec(memory_space=pltpu.HBM)


def attention_backward_kernel(
    branch_ref, qkv_ref, lse_ref, attended_ref, first_ref, weight_ref, length_ref, vector_ref,
    dfirst_ref, dweight_ref, dvector_ref,
    bias, dbias, grad_ref, dqkv, dkv, before, after,
):
    quarters, tokens, part = branch_ref.shape
    hc = weight_ref.shape[1] // 4
    head_count = hc // HD
    reach = bias.shape[0] // head_count
    fill_bias(vector_ref, bias)
    dbias[...] = jnp.zeros_like(dbias)
    dkv[...] = jnp.zeros_like(dkv)
    all_starts = sequence_starts(length_ref, tokens)
    for a in reversed(range(tokens // TILE)):
        rows = slice(a * TILE, (a + 1) * TILE)
        blocks = range(max(0, a - reach + 1), a + 1)
        starts = all_starts[rows, :]
        visible = [
            b * TILE + lax.broadcasted_iota(jnp.int32, (TILE, TILE), 1) >= starts for b in blocks
        ]
        before(a)
        total = jnp.zeros((TILE, hc), f32)
        for q in range(quarters):
            total = total + dot_nn(branch_ref[q, rows], weight_ref[q * part : (q + 1) * part, 3 * hc :])
        grad_ref[rows, :] = total.astype(bf16)

        def one_head(head, dquery):
            mine = head_lanes((TILE, hc), head)
            query = jnp.where(mine, qkv_ref[rows, :hc], 0)
            grad = jnp.where(mine, grad_ref[rows, :], 0)
            lane = lax.broadcasted_iota(jnp.int32, (TILE, 128), 1)
            lse = jnp.sum(jnp.where(lane == head, lse_ref[rows, :], 0.0), axis=1, keepdims=True)
            probs, dprobs = [], []
            inner = jnp.zeros((TILE, 1), f32)
            for b, seen in zip(blocks, visible):
                keys = slice(b * TILE, (b + 1) * TILE)
                s = dot_nt(query, qkv_ref[keys, hc : 2 * hc]) + bias[head * reach + a - b]
                p = jnp.where(seen, jnp.exp(s - lse), 0.0)
                d = dot_nt(grad, qkv_ref[keys, 2 * hc :])
                inner = inner + jnp.sum(p * d, axis=1, keepdims=True)
                probs.append(p)
                dprobs.append(d)
            for b, p, d in zip(blocks, probs, dprobs):
                keys = slice(b * TILE, (b + 1) * TILE)
                ds = p * (d - inner)
                place = head * reach + a - b
                dbias[place] = dbias[place] + ds
                low = ds.astype(bf16)
                dquery = dquery + dot_nn(low, jnp.where(mine, qkv_ref[keys, hc : 2 * hc], 0))
                dkv[keys, :hc] = dkv[keys, :hc] + dot_tn(low, query)
                dkv[keys, hc:] = dkv[keys, hc:] + dot_tn(p.astype(bf16), grad)
            return dquery

        dquery = lax.fori_loop(0, head_count, one_head, jnp.zeros((TILE, hc), f32))
        dqkv[rows, :hc] = (dquery * HD ** (-0.5)).astype(bf16)
        dqkv[rows, hc:] = dkv[rows, :].astype(bf16)
        for q in range(quarters):
            dfirst_ref[q, rows] = dot_nt(
                dqkv[rows, :], weight_ref[q * part : (q + 1) * part, : 3 * hc]
            ).astype(bf16)
        after(a)
    for q in range(quarters):
        dims = slice(q * part, (q + 1) * part)
        dweight_ref[dims, : 3 * hc] = dot_tn(first_ref[q], dqkv[...]).astype(bf16)
        dweight_ref[dims, 3 * hc :] = dot_tn(branch_ref[q], attended_ref[...]).astype(bf16)


def bias_sums(dbias, dvector_ref):
    for i in range(dbias.shape[0]):
        wide = jnp.concatenate([dbias[i], jnp.zeros((TILE, TILE), f32)], axis=1)
        level = wide[:8]
        for g in range(8, TILE, 8):
            level = level + pltpu.roll(wide[g : g + 8], 2 * TILE - g, 1)
        row = level[:1]
        for s in range(1, 8):
            row = row + pltpu.roll(level[s : s + 1], 2 * TILE - s, 1)
        dvector_ref[i : i + 1, :] = row


def half_places(rows, part):
    row = lax.broadcasted_iota(jnp.int32, (rows, EXTRA), 0) // part
    high = lax.broadcasted_iota(jnp.int32, (rows, EXTRA), 1)
    column = lax.broadcasted_iota(jnp.int32, (rows, part), 0) % part
    return (row, high, column == lax.broadcasted_iota(jnp.int32, (rows, part), 1))


def write_extra(values, part):
    row, high, column = half_places(values.shape[0], part)
    near = values.astype(bf16)
    left = (values - near.astype(f32)).astype(bf16)
    near_rows = jnp.where(row == high, 1.0, 0.0).astype(bf16)
    left_rows = jnp.where(row + 8 == high, 1.0, 0.0).astype(bf16)
    near_values = jnp.where(column, near.astype(f32), 0.0).astype(bf16)
    left_values = jnp.where(column, left.astype(f32), 0.0).astype(bf16)
    return dot_tn(near_rows, near_values) + dot_tn(left_rows, left_values)


def read_extra(extra, rows):
    part = extra.shape[1]
    row, high, column = half_places(rows, part)
    pick = jnp.where(row == high % 8, 1.0, 0.0).astype(bf16)
    return jnp.sum(jnp.where(column, dot_nn(pick, extra), 0.0), axis=1, keepdims=True)


GELU_A = 0.7978845608028654
GELU_B = 0.044715


MESH = pl.DeviceIdType.MESH


def remote(src, dst, send, recv, where):
    return pltpu.make_async_remote_copy(
        src_ref=src, dst_ref=dst, send_sem=send, recv_sem=recv, device_id=where, device_id_type=MESH
    )


def greet(wheres):
    barrier = pltpu.get_barrier_semaphore()
    for where in wheres:
        pl.semaphore_signal(barrier, inc=1, device_id=where, device_id_type=MESH)
    pl.semaphore_wait(barrier, len(wheres))


def dot_exact(a, b, dims):
    return lax.dot_general(a, b, ((dims, ((), ()))), precision=highest, preferred_element_type=f32)


def grid_peers(columns):
    row, col = lax.axis_index("row"), lax.axis_index("col")
    return [
        {"row": (row + i) % 2, "col": (col + j) % columns}
        for i in range(2)
        for j in range(columns)
        if i + j > 0
    ]


def sum_of_peers(mine, got, send, recv, columns):
    copies = [
        remote(mine, got.at[i], send.at[i], recv.at[i], where)
        for i, where in enumerate(grid_peers(columns))
    ]
    for copy in copies:
        copy.start()
    for copy in copies:
        copy.wait_recv()
    total = mine[...]
    for i in range(len(copies)):
        total = total + got[i]
    for copy in copies:
        copy.wait_send()
    return total


PIECES = 4


def project_part(
    columns, experts,
    attended_ref, weight_ref, layer_ref, gain_ref, router_ref, slot_ref,
    second_ref, mixed_ref, gate_ref, column_ref,
    core_out, core_in, keep, col_out, col_in, stat, stat_in,
    core_send, core_recv, col_send, col_recv, stat_send, stat_recv,
):
    row, col = lax.axis_index("row"), lax.axis_index("col")
    tokens, part = layer_ref.shape
    wide = columns * part
    size = tokens // PIECES
    heads = slice(3 * weight_ref.shape[1] // 4, weight_ref.shape[1])
    own_rows = pl.ds(pl.multiple_of(row * wide, wide), wide)
    other_rows = pl.ds(pl.multiple_of((1 - row) * wide, wide), wide)
    own_columns = pl.ds(pl.multiple_of(col * part, part), part)

    def core_copy(i):
        return remote(core_out.at[i], core_in.at[i], core_send.at[i], core_recv.at[i], {"row": 1 - row})

    def col_copy(i, k):
        return remote(
            col_out.at[i, k - 1], col_in.at[i, k - 1], col_send.at[i, k - 1], col_recv.at[i, k - 1],
            {"col": (col + k) % columns},
        )

    def multiply(i):
        at = slice(i * size, (i + 1) * size)
        core_out[i] = dot_nt(attended_ref[at, :], weight_ref[other_rows, heads]).astype(bf16)
        core_copy(i).start()
        keep[i] = dot_nt(attended_ref[at, :], weight_ref[own_rows, heads])

    def cross(i):
        core_copy(i).wait_recv()
        keep[i] = keep[i] + core_in[i].astype(f32)
        for k in range(1, columns):
            to = (col + k) % columns
            col_out[i, k - 1] = keep[i, :, pl.ds(pl.multiple_of(to * part, part), part)].astype(bf16)
            col_copy(i, k).start()

    def rest():
        ones = jnp.where(lax.broadcasted_iota(jnp.int32, router_ref.shape, 0) == experts, 1.0, 0.0)
        scaled_router = router_ref[...] * gain_ref[1:2]
        for i in range(PIECES):
            at = slice(i * size, (i + 1) * size)
            total = layer_ref[at, :].astype(f32) + keep[i, :, own_columns]
            for k in range(1, columns):
                col_copy(i, k).wait_recv()
                total = total + col_in[i, k - 1].astype(f32)
            second_ref[at, :] = total
            stat[:, at] = dot_exact(scaled_router, total, ((1,), (1,))) + dot_exact(
                ones, total * total, ((1,), (1,))
            )
        total = sum_of_peers(stat, stat_in, stat_send, stat_recv, columns)
        inverse = lax.rsqrt(total[experts : experts + 1] / D + norm_epsilon)
        routed = slot_ref[...] >= 0
        logits = jnp.where(routed, total * inverse, hidden_score)
        shares = jnp.where(routed, jnp.exp(logits - jnp.max(logits, axis=0, keepdims=True)), 0.0)
        gates = shares / jnp.sum(shares, axis=0, keepdims=True)
        gate_ref[...] = gates
        number = lax.broadcasted_iota(jnp.int32, gates.shape, 0)
        lanes = (gates.shape[0], 128)
        eye = jnp.where(
            lax.broadcasted_iota(jnp.int32, lanes, 0) == lax.broadcasted_iota(jnp.int32, lanes, 1), 1.0, 0.0
        )
        table = dot_exact(jnp.where(number == experts, inverse, gates), eye, ((0,), (0,)))
        column_ref[...] = table
        mixed_ref[...] = (second_ref[...] * table[:, experts : experts + 1] * gain_ref[1:2]).astype(bf16)
        for i in range(PIECES):
            core_copy(i).wait_send()
            for k in range(1, columns):
                col_copy(i, k).wait_send()

    return multiply, cross, rest


def nearest_first(experts):
    return sorted(range(1, experts), key=lambda s: min(s, experts - s))


def farthest_first(experts):
    far = experts // 2
    return [far] + [s for s in range(1, experts) if s != far]


def attend_kernel(columns, experts, *refs):
    x_hbm, gains_ref, weight_hbm, length_ref, vector_ref, layer_ref, gain_ref, router_ref, slot_ref, shares = refs[:10]
    grad_rows = refs[10 : 10 + experts]
    (
        first_hbm, qkv_hbm, attended_hbm, lse_hbm, second_hbm, column_hbm, mixed_ref, gate_ref, came, crossed, share_out,
        first_ref, qkv_ref, attended_ref, lse_ref, second_ref, column_ref,
        bias, core_out, core_in, keep, col_out, col_in, stat, stat_in,
        core_send, core_recv, col_send, col_recv, stat_send, stat_recv,
        z_send, z_recv, x_send, x_recv, store, x_ref, weight_ref, load, share_send, share_recv,
    ) = refs[10 + experts :]
    loads = [
        pltpu.make_async_copy(x_hbm, x_ref, load.at[0]),
        pltpu.make_async_copy(weight_hbm, weight_ref, load.at[1]),
    ]
    for copy in loads:
        copy.start()
    ex, col = lax.axis_index("ex"), lax.axis_index("col")
    greet(
        grid_peers(columns)
        + [{"ex": (ex + s) % experts} for s in range(1, experts)]
        + [{"half": 1 - lax.axis_index("half")}]
    )
    share = remote(
        shares, share_out, share_send.at[0], share_recv.at[0], {"half": 1 - lax.axis_index("half")}
    )
    share.start()

    def z_copy(s):
        return remote(grad_rows[s], came.at[s], z_send.at[s], z_recv.at[s], {"ex": (ex + s) % experts})

    def x_copy(s, k):
        return remote(
            came.at[s], crossed.at[s, k - 1], x_send.at[s, k - 1], x_recv.at[s, k - 1], {"col": (col + k) % columns}
        )

    far, *near = farthest_first(experts)
    for s in near + [far]:
        z_copy(s).start()
    for copy in loads:
        copy.wait()

    def go_on(s):
        z_copy(s).wait_recv()
        for k in range(1, columns):
            x_copy(s, k).start()

    multiply, cross, rest = project_part(
        columns, experts,
        attended_ref, weight_ref, layer_ref, gain_ref, router_ref, slot_ref,
        second_ref, mixed_ref, gate_ref, column_ref,
        core_out, core_in, keep, col_out, col_in, stat, stat_in,
        core_send, core_recv, col_send, col_recv, stat_send, stat_recv,
    )

    def between(a):
        if a >= 0:
            multiply(a)
        if a > 0:
            cross(a - 1)
        if a == 2:
            for s in near[:-1]:
                go_on(s)

    attention_forward_kernel(
        x_ref, gains_ref, weight_ref, length_ref, vector_ref,
        first_ref, qkv_ref, attended_ref, lse_ref, bias, between,
    )
    cross(PIECES - 1)

    def stored(pairs, first):
        copies = [pltpu.make_async_copy(a, b, store.at[first + i]) for i, (a, b) in enumerate(pairs)]
        for copy in copies:
            copy.start()
        return copies

    stores = stored(
        [(first_ref, first_hbm), (qkv_ref, qkv_hbm), (attended_ref, attended_hbm), (lse_ref, lse_hbm)], 0
    )

    go_on(far)
    rest()
    stores = stores + stored([(second_ref, second_hbm), (column_ref, column_hbm)], 4)
    z_copy(near[-1]).wait_recv()
    for copy in stores:
        copy.wait()
    share.wait()
    for s in [far] + near[:-1]:
        for k in range(1, columns):
            x_copy(s, k).wait()
    for s in near + [far]:
        z_copy(s).wait_send()


def attend(x, gains, weight, lengths, vectors, layer_in, gain, router_rows, slots, shares, grad_rows, columns):
    quarters, tokens, part = x.shape
    experts = len(grad_rows)
    ext = grad_rows[0].shape[0]
    hc = weight.shape[1] // 4
    size = tokens // PIECES
    rows = router_rows.shape[0]
    dma = pltpu.SemaphoreType.DMA
    others = columns - 1
    kept = (
        jax.ShapeDtypeStruct(x.shape, bf16),
        jax.ShapeDtypeStruct((tokens, 3 * hc), bf16),
        jax.ShapeDtypeStruct((tokens, hc), bf16),
        jax.ShapeDtypeStruct((tokens, 128), f32),
        jax.ShapeDtypeStruct((tokens, part), f32),
        jax.ShapeDtypeStruct((tokens, 128), f32),
    )
    return pl.pallas_call(
        functools.partial(attend_kernel, columns, experts),
        out_shape=kept
        + (
            jax.ShapeDtypeStruct((tokens, part), bf16),
            jax.ShapeDtypeStruct((rows, tokens), f32),
            jax.ShapeDtypeStruct((experts, ext, part), bf16),
            jax.ShapeDtypeStruct((experts, others, ext, part), bf16),
            jax.ShapeDtypeStruct(shares.shape, bf16),
        ),
        in_specs=[hbm(), vmem(), hbm(), pl.BlockSpec(memory_space=pltpu.SMEM)]
        + [vmem()] * 5
        + [hbm()] * (1 + experts),
        out_specs=(hbm(),) * 6 + (vmem(),) * 2 + (hbm(),) * 3,
        scratch_shapes=[pltpu.VMEM(each.shape, each.dtype) for each in kept]
        + [
            pltpu.VMEM((vectors.shape[0], TILE, TILE), f32),
            pltpu.VMEM((PIECES, size, columns * part), bf16),
            pltpu.VMEM((PIECES, size, columns * part), bf16),
            pltpu.VMEM((PIECES, size, columns * part), f32),
            pltpu.VMEM((PIECES, others, size, part), bf16),
            pltpu.VMEM((PIECES, others, size, part), bf16),
            pltpu.VMEM((rows, tokens), f32),
            pltpu.VMEM((quarters - 1, rows, tokens), f32),
            dma((PIECES,)), dma((PIECES,)), dma((PIECES, others)), dma((PIECES, others)),
            dma((quarters - 1,)), dma((quarters - 1,)),
            dma((experts,)), dma((experts,)), dma((experts, others)), dma((experts, others)), dma((6,)),
            pltpu.VMEM(x.shape, bf16), pltpu.VMEM(weight.shape, bf16), dma((2,)), dma((1,)), dma((1,)),
        ],
        compiler_params=pltpu.CompilerParams(
            collective_id=1, has_side_effects=True, vmem_limit_bytes=52 * MIB
        ),
        cost_estimate=microseconds(45),
        name="attend",
    )(x, gains, weight, lengths, vectors, layer_in, gain, router_rows, slots, shares, *grad_rows)


def gather_kernel(columns, experts, *refs):
    layer_ref, gain_ref, shard_ref, place_row, route_ref, cotangent_ref = refs[:6]
    x_ref, gains_ref, weight_ref, slot_row_ref, slot_column_ref, crossed_ref, placed_ref, placed_cot = refs[6:14]
    slot_grads = refs[14 : 14 + experts]
    (
        x_send, x_recv, own_send, own_recv, pass_send, pass_recv, gain_send, gain_recv,
        swap_send, swap_recv, z_send, z_recv, y_send, y_recv, place, cross_send, cross_recv,
        stay, slots, slot_store,
    ) = refs[14 + experts :]
    ex, half = lax.axis_index("ex"), lax.axis_index("half")
    row, col = lax.axis_index("row"), lax.axis_index("col")
    mine = row * columns + col
    tokens, part = layer_ref.shape
    greet(
        grid_peers(columns)
        + [{"ex": (ex + s) % experts} for s in range(1, experts)]
        + [{"half": 1 - half}]
    )
    spread = Spread(
        x_ref, placed_ref, columns, x_send, x_recv, own_send, own_recv, pass_send, pass_recv, stay
    )
    member = 2 * ex + half
    swap = remote(
        shard_ref.at[1 - row], weight_ref.at[row, member], swap_send.at[0], swap_recv.at[0], {"row": 1 - row}
    )
    swap.start()
    arrived = remote(
        shard_ref.at[1 - row], weight_ref.at[1 - row, member], swap_send.at[0], swap_recv.at[0], {"row": 1 - row}
    )
    place_shard = pltpu.make_async_copy(shard_ref.at[row], weight_ref.at[row, member], place.at[0])
    place_shard.start()

    def z_copy(s, a):
        block = weight_ref.at[a, member]
        return remote(block, block, z_send.at[s, a], z_recv.at[s, a], {"ex": (ex + s) % experts})

    def z_arrival(s, a):
        block = weight_ref.at[a, 2 * ((ex - s + experts) % experts) + half]
        return remote(block, block, z_send.at[s, a], z_recv.at[s, a], {"ex": (ex + s) % experts})

    def y_copy(s, a):
        block = weight_ref.at[a, 2 * ((ex - s + experts) % experts) + half]
        return remote(block, block, y_send.at[s, a], y_recv.at[s, a], {"half": 1 - half})

    def y_arrival(s, a):
        block = weight_ref.at[a, 2 * ((ex - s + experts) % experts) + 1 - half]
        return remote(block, block, y_send.at[s, a], y_recv.at[s, a], {"half": 1 - half})

    queue = [(s, a) for s in nearest_first(experts) for a in (row, 1 - row)]
    place_shard.wait()
    z_copy(*queue[0]).start()
    y_copy(0, row).start()
    arrived.wait_recv()
    z_copy(*queue[1]).start()
    y_copy(0, 1 - row).start()
    to_given = given_table(place_row, tokens)
    placed_ref[...] = dot_tn(to_given, layer_ref[...]).astype(bf16)
    spread.start()
    gains_ref[mine] = gain_ref[...]
    gain_copies = [
        remote(gain_ref, gains_ref.at[mine], gain_send.at[i], gain_recv.at[i], where)
        for i, where in enumerate(grid_peers(columns))
    ]
    for copy in gain_copies:
        copy.start()

    number = lax.broadcasted_iota(jnp.int32, (128, tokens), 0)
    hits = jnp.where((route_ref[:1] == number) | (route_ref[1:] == number), 1.0, 0.0)
    low_hits = hits.astype(bf16)
    first_at = lax.broadcasted_iota(jnp.int32, (tokens, tokens), 0)
    second_at = lax.broadcasted_iota(jnp.int32, (tokens, tokens), 1)

    def slot_columns():
        placed_cot[...] = dot_tn(to_given, cotangent_ref[...]).astype(bf16)
        up_to = jnp.where(second_at <= first_at, 1.0, 0.0).astype(bf16)
        same = jnp.where(first_at == second_at, 1.0, 0.0).astype(bf16)
        slot_column_ref[...] = jnp.where(dot_nt(same, low_hits) > 0.5, dot_nt(up_to, low_hits) - 1.0, -1.0)

    def slot_rows():
        from_on = jnp.where(first_at <= second_at, 1.0, 0.0).astype(bf16)
        rows = slot_row_ref.shape[0]
        row_counts = dot_nn(low_hits, from_on)[:rows]
        slot_row_ref[...] = jnp.where(hits[:rows] > 0.5, row_counts - 1.0, -1.0)

    def cotangent_slots(s):
        e = (ex + s) % experts
        ext = slot_grads[s].shape[0]
        hit = slot_row_ref[pl.ds(e, 1), :] == lax.broadcasted_iota(jnp.int32, (ext, tokens), 0).astype(f32)
        slots[s] = dot_nn(jnp.where(hit, 1.0, 0.0).astype(bf16), placed_cot[...]).astype(bf16)
        pltpu.make_async_copy(slots.at[s], slot_grads[s], slot_store.at[s]).start()

    crossing = [
        remote(
            slots.at[0], crossed_ref.at[k - 1], cross_send.at[k - 1], cross_recv.at[k - 1],
            {"col": (col + k) % columns},
        )
        for k in range(1, columns)
    ]
    def first_slots():
        cotangent_slots(0)
        for copy in crossing:
            copy.start()

    jobs = [slot_columns, slot_rows, first_slots] + [functools.partial(cotangent_slots, s) for s in range(1, experts)]
    jobs.pop(0)()
    for i, (s, a) in enumerate(queue):
        z_copy(s, a).wait_send()
        if i + 2 < len(queue):
            z_copy(*queue[i + 2]).start()
        z_arrival(s, a).wait_recv()
        y_copy(s, a).start()
        if i < PIECES:
            spread.hand_on_piece(i)
        if jobs:
            jobs.pop(0)()
    while jobs:
        jobs.pop(0)()
    spread.finish()
    for copy in gain_copies + crossing:
        copy.wait()
    for s in range(experts):
        pltpu.make_async_copy(slots.at[s], slot_grads[s], slot_store.at[s]).wait()
    swap.wait_send()
    for s in range(experts):
        for a in range(2):
            y_arrival(s, a).wait_recv()
            y_copy(s, a).wait_send()


class Spread:
    def __init__(
        self, out, source, columns, x_send, x_recv, own_send, own_recv, pass_send, pass_recv, stay=None
    ):
        self.stay = stay
        row, col = lax.axis_index("row"), lax.axis_index("col")
        mine = row * columns + col
        size = source.shape[0] // PIECES
        self.out, self.source, self.mine = out, source, mine
        self.across, self.own, self.passed = [], [], []
        for i in range(PIECES):
            at = pl.ds(i * size, size)
            for k in range(1, columns):
                self.across.append(
                    remote(
                        source.at[at], out.at[mine, at], x_send.at[i, k - 1], x_recv.at[i, k - 1],
                        {"col": (col + k) % columns},
                    )
                )
                block = out.at[row * columns + (col - k + columns) % columns, at]
                self.passed.append(
                    remote(block, block, pass_send.at[i, k - 1], pass_recv.at[i, k - 1], {"row": 1 - row})
                )
            self.own.append(
                remote(source.at[at], out.at[mine, at], own_send.at[i], own_recv.at[i], {"row": 1 - row})
            )

    def start(self):
        for i in range(PIECES):
            self.start_piece(i)

    def start_piece(self, i):
        others = len(self.across) // PIECES
        for copy in self.across[i * others : (i + 1) * others] + [self.own[i]]:
            copy.start()
        size = self.source.shape[0] // PIECES
        at = pl.ds(i * size, size)
        if self.stay is None:
            self.out[self.mine, at] = self.source[at]
        else:
            pltpu.make_async_copy(self.source.at[at], self.out.at[self.mine, at], self.stay.at[i]).start()

    def hand_on_piece(self, i):
        others = len(self.across) // PIECES
        for n in range(i * others, (i + 1) * others):
            self.across[n].wait_recv()
            self.passed[n].start()

    def wait_piece(self, i):
        others = len(self.across) // PIECES
        for copy in self.passed[i * others : (i + 1) * others] + [self.own[i]]:
            copy.wait_recv()

    def wait_sends(self):
        for copy in self.across + self.own + self.passed:
            copy.wait_send()

    def finish(self):
        if self.stay is not None:
            size = self.source.shape[0] // PIECES
            for i in range(PIECES):
                at = pl.ds(i * size, size)
                pltpu.make_async_copy(self.source.at[at], self.out.at[self.mine, at], self.stay.at[i]).wait()
        for i in range(PIECES):
            self.wait_piece(i)
        self.wait_sends()


def spread_semaphores(columns):
    dma = pltpu.SemaphoreType.DMA
    return [dma((PIECES, columns - 1))] * 2 + [dma((PIECES,))] * 2 + [dma((PIECES, columns - 1))] * 2


def gather(layer_in, gains, shard, place_row, routes, cotangent, stat_rows, ext, experts, columns):
    tokens, part = layer_in.shape
    _, rows, width = shard.shape
    quarters = 2 * columns
    dma = pltpu.SemaphoreType.DMA
    return pl.pallas_call(
        functools.partial(gather_kernel, columns, experts),
        out_shape=(
            jax.ShapeDtypeStruct((quarters, tokens, part), bf16),
            jax.ShapeDtypeStruct((quarters,) + gains.shape, f32),
            jax.ShapeDtypeStruct((2, 2 * experts, rows, width), bf16),
            jax.ShapeDtypeStruct((stat_rows, tokens), f32),
            jax.ShapeDtypeStruct((tokens, 128), f32),
            jax.ShapeDtypeStruct((columns - 1, ext, part), bf16),
            jax.ShapeDtypeStruct((tokens, part), bf16),
            jax.ShapeDtypeStruct((tokens, part), bf16),
        )
        + (jax.ShapeDtypeStruct((ext, part), bf16),) * experts,
        in_specs=[vmem()] * 6,
        out_specs=(hbm(), vmem(), hbm(), vmem(), vmem(), hbm(), vmem(), vmem()) + (hbm(),) * experts,
        scratch_shapes=spread_semaphores(columns)
        + [
            dma((quarters - 1,)), dma((quarters - 1,)), dma((1,)), dma((1,)),
            dma((experts, 2)), dma((experts, 2)), dma((experts, 2)), dma((experts, 2)), dma((1,)),
            dma((columns - 1,)), dma((columns - 1,)), dma((PIECES,)),
            pltpu.VMEM((experts, ext, part), bf16), dma((experts,)),
        ],
        compiler_params=pltpu.CompilerParams(
            collective_id=0, has_side_effects=True, vmem_limit_bytes=52 * MIB
        ),
        cost_estimate=microseconds(30),
        name="gather",
    )(layer_in, gains, shard, place_row, routes, cotangent)


def expert_kernel(
    columns, experts,
    *refs,
):
    mixed_ref, slot_ref, gate_ref, shares, share_came, own_grads, own_crossed, came, crossed = refs[:9]
    (
        home_ref, y_hbm, y_far, keep_up, keep_down, away_up, away_down,
        x, xs, grads, weight, da, db, scaled, core_out, core_in, keep, col_out, col_in,
        load, grad_load, grad_send, grad_recv, z_send, z_recv, own_send, own_recv, col_send, col_recv, pass_send, pass_recv,
        core_send, core_recv, back_send, back_recv, home_send, home_recv, y_send, y_recv, y_sem, store, far_send, far_recv,
        free, last_send, last_recv, on_send, on_recv, y_far_send, y_far_recv,
        hand_send, hand_recv,
    ) = refs[9:]
    ex, half = lax.axis_index("ex"), lax.axis_index("half")
    row, col = lax.axis_index("row"), lax.axis_index("col")
    tokens, part = mixed_ref.shape
    ext = x.shape[2]
    cap = ext - EXTRA
    quarters = 2 * columns
    wide = columns * part
    mine = row * columns + col
    last = experts - 1
    greet(
        [{"ex": (ex + s) % experts} for s in range(1, experts)]
        + [{"col": (col + k) % columns} for k in range(1, columns)]
        + [{"row": 1 - row}]
    )

    own_dims = pl.ds(pl.multiple_of(row * wide, wide), wide)
    other_dims = pl.ds(pl.multiple_of((1 - row) * wide, wide), wide)
    at_home = row == half
    loads, handed = [], []

    def to_row(source, place, i, stays):
        here = pltpu.make_async_copy(source, place, load.at[i])
        there = remote(source, place, hand_send.at[i], hand_recv.at[i], {"row": 1 - row})

        def start():
            pl.when(stays)(here.start)
            pl.when(jnp.logical_not(stays))(there.start)

        def wait():
            pl.when(stays)(here.wait)
            pl.when(jnp.logical_not(stays))(there.wait_send)

        def arrive():
            pl.when(stays)(there.wait_recv)

        return start, wait, arrive

    own_start, own_wait, own_arrive = to_row(shares, weight.at[:, :, own_dims], 0, at_home)
    came_start, came_wait, came_arrive = to_row(
        share_came, weight.at[:, :, own_dims], 1, jnp.logical_not(at_home)
    )
    own_start()
    came_start()
    final_chunk = farthest_first(experts)[-1]
    for s in range(experts):
        for k in range(columns):
            if k and s == final_chunk:
                continue
            at = (s, k)
            place = row * columns + (col - k + columns) % columns
            if s == 0:
                block = own_crossed.at[k - 1] if k else own_grads
            else:
                block = crossed.at[s, k - 1] if k else came.at[s]
            loads.append(pltpu.make_async_copy(block, grads.at[place, s], grad_load.at[at]))
            handed.append(
                remote(block, grads.at[place, s], grad_send.at[at], grad_recv.at[at], {"row": 1 - row})
            )
    for copy in loads + handed:
        copy.start()

    def last_copy(k):
        return remote(
            came.at[final_chunk], grads.at[mine, final_chunk], last_send.at[k - 1], last_recv.at[k - 1],
            {"col": (col + k) % columns},
        )

    def last_on(k):
        block = grads.at[row * columns + (col - k + columns) % columns, final_chunk]
        return remote(block, block, on_send.at[k - 1], on_recv.at[k - 1], {"row": 1 - row})

    def z_copy(s):
        return remote(
            xs.at[s], x.at[mine, s], z_send.at[s], z_recv.at[s], {"ex": (ex + s) % experts}
        )

    def own_copy(s):
        block = x.at[mine, s]
        return remote(block, block, own_send.at[s], own_recv.at[s], {"row": 1 - row})

    def col_copy(s, k):
        block = x.at[mine, s]
        return remote(
            block, block, col_send.at[s, k - 1], col_recv.at[s, k - 1], {"col": (col + k) % columns}
        )

    def pass_copy(s, k):
        block = x.at[row * columns + (col - k + columns) % columns, s]
        return remote(
            block, block, pass_send.at[s, k - 1], pass_recv.at[s, k - 1], {"row": 1 - row}
        )

    def spread(s):
        own_copy(s).start()
        for k in range(1, columns):
            col_copy(s, k).start()

    def hand_on(s):
        for k in range(1, columns):
            col_copy(s, k).wait_recv()
            pass_copy(s, k).start()

    def slots_of(e):
        hit = slot_ref[pl.ds(e, 1), :] == lax.broadcasted_iota(jnp.int32, (cap, tokens), 0).astype(f32)
        values = dot_nn(jnp.where(hit, 1.0, 0.0).astype(bf16), mixed_ref[...]).astype(bf16)
        gate = jnp.sum(jnp.where(hit, gate_ref[pl.ds(e, 1), :], 0.0), axis=1, keepdims=True)
        return values, write_extra(gate, part).astype(bf16)

    def build(s):
        values, extra = slots_of((ex + s) % experts)
        xs[s, :cap] = values
        xs[s, cap:] = extra

    def nth(p):
        far = experts // 2
        return jnp.where(p == 1, far, jnp.where((p > 1) & (p <= far), p - 1, p))

    build(nth(1))
    z_copy(nth(1)).start()
    values, extra = slots_of(ex)
    x[mine, 0, :cap] = values
    x[mine, 0, cap:] = extra
    spread(0)
    for k in range(1, columns):
        last_copy(k).start()

    @pl.loop(2, experts)
    def _(p):
        build(nth(p))

    for copy in loads:
        copy.wait()
    for copy in handed:
        copy.wait()
    hand_on(0)
    z_copy(nth(1)).wait_send()
    z_copy(nth(2)).start()
    z_copy(nth(1)).wait_recv()
    spread(nth(1))
    for wait in (own_wait, own_arrive, came_wait, came_arrive):
        wait()

    def core_copy(s):
        return remote(core_out.at[s], core_in.at[s], core_send.at[s], core_recv.at[s], {"row": 1 - row})

    def back_copy(s, k):
        return remote(
            col_out.at[s, k - 1], col_in.at[s, k - 1], back_send.at[s, k - 1], back_recv.at[s, k - 1],
            {"col": (col + k) % columns},
        )

    def home_copy(s):
        return remote(
            xs.at[s], home_ref.at[s], home_send.at[s], home_recv.at[s], {"ex": (ex - s + experts) % experts}
        )

    def stores(ups, downs):
        parts = [(weight.at[:2], ups, 0), (weight.at[2], downs, 1)]
        return [
            (
                pltpu.make_async_copy(source.at[(slice(None),) * (2 - i) + (own_dims,)], out, store.at[i]),
                remote(
                    source.at[(slice(None),) * (2 - i) + (other_dims,)], out, far_send.at[i], far_recv.at[i],
                    {"row": 1 - row},
                ),
            )
            for source, out, i in parts
        ]

    def store_gradients(i):
        for mine_here, (ups, downs) in ((True, (keep_up, keep_down)), (False, (away_up, away_down))):

            @pl.when((row == half) == mine_here)
            def _():
                for copy in stores(ups, downs)[i]:
                    copy.start()

    def wait_gradients(i):
        for copy in stores(keep_up, keep_down)[i]:
            copy.wait()

    def y_share(s):
        return remote(core_out.at[s], core_in.at[s], y_send.at[s], y_recv.at[s], {"row": 1 - row})

    def y_copy(s):
        return pltpu.make_async_copy(core_in.at[s], y_hbm.at[:, s], y_sem.at[s])

    def after_core(s, slot):
        core_copy(s).wait_recv()
        keep[slot] = keep[slot] + core_in[s].astype(f32)
        for k in range(1, columns):
            to = (col + k) % columns
            col_out[s, k - 1] = keep[slot, to].astype(bf16)
            back_copy(s, k).start()

    def after_columns(s, slot):
        total = keep[slot, col]
        for k in range(1, columns):
            back_copy(s, k).wait_recv()
            total = total + col_in[s, k - 1].astype(f32)
        return total.astype(bf16)

    def send_home(s, slot):
        xs[s] = after_columns(s, slot)
        home_copy(s).start()

    @pl.loop(0, experts)
    def _(p):
        s = nth(p)
        slot = jnp.where(p == 0, 2, p % 2)

        @pl.when(p == 1)
        def _():
            for k in range(1, columns):
                last_copy(k).wait_recv()
                last_on(k).start()

        @pl.when(p == last)
        def _():
            for k in range(1, columns):
                last_on(k).wait_recv()

        grad = jnp.concatenate([grads[q, s] for q in range(quarters)], axis=1)
        d = dot_nt(grad, weight[2])
        own_copy(s).wait_recv()
        for k in range(1, columns):
            pass_copy(s, k).wait_recv()

        @pl.when(p > 1)
        def _():
            after_core(nth(p - 1), (p - 1) % 2)

        @pl.when(p > 2)
        def _():
            send_home(nth(p - 2), p % 2)

        rows = jnp.concatenate([x[q, s] for q in range(quarters)], axis=1)
        gate = read_extra(x[mine, s, cap:], ext)
        a = dot_nt(rows, weight[0])
        b = dot_nt(rows, weight[1])
        d = d * gate
        square = a * a
        t = jnp.tanh(a * (GELU_A + (GELU_A * GELU_B) * square))
        part_on = 0.5 + 0.5 * t
        smooth = a * part_on
        slope = part_on + (a * (0.5 - 0.5 * t * t)) * (GELU_A + (3 * GELU_A * GELU_B) * square)
        active = smooth * b
        da[s] = (d * b * slope).astype(bf16)
        db[s] = (d * smooth).astype(bf16)
        scaled[s] = (active * gate).astype(bf16)
        extra = write_extra(jnp.sum(d * active, axis=1, keepdims=True), part)

        @pl.when((p > 0) & (p + 2 < experts))
        def _():
            z_copy(nth(p + 2)).wait_recv()
            spread(nth(p + 2))

        @pl.when((p > 0) & (p + 1 < experts))
        def _():
            hand_on(nth(p + 1))

        @pl.when((p > 0) & (p + 3 < experts))
        def _():
            z_copy(nth(p + 2)).wait_send()
            z_copy(nth(p + 3)).start()

        for j in range(columns):
            dims = pl.ds(pl.multiple_of(((1 - row) * columns + j) * part, part), part)
            value = dot_nn(da[s], weight[0, :, dims]) + dot_nn(db[s], weight[1, :, dims])
            core_out[s, j] = value.astype(bf16)
            core_out[s, j, cap:] = extra.astype(bf16)
        core_copy(s).start()
        for j in range(columns):
            dims = pl.ds(pl.multiple_of((row * columns + j) * part, part), part)
            keep[slot, j] = dot_nn(da[s], weight[0, :, dims]) + dot_nn(db[s], weight[1, :, dims])
            keep[slot, j, cap:] = extra

        @pl.when(p == 0)
        def _():
            hand_on(nth(1))
            z_copy(nth(2)).wait_send()
            z_copy(nth(3)).start()
            z_copy(nth(2)).wait_recv()
            spread(nth(2))

    def flat(ref, *at):
        block = ref[at] if at else ref[...]
        return block.reshape(experts * ext, block.shape[-1])

    before, final = nth(last - 1), nth(last)
    z_copy(final).wait_send()
    after_core(final, last % 2)
    after_core(0, 2)
    pl.semaphore_signal(free, inc=1, device_id={"row": 1 - row}, device_id_type=MESH)
    send_home(before, (last - 1) % 2)

    pl.semaphore_wait(free, 1)

    @pl.loop(0, experts)
    def _(s):
        core_copy(s).wait_send()
        for j in range(columns):
            dims = pl.ds(pl.multiple_of(((1 - row) * columns + j) * part, part), part)
            core_out[s, j] = dot_nn(scaled[s], weight[2, :, dims]).astype(bf16)
        y_share(s).start()

    def y_far_copy(k):
        return remote(
            core_in.at[nth(1), (col + k) % columns], y_far.at[k - 1], y_far_send.at[k - 1], y_far_recv.at[k - 1],
            {"col": (col + k) % columns},
        )

    @pl.loop(0, experts)
    def _(p):
        s = nth((p + 1) % experts)
        y_share(s).wait_recv()
        for j in range(columns):
            dims = pl.ds(pl.multiple_of((row * columns + j) * part, part), part)
            value = dot_nn(scaled[s], weight[2, :, dims]) + core_in[s, j].astype(f32)
            core_in[s, j] = value.astype(bf16)
        y_copy(s).start()

        @pl.when(p == 0)
        def _():
            for k in range(1, columns):
                y_far_copy(k).start()

    low = flat(scaled)
    for q in range(quarters):
        weight[2, :, q * part : (q + 1) * part] = dot_tn(low, flat(grads, q)).astype(bf16)
    store_gradients(1)
    send_home(final, last % 2)
    for g, hidden in enumerate((da, db)):
        low = flat(hidden)
        for q in range(quarters):
            weight[g, :, q * part : (q + 1) * part] = dot_tn(low, flat(x, q)).astype(bf16)
    store_gradients(0)
    home_ref[0] = after_columns(0, 2)
    wait_gradients(0)
    wait_gradients(1)
    for k in range(1, columns):
        y_far_copy(k).wait()
        last_copy(k).wait_send()
        last_on(k).wait_send()

    @pl.loop(1, experts)
    def _(s):
        home_copy(s).wait_recv()
        home_copy(s).wait_send()

    @pl.loop(0, experts)
    def _(s):
        own_copy(s).wait_send()
        y_share(s).wait_send()
        y_copy(s).wait()
        for k in range(1, columns):
            col_copy(s, k).wait_send()
            pass_copy(s, k).wait_send()
            back_copy(s, k).wait_send()


def expert_block(mixed, slots, gates, shares, share_came, own_grads, own_crossed, came, crossed, columns):
    tokens, part = mixed.shape
    quarters = 2 * columns
    experts, ext, _ = came.shape
    _, ff, wide = shares.shape
    dma = pltpu.SemaphoreType.DMA
    others = columns - 1
    return pl.pallas_call(
        functools.partial(expert_kernel, columns, experts),
        out_shape=(
            jax.ShapeDtypeStruct((experts, ext, part), bf16),
            jax.ShapeDtypeStruct((columns, experts, ext, part), bf16),
            jax.ShapeDtypeStruct((others, ext, part), bf16),
        )
        + (jax.ShapeDtypeStruct((2, ff, wide), bf16), jax.ShapeDtypeStruct((ff, wide), bf16)) * 2,
        in_specs=[vmem()] * 3 + [hbm()] * 6,
        out_specs=(vmem(),) + (hbm(),) * 6,
        scratch_shapes=[
            pltpu.VMEM((quarters, experts, ext, part), bf16),
            pltpu.VMEM((experts, ext, part), bf16),
            pltpu.VMEM((quarters, experts, ext, part), bf16),
            pltpu.VMEM((3, ff, D), bf16),
            pltpu.VMEM((experts, ext, ff), bf16),
            pltpu.VMEM((experts, ext, ff), bf16),
            pltpu.VMEM((experts, ext, ff), bf16),
            pltpu.VMEM((experts, columns, ext, part), bf16),
            pltpu.VMEM((experts, columns, ext, part), bf16),
            pltpu.VMEM((3, columns, ext, part), f32),
            pltpu.VMEM((experts, others, ext, part), bf16),
            pltpu.VMEM((experts, others, ext, part), bf16),
            dma((2,)), dma((experts, columns)), dma((experts, columns)), dma((experts, columns)),
            dma((experts,)), dma((experts,)), dma((experts,)), dma((experts,)),
            dma((experts, others)), dma((experts, others)), dma((experts, others)), dma((experts, others)),
            dma((experts,)), dma((experts,)), dma((experts, others)), dma((experts, others)),
            dma((experts,)), dma((experts,)), dma((experts,)), dma((experts,)), dma((experts,)),
            dma((2,)), dma((2,)), dma((2,)), pltpu.SemaphoreType.REGULAR,
            dma((others,)), dma((others,)), dma((others,)), dma((others,)), dma((others,)), dma((others,)),
            dma((2,)), dma((2,)),
        ],
        compiler_params=pltpu.CompilerParams(
            collective_id=2, has_side_effects=True, vmem_limit_bytes=56 * MIB
        ),
        cost_estimate=microseconds(80),
        name="expert_block",
    )(mixed, slots, gates, shares, share_came, own_grads, own_crossed, came, crossed)


def settle_part(
    columns, experts,
    home_ref, slot_ref, column_ref, second_ref, mixed_ref, cotangent_ref, gain_ref, router_ref,
    branch_ref, two_ref, drouter_ref, dgain_ref,
    low, dmixed_ref, dlogit_ref, stat, stat_in, stat_send, stat_recv, *rest,
):
    *spread_sems, after_spread = rest
    ex = lax.axis_index("ex")
    tokens, part = second_ref.shape
    ext = home_ref.shape[1]
    cap = ext - EXTRA
    size = tokens // PIECES
    lane = lax.broadcasted_iota(jnp.int32, (size, 128), 1)
    extras = []
    for s in range(experts):
        values = read_extra(home_ref[s, cap:], ext)
        near = values.astype(bf16)
        left = (values - near.astype(f32)).astype(bf16)
        extras.append(
            jnp.concatenate([jnp.broadcast_to(near, (ext, 128)), jnp.broadcast_to(left, (ext, 128))], axis=1)
        )
    peers = grid_peers(columns)
    spread = Spread(branch_ref, low, columns, *spread_sems)

    def stat_copy(i, n):
        at = pl.ds(i * size, size)
        return remote(
            stat.at[:, at], stat_in.at[n, :, at], stat_send.at[i, n], stat_recv.at[i, n], peers[n]
        )

    def combine(i):
        at = slice(i * size, (i + 1) * size)
        dmixed = jnp.zeros((size, part), f32)
        gate_grads = jnp.zeros((size, 128), f32)
        for s in range(experts):
            e = (ex + s) % experts
            place = jnp.sum(jnp.where(lane == e, slot_ref[at, :], 0.0), axis=1, keepdims=True)
            hit = place == lax.broadcasted_iota(jnp.int32, (size, ext), 1).astype(f32)
            pick_rows = jnp.where(hit, 1.0, 0.0).astype(bf16)
            dmixed = dmixed + dot_nn(pick_rows, home_ref[s])
            found = dot_nn(pick_rows, extras[s])
            gate_grads = jnp.where(lane == e, found[:, :128] + found[:, 128:], gate_grads)
        gates = jnp.where(lane < experts, column_ref[at, :], 0.0)
        dlogits = gate_grads - gates * jnp.sum(gate_grads, axis=1, keepdims=True)
        dlogit_ref[at, :] = dlogits
        dmixed = dmixed + dot_exact(dlogits[:, : router_ref.shape[0]], router_ref[...], ((1,), (0,)))
        dmixed_ref[at, :] = dmixed
        stat[:, at] = dot_exact(
            jnp.ones((8, part), f32), second_ref[at, :] * dmixed * gain_ref[1:2], ((1,), (1,))
        )
        for n in range(len(peers)):
            stat_copy(i, n).start()

    first_row = jnp.where(lax.broadcasted_iota(jnp.int32, (8, 128), 0) == 0, 1.0, 0.0)

    def close(i):
        at = slice(i * size, (i + 1) * size)
        total = stat[:, at]
        for n in range(len(peers)):
            stat_copy(i, n).wait_recv()
            total = total + stat_in[n, :, at]
        row_total = dot_exact(total, first_row, ((0,), (0,)))[:, :1]
        inverse = column_ref[at, experts : experts + 1]
        two = cotangent_ref[at, :].astype(f32) + inverse * (
            dmixed_ref[at, :] * gain_ref[1:2] - second_ref[at, :] * (inverse * inverse * row_total / D)
        )
        two_ref[at, :] = two
        low[at, :] = two.astype(bf16)
        spread.start_piece(i)

    for i in reversed(range(PIECES)):
        combine(i)
        if i + 1 < PIECES:
            close(i + 1)
            if i + 2 < PIECES:
                spread.hand_on_piece(i + 2)
    close(0)
    after_spread()

    def sums():
        rows = drouter_ref.shape[0]
        drouter_ref[...] = dot_exact(dlogit_ref[...], mixed_ref[...].astype(f32), ((0,), (0,)))[:rows]
        normed = second_ref[...] * column_ref[:, experts : experts + 1]
        dgain_ref[...] = jnp.broadcast_to(
            jnp.sum(dmixed_ref[...] * normed, axis=0, keepdims=True), dgain_ref.shape
        )

    for i in range(PIECES):
        for n in range(len(peers)):
            stat_copy(i, n).wait_send()
    return spread, sums


def finish_part(
    columns, experts,
    dfirst_ref, dweight_ref, small, layer_ref, two_ref, gain_ref, inverse_ref,
    placed_grad, qkv_grad_ref, proj_grad_ref, sums_ref,
    core_in, keep, col_out, col_in, stat, stat_in, y_in, z_out, z_in, held, row_out, row_in, small_in,
    core_send, core_recv, col_send, col_recv, stat_send, stat_recv,
    y_send, y_recv, z_send, z_recv, row_send, row_recv, small_send, small_recv, others, others_meanwhile, while_waiting,
):
    ex, half = lax.axis_index("ex"), lax.axis_index("half")
    row, col = lax.axis_index("row"), lax.axis_index("col")
    tokens, part = layer_ref.shape
    size = tokens // PIECES
    members = 2 * experts
    rows = held.shape[1]
    hc = held.shape[2] // 4

    def core_copy(i):
        at = pl.ds(i * size, size)
        return remote(
            dfirst_ref.at[pl.ds((1 - row) * columns, columns), at], core_in.at[:, at],
            core_send.at[i], core_recv.at[i], {"row": 1 - row},
        )

    def block_of(member, a):
        return pl.ds(pl.multiple_of((a * members + member) * rows, rows), rows)

    def y_copy(s, a):
        to = 2 * ((ex + s) % experts) + 1 - half
        return remote(
            dweight_ref.at[block_of(to, a)], y_in.at[s, a], y_send.at[s, a], y_recv.at[s, a], {"half": 1 - half}
        )

    def z_copy(s, a):
        return remote(
            z_out.at[s, a], z_in.at[s, a], z_send.at[s, a], z_recv.at[s, a], {"ex": (ex + s) % experts}
        )

    queue = [(s, a) for s in nearest_first(experts)[::-1] + [0] for a in range(2)]
    cell = {}

    def col_copy(i, k):
        at = pl.ds(i * size, size)
        return remote(
            col_out.at[k - 1, at], col_in.at[k - 1, at], col_send.at[i, k - 1], col_recv.at[i, k - 1],
            {"col": (col + k) % columns},
        )

    def start(i):
        core_copy(i).start()

    def cross(i):
        at = slice(i * size, (i + 1) * size)
        core_copy(i).wait_recv()
        for j in range(columns):
            keep[j, at] = dfirst_ref[row * columns + j, at].astype(f32) + core_in[j, at].astype(f32)
        for k in range(1, columns):
            col_out[k - 1, at] = keep[(col + k) % columns, at].astype(bf16)
            col_copy(i, k).start()

    def normed():
        return layer_ref[...].astype(f32) * inverse_ref[:, 127:128]

    peers = grid_peers(columns)

    def stat_copy(n):
        return remote(stat, stat_in.at[n], stat_send.at[n], stat_recv.at[n], peers[n])

    def arrive():
        for i in range(PIECES):
            for k in range(1, columns):
                col_copy(i, k).wait_recv()
        dnorm = keep[col]
        for k in range(1, columns):
            dnorm = dnorm + col_in[k - 1].astype(f32)
        keep[col] = dnorm
        stat[...] = dot_exact(
            jnp.ones((8, part), f32), layer_ref[...].astype(f32) * (dnorm * gain_ref[:1]), ((1,), (1,))
        )
        for n in range(len(peers)):
            stat_copy(n).start()
        small[:8] = jnp.broadcast_to(jnp.sum(dnorm * normed(), axis=0, keepdims=True), (8, part))
        cell["smalls"] = [
            remote(small, small_in.at[i], small_send.at[i], small_recv.at[i], where)
            for i, where in enumerate(others)
        ]
        for copy in cell["smalls"]:
            copy.start()

    def close():
        total = stat[...]
        for n in range(len(peers)):
            stat_copy(n).wait_recv()
            total = total + stat_in[n]
        first_row = jnp.where(lax.broadcasted_iota(jnp.int32, (8, 128), 0) == 0, 1.0, 0.0)
        row_total = dot_exact(total, first_row, ((0,), (0,)))[:, :1]
        inverse = inverse_ref[:, 127:128]
        placed_grad[...] = (
            two_ref[...] + inverse * (keep[col] * gain_ref[:1] - normed() * (inverse * row_total / D))
        ).astype(bf16)

    def rest():
        for at in queue[:2]:
            y_copy(*at).start()
        cross(0)
        others_meanwhile()
        for n, (s, a) in enumerate(queue):
            y_copy(s, a).wait_send()
            if n + 2 < len(queue):
                y_copy(*queue[n + 2]).start()
            y_copy(s, a).wait_recv()
            own = dweight_ref[block_of(2 * ((ex + s) % experts) + half, a), :]
            total = own.astype(f32) + y_in[s, a].astype(f32)
            if s > 0:
                z_out[s, a] = total.astype(bf16)
                z_copy(s, a).start()
            else:
                held[a] = total
            if n == 2:
                arrive()
            if n == 4:
                close()
        while_waiting()
        for s in nearest_first(experts)[::-1]:
            for a in range(2):
                z_copy(s, a).wait_recv()
                held[a] = held[a] + z_in[s, a].astype(f32)
        row_out[...] = held[1 - row].astype(bf16)
        swap = remote(row_out, row_in, row_send.at[0], row_recv.at[0], {"row": 1 - row})
        swap.start()
        sums = small[...]
        for i, copy in enumerate(cell["smalls"]):
            copy.wait_recv()
            sums = sums + small_in[i]
        sums_ref[...] = sums
        swap.wait_recv()
        for at_row, values in ((row, held[row]), (1 - row, row_in[...].astype(f32))):
            proj_grad_ref[at_row] = values[:, 3 * hc :]
            for k in range(3):
                qkv_grad_ref[:, k, at_row, :] = values[:, k * hc : (k + 1) * hc]
        swap.wait_send()
        for copy in cell["smalls"]:
            copy.wait_send()
        for n in range(len(peers)):
            stat_copy(n).wait_send()
        for i in range(PIECES):
            core_copy(i).wait_send()
            for k in range(1, columns):
                col_copy(i, k).wait_send()
        for s, a in queue:
            if s > 0:
                z_copy(s, a).wait_send()

    return start, cross, rest


def tail_kernel(columns, experts, *refs):
    (
        home_ref, slot_ref, column_ref, second_ref, mixed_ref, cotangent_ref, gain_two, router_ref,
        qkv_ref, lse_ref, attended_ref, first_ref, weight_ref, place_row, length_ref, vector_ref,
        layer_ref, gain_one, y_hbm, y_far, away_up, away_down,
    ) = refs[:22]
    layer_out_ref, input_grad_ref, qkv_grad_ref, proj_grad_ref, sums_ref, came_up, came_down = refs[22:29]
    scratch = list(refs[29:])

    def take(count):
        taken = scratch[:count]
        del scratch[:count]
        return taken

    branch_ref, two_ref, drouter_ref, dgain_ref, dfirst_ref, dweight_ref, dvector_ref, small = take(8)
    y_own, y_in, y_home = take(3)
    y_load, y_send, y_recv, y_away, y_came, half_send, half_recv = take(7)
    y_far_in, placed_out, placed_grad = take(3)
    settle_scratch = take(7 + 6)
    attention_scratch = take(5)
    finish_scratch = take(13 + 14)
    ex, half, col = lax.axis_index("ex"), lax.axis_index("half"), lax.axis_index("col")
    members = [
        {"ex": (ex + s) % experts, "half": (half + h) % 2}
        for s in range(experts)
        for h in range(2)
        if s + h > 0
    ]
    greet(grid_peers(columns) + members)

    halves = [
        remote(source, out, half_send.at[i], half_recv.at[i], {"half": 1 - half})
        for i, (source, out) in enumerate(((away_up, came_up), (away_down, came_down)))
    ]
    for copy in halves:
        copy.start()

    far, *near = farthest_first(experts)
    y_stay = pltpu.make_async_copy(y_hbm.at[col], y_own, y_load.at[0])
    y_stay.start()
    y_far_load = pltpu.make_async_copy(y_far, y_far_in, y_load.at[1])
    y_far_load.start()

    def y_cross(s, k):
        to = (col + k) % columns
        return remote(
            y_hbm.at[to, s], y_in.at[s, k - 1], y_send.at[s, k - 1], y_recv.at[s, k - 1], {"col": to}
        )

    def y_copy(s):
        return remote(
            y_own.at[s], y_home.at[s], y_away.at[s], y_came.at[s], {"ex": (ex - s + experts) % experts}
        )

    def y_sum(s, others):
        total = y_own[s].astype(f32)
        for other in others:
            total = total + other.astype(f32)
        if s > 0:
            y_own[s] = total.astype(bf16)
            y_copy(s).start()
        else:
            y_home[0] = total.astype(bf16)

    def y_homeward(s):
        for k in range(1, columns):
            y_cross(s, k).wait_recv()
        y_sum(s, [y_in[s, k - 1] for k in range(1, columns)])

    def after_spread():
        for s in near + [0]:
            for k in range(1, columns):
                y_cross(s, k).start()

    y_stay.wait()
    y_far_load.wait()
    y_sum(far, [y_far_in[k - 1] for k in range(1, columns)])
    spread, settle_sums = settle_part(
        columns, experts,
        home_ref, slot_ref, column_ref, second_ref, mixed_ref, cotangent_ref, gain_two, router_ref,
        branch_ref, two_ref, drouter_ref, dgain_ref, *settle_scratch, after_spread,
    )
    ways = near + [0]
    tokens, part = second_ref.shape
    stat_rows = drouter_ref.shape[0]

    def others_meanwhile():
        settle_sums()
        bias_sums(attention_scratch[1], dvector_ref)
        small[8:16] = dgain_ref[...]
        small[16 : 16 + stat_rows] = drouter_ref[...]
        pieces = 2 * TILE // part
        for i in range(dvector_ref.shape[0]):
            for n in range(pieces):
                at = 16 + stat_rows + i * pieces + n
                small[at : at + 1] = dvector_ref[i : i + 1, n * part : (n + 1) * part]

    def while_waiting():
        for s in range(1, experts):
            y_copy(s).wait_recv()
        ext = y_own.shape[1]
        size = tokens // PIECES
        lane = lax.broadcasted_iota(jnp.int32, (size, 128), 1)
        for i in range(PIECES):
            at = slice(i * size, (i + 1) * size)
            total = second_ref[at, :]
            for s in range(experts):
                place = jnp.sum(jnp.where(lane == (ex + s) % experts, slot_ref[at, :], 0.0), axis=1, keepdims=True)
                hit = place == lax.broadcasted_iota(jnp.int32, (size, ext), 1).astype(f32)
                total = total + dot_nn(jnp.where(hit, 1.0, 0.0).astype(bf16), y_home[s])
            placed_out[at, :] = total.astype(bf16)
        to_given = given_table(place_row, tokens)
        layer_out_ref[...] = dot_nn(to_given, placed_out[...]).astype(bf16)
        input_grad_ref[...] = dot_nn(to_given, placed_grad[...]).astype(bf16)

    start, cross, rest = finish_part(
        columns, experts,
        dfirst_ref, dweight_ref, small, layer_ref, two_ref, gain_one, lse_ref,
        placed_grad, qkv_grad_ref, proj_grad_ref, sums_ref, *finish_scratch, members, others_meanwhile, while_waiting,
    )

    def before(a):
        if a + 1 == PIECES:
            spread.hand_on_piece(1)
        elif a == 2:
            spread.hand_on_piece(0)
        spread.wait_piece(a)

    def after(a):
        start(a)
        if a + 1 < PIECES:
            cross(a + 1)
        if a == 0:
            while ways:
                y_homeward(ways.pop(0))
        elif a + 2 < PIECES and len(ways) > 1:
            y_homeward(ways.pop(0))

    attention_backward_kernel(
        branch_ref, qkv_ref, lse_ref, attended_ref, first_ref, weight_ref, length_ref, vector_ref,
        dfirst_ref, dweight_ref, dvector_ref, *attention_scratch, before, after,
    )
    rest()
    spread.wait_sends()
    for copy in halves:
        copy.wait()
    for s in near + [0]:
        for k in range(1, columns):
            y_cross(s, k).wait_send()
    for s in range(1, experts):
        y_copy(s).wait_send()


def tail(
    home, slots, table, second, mixed, cotangent, gain_two, router_rows,
    qkv, lse, attended, first, weight, placing, lengths, vectors, layer_in, gain_one, y, y_far, away_up, away_down,
    stat_rows, experts, columns,
):
    tokens, part = second.shape
    quarters, others = 2 * columns, columns - 1
    hc = weight.shape[1] // 4
    ext = home.shape[1]
    rows, width = D // (4 * experts), 4 * hc
    small = (16 + stat_rows + vectors.size // part, part)
    dma = pltpu.SemaphoreType.DMA
    members = 2 * experts
    return pl.pallas_call(
        functools.partial(tail_kernel, columns, experts),
        out_shape=(
            jax.ShapeDtypeStruct((tokens, part), bf16),
            jax.ShapeDtypeStruct((tokens, part), bf16),
            jax.ShapeDtypeStruct((rows, 3, 2, hc), f32),
            jax.ShapeDtypeStruct((2, rows, hc), f32),
            jax.ShapeDtypeStruct(small, f32),
            jax.ShapeDtypeStruct(away_up.shape, bf16),
            jax.ShapeDtypeStruct(away_down.shape, bf16),
        ),
        in_specs=[vmem()] * 14 + [pl.BlockSpec(memory_space=pltpu.SMEM)] + [vmem()] * 3 + [hbm()] * 4,
        out_specs=(vmem(),) * 5 + (hbm(),) * 2,
        scratch_shapes=[
            pltpu.VMEM((quarters, tokens, part), bf16),
            pltpu.VMEM((tokens, part), f32),
            pltpu.VMEM((stat_rows, part), f32),
            pltpu.VMEM((8, part), f32),
            pltpu.VMEM((quarters, tokens, part), bf16),
            pltpu.VMEM((D, width), bf16),
            pltpu.VMEM(vectors.shape, f32),
            pltpu.VMEM(small, f32),
            pltpu.VMEM((experts, ext, part), bf16),
            pltpu.VMEM((experts, others, ext, part), bf16),
            pltpu.VMEM((experts, ext, part), bf16),
            dma((2,)), dma((experts, others)), dma((experts, others)), dma((experts,)), dma((experts,)), dma((2,)), dma((2,)),
            pltpu.VMEM((others, ext, part), bf16),
            pltpu.VMEM((tokens, part), bf16),
            pltpu.VMEM((tokens, part), bf16),
            pltpu.VMEM((tokens, part), bf16),
            pltpu.VMEM((tokens, part), f32),
            pltpu.VMEM((tokens, 128), f32),
            pltpu.VMEM((8, tokens), f32),
            pltpu.VMEM((quarters - 1, 8, tokens), f32),
            dma((PIECES, quarters - 1)), dma((PIECES, quarters - 1)),
        ]
        + spread_semaphores(columns)
        + [
            pltpu.VMEM((vectors.shape[0], TILE, TILE), f32),
            pltpu.VMEM((vectors.shape[0], TILE, TILE), f32),
            pltpu.VMEM((tokens, hc), bf16),
            pltpu.VMEM((tokens, 3 * hc), bf16),
            pltpu.VMEM((tokens, 2 * hc), f32),
            pltpu.VMEM((columns, tokens, part), bf16),
            pltpu.VMEM((columns, tokens, part), f32),
            pltpu.VMEM((others, tokens, part), bf16),
            pltpu.VMEM((others, tokens, part), bf16),
            pltpu.VMEM((8, tokens), f32),
            pltpu.VMEM((quarters - 1, 8, tokens), f32),
            pltpu.VMEM((experts, 2, rows, width), bf16),
            pltpu.VMEM((experts, 2, rows, width), bf16),
            pltpu.VMEM((experts, 2, rows, width), bf16),
            pltpu.VMEM((2, rows, width), f32),
            pltpu.VMEM((rows, width), bf16),
            pltpu.VMEM((rows, width), bf16),
            pltpu.VMEM((members - 1,) + small, f32),
            dma((PIECES,)), dma((PIECES,)), dma((PIECES, others)), dma((PIECES, others)),
            dma((quarters - 1,)), dma((quarters - 1,)),
            dma((experts, 2)), dma((experts, 2)), dma((experts, 2)), dma((experts, 2)),
            dma((1,)), dma((1,)), dma((members - 1,)), dma((members - 1,)),
        ],
        compiler_params=pltpu.CompilerParams(
            collective_id=3, has_side_effects=True, vmem_limit_bytes=47 * MIB
        ),
        cost_estimate=microseconds(90),
        name="tail",
    )(
        home, slots, table, second, mixed, cotangent, gain_two, router_rows,
        qkv, lse, attended, first, weight, placing, lengths, vectors, layer_in, gain_one, y, y_far, away_up, away_down,
    )


def adamw_step(weight, grad, first, second, rate):
    first_new = beta_first * first + (1.0 - beta_first) * grad
    second_new = beta_second * second + (1.0 - beta_second) * grad * grad
    moment = first_new / (1.0 - beta_first**STEP)
    spread = second_new / (1.0 - beta_second**STEP)
    weight_new = weight - rate * (
        moment / (jnp.sqrt(spread) + adam_epsilon) + weight_decay * weight
    )
    return (weight_new, first_new, second_new)


def local(
    layer_in, lengths, placing, routes, cotangent,
    norm_gains, gain_first, gain_second, rel_bias, bias_first, bias_second,
    router, router_first, router_second, qkv_weight, qkv_first, qkv_second,
    proj_weight, proj_first, proj_second, expert_up, up_first, up_second,
    expert_down, down_first, down_second,
):
    tokens, part = layer_in.shape
    experts, columns = lax.axis_size("ex"), lax.axis_size("col")
    quarters = 2 * columns
    cap = min(tokens, 5 * TOP * tokens // (4 * experts))
    ext = cap + EXTRA
    hc = qkv_weight.shape[5]
    head_count = hc // HD
    wide = D // 2

    qkv_low = jnp.moveaxis(qkv_weight[0, 0].astype(bf16), 1, 0).reshape(2, -1, 3 * hc)
    proj_low = jnp.swapaxes(proj_weight[:, :, 0, 0].astype(bf16), 1, 2)
    shard = jnp.concatenate([qkv_low, proj_low], axis=2)
    stat_rows = (experts + 8) // 8 * 8
    ff = expert_down.shape[1]
    shares = jnp.concatenate(
        [jnp.transpose(expert_up[0], (1, 2, 0)).reshape(2 * ff, wide).astype(bf16), expert_down[0].astype(bf16)]
    ).reshape(3, ff, wide)
    vectors = bias_vectors(rel_bias, tokens)
    router_rows = jnp.pad(router.T, ((0, stat_rows - experts), (0, 0)))
    x_all, gains_all, weight, slot_rows, slot_columns, own_crossed, placed, placed_cot, *grad_rows = gather(
        layer_in, norm_gains, shard, placing, routes.T, cotangent, stat_rows, ext, experts, columns
    )
    weight = weight.reshape(D, 4 * hc)
    first, qkv, attended, lse, second, table, mixed, gates, came, crossed, share_came = attend(
        x_all, gains_all, weight, lengths, vectors, placed, norm_gains, router_rows, slot_rows, shares,
        grad_rows, columns,
    )
    home, y, y_far, keep_up, keep_down, away_up, away_down = expert_block(
        mixed, slot_rows, gates, shares, share_came, grad_rows[0], own_crossed, came, crossed, columns
    )
    layer_out, input_grad, grad_qkv, grad_proj, sums, came_up, came_down = tail(
        home, slot_columns, table, second, mixed, placed_cot, norm_gains,
        router_rows, qkv, lse, attended, first, weight, placing, lengths, vectors, placed, norm_gains,
        y, y_far, away_up, away_down, stat_rows, experts, columns,
    )
    grad_gains = jnp.stack([sums[0], sums[8]])
    grad_router = sums[16 : 16 + experts].T
    grad_bias = bias_gradient(sums[16 + stat_rows :].reshape(vectors.shape), head_count, tokens)
    grad_qkv = jnp.swapaxes(grad_qkv, 1, 2).reshape(qkv_weight.shape)
    grad_proj = jnp.swapaxes(grad_proj, 1, 2).reshape(proj_weight.shape)
    grad_up = jnp.transpose(keep_up.astype(f32) + came_up.astype(f32), (2, 0, 1))[None]
    grad_down = (keep_down.astype(f32) + came_down.astype(f32))[None]
    ups = adamw_step(expert_up, grad_up, up_first, up_second, 2.0 * D ** (-0.5))
    downs = adamw_step(expert_down, grad_down, down_first, down_second, 2.0 * (FF / 2) ** (-0.5))
    gains = adamw_step(norm_gains, grad_gains, gain_first, gain_second, 0.5)
    bias = adamw_step(rel_bias, grad_bias, bias_first, bias_second, 1.0)
    routers = adamw_step(router, grad_router, router_first, router_second, 2.0 * (2 * D) ** (-0.5))
    qkvs = adamw_step(qkv_weight, grad_qkv, qkv_first, qkv_second, 2.0 * D ** (-0.5))
    projs = adamw_step(proj_weight, grad_proj, proj_first, proj_second, 2.0 * (HEADS * HD / 8) ** (-0.5))
    out = (layer_out, input_grad) + gains + bias + routers
    for group in (qkvs, projs, ups, downs):
        out = out + group + (group[0].astype(bf16),)
    return out


def solution(mesh):
    shape = mesh.devices.shape
    fine = Mesh(
        mesh.devices.reshape((shape[0] // 2, 2) + shape[1:]), ("ex", "half", "row", "col")
    )
    dp, grid = ("ex", "half"), ("row", "col")
    tokens, own = P(dp, grid), P(dp, None)
    gain, router = P(None, grid), P(grid, None)
    qkv, proj = P("row", dp, None, None, None, "col"), P(None, "col", "row", dp, None)
    up, down = P(dp, "row", None, "col"), P(dp, "col", "row")
    in_specs = (
        (tokens, own, own, own, tokens) + (gain,) * 6 + (router,) * 3
        + (qkv,) * 3 + (proj,) * 3 + (up,) * 3 + (down,) * 3
    )
    out_specs = (
        (tokens, tokens) + (gain,) * 6 + (router,) * 3
        + (qkv,) * 4 + (proj,) * 4 + (up,) * 4 + (down,) * 4
    )
    return jax.shard_map(local, mesh=fine, in_specs=in_specs, out_specs=out_specs, check_vma=False)
```

```python
import functools

import jax
import jax.numpy as jnp
import numpy as np
from jax import lax
from jax.experimental import pallas as pl
from jax.experimental.pallas import tpu as pltpu
from jax.sharding import Mesh, PartitionSpec as P

D = 1024
HEADS = 16
FF = 2816
TOP = 2
STEP = 5
beta_first = 0.5
beta_second = 0.5
adam_epsilon = 1e-08
weight_decay = 0.01
highest = lax.Precision.HIGHEST
EXTRA = 16
HD = 64
BUCKETS = 32
LONGEST = 512
TILE = 256
norm_epsilon = 1e-06
hidden_score = -1e30
bucket_edges = np.floor(16.0 * 2.0 ** (np.arange(16) * 0.375)).astype(np.int32)
f32 = jnp.float32
bf16 = jnp.bfloat16
MIB = 1 << 20


def dot_nn(a, b):
    return lax.dot_general(a, b, (((1,), (0,)), ((), ())), preferred_element_type=f32)


def dot_nt(a, b):
    return lax.dot_general(a, b, (((1,), (1,)), ((), ())), preferred_element_type=f32)


def dot_tn(a, b):
    return lax.dot_general(a, b, (((0,), (0,)), ((), ())), preferred_element_type=f32)


def tile_reach(tokens):
    return min(tokens // TILE, (LONGEST - 1 + TILE - 1) // TILE + 1)


def toeplitz_places(tokens):
    reach = tile_reach(tokens)
    m = np.arange(2 * TILE)
    base = np.where(m < TILE, -m, 2 * TILE - m)
    distance = np.arange(reach)[:, None] * TILE + base[None, :]
    clipped = np.maximum(distance, 0)
    buckets = np.where(
        clipped < 16, clipped, 15 + (clipped[..., None] >= bucket_edges).sum(-1)
    )
    return (distance, buckets)


def bias_vectors(rel_bias, tokens):
    distance, buckets = toeplitz_places(tokens)
    table = jnp.asarray((buckets[..., None] == np.arange(BUCKETS)).astype(np.float32))
    values = jnp.einsum("dmb,bh->hdm", table, rel_bias, precision=lax.Precision.HIGHEST)
    values = jnp.where(jnp.asarray(distance < 0)[None], hidden_score, values)
    return values.reshape(-1, 2 * TILE)


def bias_gradient(vectors, head_count, tokens):
    distance, buckets = toeplitz_places(tokens)
    table = ((buckets[..., None] == np.arange(BUCKETS)) & (distance >= 0)[..., None]).astype(np.float32)
    return jnp.einsum(
        "dmb,hdm->bh",
        jnp.asarray(table),
        vectors.reshape(head_count, distance.shape[0], 2 * TILE),
        precision=lax.Precision.HIGHEST,
    )


def fill_bias(vector_ref, bias):
    for i in range(bias.shape[0]):
        wide = jnp.broadcast_to(vector_ref[i : i + 1, :], (TILE, 2 * TILE))
        bias[i] = pltpu.roll(wide, 0, 1, stride=1, stride_axis=0)[:, :TILE]


def head_lanes(shape, head):
    return lax.broadcasted_iota(jnp.int32, shape, 1) // HD == head


def given_table(place_row, tokens):
    return jnp.where(
        place_row[...] == lax.broadcasted_iota(jnp.int32, (tokens, tokens), 0), 1.0, 0.0
    ).astype(bf16)


def sequence_starts(length_ref, tokens):
    at = lax.broadcasted_iota(jnp.int32, (tokens, 1), 0)
    starts = jnp.zeros((tokens, 1), jnp.int32)
    end = 0
    for k in range(length_ref.shape[1]):
        end = end + length_ref[0, k]
        starts = jnp.where(at >= end, end, starts)
    return starts


def attention_forward_kernel(
    x_ref, gain_ref, weight_ref, length_ref, vector_ref,
    first_ref, qkv_ref, attended_ref, lse_ref, bias, between,
):
    quarters, tokens, part = x_ref.shape
    width = quarters * part
    hc = weight_ref.shape[1] // 4
    head_count = hc // HD
    reach = bias.shape[0] // head_count
    fill_bias(vector_ref, bias)
    squares = jnp.zeros((tokens, 1), f32)
    for q in range(quarters):
        v = x_ref[q].astype(f32)
        squares = squares + jnp.sum(v * v, axis=1, keepdims=True)
    inverse = lax.rsqrt(squares / width + norm_epsilon)
    total = jnp.zeros((tokens, 3 * hc), f32)
    for q in range(quarters):
        first = (x_ref[q].astype(f32) * inverse * gain_ref[q, :1]).astype(bf16)
        first_ref[q] = first
        total = total + dot_nn(first, weight_ref[q * part : (q + 1) * part, : 3 * hc])
    all_starts = sequence_starts(length_ref, tokens)
    scale = jnp.where(
        lax.broadcasted_iota(jnp.int32, (1, 3 * hc), 1) < hc, HD ** (-0.5), 1.0
    )
    qkv_ref[...] = (total * scale).astype(bf16)
    between(-1)
    for a in range(tokens // TILE):
        rows = slice(a * TILE, (a + 1) * TILE)
        blocks = range(max(0, a - reach + 1), a + 1)
        starts = all_starts[rows, :]
        visible = [
            b * TILE + lax.broadcasted_iota(jnp.int32, (TILE, TILE), 1) >= starts for b in blocks
        ]

        def one_head(head, carry):
            out, lse = carry
            mine = head_lanes((TILE, hc), head)
            query = jnp.where(mine, qkv_ref[rows, :hc], 0)
            scores = []
            for b, seen in zip(blocks, visible):
                s = dot_nt(query, qkv_ref[b * TILE : (b + 1) * TILE, hc : 2 * hc])
                scores.append(jnp.where(seen, s + bias[head * reach + a - b], hidden_score))
            top = functools.reduce(jnp.maximum, [jnp.max(s, axis=1, keepdims=True) for s in scores])
            exps = [jnp.exp(s - top) for s in scores]
            denominator = functools.reduce(jnp.add, [jnp.sum(e, axis=1, keepdims=True) for e in exps])
            share = 1.0 / denominator
            value = jnp.zeros((TILE, hc), f32)
            for b, e in zip(blocks, exps):
                value = value + dot_nn(
                    (e * share).astype(bf16), qkv_ref[b * TILE : (b + 1) * TILE, 2 * hc :]
                )
            lane = lax.broadcasted_iota(jnp.int32, (TILE, 128), 1)
            return (
                jnp.where(mine, value, out),
                jnp.where(lane == head, top + jnp.log(denominator), lse),
            )

        out, lse = lax.fori_loop(
            0, head_count, one_head, (jnp.zeros((TILE, hc), f32), jnp.zeros((TILE, 128), f32))
        )
        attended_ref[rows, :] = out.astype(bf16)
        lane = lax.broadcasted_iota(jnp.int32, (TILE, 128), 1)
        lse_ref[rows, :] = jnp.where(lane == 127, inverse[rows], lse)
        between(a)


def microseconds(time):
    return pl.CostEstimate(flops=0, bytes_accessed=int(time * 3.5e6), transcendentals=0)


def vmem():
    return pl.BlockSpec(memory_space=pltpu.VMEM)


def hbm():
    return pl.BlockSpec(memory_space=pltpu.HBM)


def attention_backward_kernel(
    branch_ref, qkv_ref, lse_ref, attended_ref, first_ref, weight_ref, length_ref, vector_ref,
    dfirst_ref, dweight_ref, dvector_ref,
    bias, dbias, grad_ref, dqkv, dkv, before, after,
):
    quarters, tokens, part = branch_ref.shape
    hc = weight_ref.shape[1] // 4
    head_count = hc // HD
    reach = bias.shape[0] // head_count
    fill_bias(vector_ref, bias)
    dbias[...] = jnp.zeros_like(dbias)
    dkv[...] = jnp.zeros_like(dkv)
    all_starts = sequence_starts(length_ref, tokens)
    for a in reversed(range(tokens // TILE)):
        rows = slice(a * TILE, (a + 1) * TILE)
        blocks = range(max(0, a - reach + 1), a + 1)
        starts = all_starts[rows, :]
        visible = [
            b * TILE + lax.broadcasted_iota(jnp.int32, (TILE, TILE), 1) >= starts for b in blocks
        ]
        before(a)
        total = jnp.zeros((TILE, hc), f32)
        for q in range(quarters):
            total = total + dot_nn(branch_ref[q, rows], weight_ref[q * part : (q + 1) * part, 3 * hc :])
        grad_ref[rows, :] = total.astype(bf16)

        def one_head(head, dquery):
            mine = head_lanes((TILE, hc), head)
            query = jnp.where(mine, qkv_ref[rows, :hc], 0)
            grad = jnp.where(mine, grad_ref[rows, :], 0)
            lane = lax.broadcasted_iota(jnp.int32, (TILE, 128), 1)
            lse = jnp.sum(jnp.where(lane == head, lse_ref[rows, :], 0.0), axis=1, keepdims=True)
            probs, dprobs = [], []
            inner = jnp.zeros((TILE, 1), f32)
            for b, seen in zip(blocks, visible):
                keys = slice(b * TILE, (b + 1) * TILE)
                s = dot_nt(query, qkv_ref[keys, hc : 2 * hc]) + bias[head * reach + a - b]
                p = jnp.where(seen, jnp.exp(s - lse), 0.0)
                d = dot_nt(grad, qkv_ref[keys, 2 * hc :])
                inner = inner + jnp.sum(p * d, axis=1, keepdims=True)
                probs.append(p)
                dprobs.append(d)
            for b, p, d in zip(blocks, probs, dprobs):
                keys = slice(b * TILE, (b + 1) * TILE)
                ds = p * (d - inner)
                place = head * reach + a - b
                dbias[place] = dbias[place] + ds
                low = ds.astype(bf16)
                dquery = dquery + dot_nn(low, jnp.where(mine, qkv_ref[keys, hc : 2 * hc], 0))
                dkv[keys, :hc] = dkv[keys, :hc] + dot_tn(low, query)
                dkv[keys, hc:] = dkv[keys, hc:] + dot_tn(p.astype(bf16), grad)
            return dquery

        dquery = lax.fori_loop(0, head_count, one_head, jnp.zeros((TILE, hc), f32))
        dqkv[rows, :hc] = (dquery * HD ** (-0.5)).astype(bf16)
        dqkv[rows, hc:] = dkv[rows, :].astype(bf16)
        for q in range(quarters):
            dfirst_ref[q, rows] = dot_nt(
                dqkv[rows, :], weight_ref[q * part : (q + 1) * part, : 3 * hc]
            ).astype(bf16)
        after(a)
    for q in range(quarters):
        dims = slice(q * part, (q + 1) * part)
        dweight_ref[dims, : 3 * hc] = dot_tn(first_ref[q], dqkv[...]).astype(bf16)
        dweight_ref[dims, 3 * hc :] = dot_tn(branch_ref[q], attended_ref[...]).astype(bf16)


def bias_sums(dbias, dvector_ref):
    for i in range(dbias.shape[0]):
        wide = jnp.concatenate([dbias[i], jnp.zeros((TILE, TILE), f32)], axis=1)
        level = wide[:8]
        for g in range(8, TILE, 8):
            level = level + pltpu.roll(wide[g : g + 8], 2 * TILE - g, 1)
        row = level[:1]
        for s in range(1, 8):
            row = row + pltpu.roll(level[s : s + 1], 2 * TILE - s, 1)
        dvector_ref[i : i + 1, :] = row


def half_places(rows, part):
    row = lax.broadcasted_iota(jnp.int32, (rows, EXTRA), 0) // part
    high = lax.broadcasted_iota(jnp.int32, (rows, EXTRA), 1)
    column = lax.broadcasted_iota(jnp.int32, (rows, part), 0) % part
    return (row, high, column == lax.broadcasted_iota(jnp.int32, (rows, part), 1))


def write_extra(values, part):
    row, high, column = half_places(values.shape[0], part)
    near = values.astype(bf16)
    left = (values - near.astype(f32)).astype(bf16)
    near_rows = jnp.where(row == high, 1.0, 0.0).astype(bf16)
    left_rows = jnp.where(row + 8 == high, 1.0, 0.0).astype(bf16)
    near_values = jnp.where(column, near.astype(f32), 0.0).astype(bf16)
    left_values = jnp.where(column, left.astype(f32), 0.0).astype(bf16)
    return dot_tn(near_rows, near_values) + dot_tn(left_rows, left_values)


def read_extra(extra, rows):
    part = extra.shape[1]
    row, high, column = half_places(rows, part)
    pick = jnp.where(row == high % 8, 1.0, 0.0).astype(bf16)
    return jnp.sum(jnp.where(column, dot_nn(pick, extra), 0.0), axis=1, keepdims=True)


GELU_A = 0.7978845608028654
GELU_B = 0.044715


MESH = pl.DeviceIdType.MESH


def remote(src, dst, send, recv, where):
    return pltpu.make_async_remote_copy(
        src_ref=src, dst_ref=dst, send_sem=send, recv_sem=recv, device_id=where, device_id_type=MESH
    )


def greet(wheres):
    barrier = pltpu.get_barrier_semaphore()
    for where in wheres:
        pl.semaphore_signal(barrier, inc=1, device_id=where, device_id_type=MESH)
    pl.semaphore_wait(barrier, len(wheres))


def dot_exact(a, b, dims):
    return lax.dot_general(a, b, ((dims, ((), ()))), precision=highest, preferred_element_type=f32)


def grid_peers(columns):
    row, col = lax.axis_index("row"), lax.axis_index("col")
    return [
        {"row": (row + i) % 2, "col": (col + j) % columns}
        for i in range(2)
        for j in range(columns)
        if i + j > 0
    ]


def sum_of_peers(mine, got, send, recv, columns):
    copies = [
        remote(mine, got.at[i], send.at[i], recv.at[i], where)
        for i, where in enumerate(grid_peers(columns))
    ]
    for copy in copies:
        copy.start()
    for copy in copies:
        copy.wait_recv()
    total = mine[...]
    for i in range(len(copies)):
        total = total + got[i]
    for copy in copies:
        copy.wait_send()
    return total


PIECES = 4


def project_part(
    columns, experts,
    attended_ref, weight_ref, layer_ref, gain_ref, router_ref, slot_ref,
    second_ref, mixed_ref, gate_ref, column_ref,
    core_out, core_in, keep, col_out, col_in, stat, stat_in,
    core_send, core_recv, col_send, col_recv, stat_send, stat_recv,
):
    row, col = lax.axis_index("row"), lax.axis_index("col")
    tokens, part = layer_ref.shape
    wide = columns * part
    size = tokens // PIECES
    heads = slice(3 * weight_ref.shape[1] // 4, weight_ref.shape[1])
    own_rows = pl.ds(pl.multiple_of(row * wide, wide), wide)
    other_rows = pl.ds(pl.multiple_of((1 - row) * wide, wide), wide)
    own_columns = pl.ds(pl.multiple_of(col * part, part), part)

    def core_copy(i):
        return remote(core_out.at[i], core_in.at[i], core_send.at[i], core_recv.at[i], {"row": 1 - row})

    def col_copy(i, k):
        return remote(
            col_out.at[i, k - 1], col_in.at[i, k - 1], col_send.at[i, k - 1], col_recv.at[i, k - 1],
            {"col": (col + k) % columns},
        )

    def multiply(i):
        at = slice(i * size, (i + 1) * size)
        core_out[i] = dot_nt(attended_ref[at, :], weight_ref[other_rows, heads]).astype(bf16)
        core_copy(i).start()
        keep[i] = dot_nt(attended_ref[at, :], weight_ref[own_rows, heads])

    def cross(i):
        core_copy(i).wait_recv()
        keep[i] = keep[i] + core_in[i].astype(f32)
        for k in range(1, columns):
            to = (col + k) % columns
            col_out[i, k - 1] = keep[i, :, pl.ds(pl.multiple_of(to * part, part), part)].astype(bf16)
            col_copy(i, k).start()

    def rest():
        ones = jnp.where(lax.broadcasted_iota(jnp.int32, router_ref.shape, 0) == experts, 1.0, 0.0)
        scaled_router = router_ref[...] * gain_ref[1:2]
        for i in range(PIECES):
            at = slice(i * size, (i + 1) * size)
            total = layer_ref[at, :].astype(f32) + keep[i, :, own_columns]
            for k in range(1, columns):
                col_copy(i, k).wait_recv()
                total = total + col_in[i, k - 1].astype(f32)
            second_ref[at, :] = total
            stat[:, at] = dot_exact(scaled_router, total, ((1,), (1,))) + dot_exact(
                ones, total * total, ((1,), (1,))
            )
        total = sum_of_peers(stat, stat_in, stat_send, stat_recv, columns)
        inverse = lax.rsqrt(total[experts : experts + 1] / D + norm_epsilon)
        routed = slot_ref[...] >= 0
        logits = jnp.where(routed, total * inverse, hidden_score)
        shares = jnp.where(routed, jnp.exp(logits - jnp.max(logits, axis=0, keepdims=True)), 0.0)
        gates = shares / jnp.sum(shares, axis=0, keepdims=True)
        gate_ref[...] = gates
        number = lax.broadcasted_iota(jnp.int32, gates.shape, 0)
        lanes = (gates.shape[0], 128)
        eye = jnp.where(
            lax.broadcasted_iota(jnp.int32, lanes, 0) == lax.broadcasted_iota(jnp.int32, lanes, 1), 1.0, 0.0
        )
        table = dot_exact(jnp.where(number == experts, inverse, gates), eye, ((0,), (0,)))
        column_ref[...] = table
        mixed_ref[...] = (second_ref[...] * table[:, experts : experts + 1] * gain_ref[1:2]).astype(bf16)
        for i in range(PIECES):
            core_copy(i).wait_send()
            for k in range(1, columns):
                col_copy(i, k).wait_send()

    return multiply, cross, rest


def nearest_first(experts):
    return sorted(range(1, experts), key=lambda s: min(s, experts - s))


def farthest_first(experts):
    far = experts // 2
    return [far] + [s for s in range(1, experts) if s != far]


def attend_kernel(columns, experts, *refs):
    x_hbm, gains_ref, weight_hbm, length_ref, vector_ref, layer_ref, gain_ref, router_ref, slot_ref, shares = refs[:10]
    grad_rows = refs[10 : 10 + experts]
    (
        first_hbm, qkv_hbm, attended_hbm, lse_hbm, second_hbm, column_hbm, mixed_ref, gate_ref, came, crossed, share_out,
        first_ref, qkv_ref, attended_ref, lse_ref, second_ref, column_ref,
        bias, core_out, core_in, keep, col_out, col_in, stat, stat_in,
        core_send, core_recv, col_send, col_recv, stat_send, stat_recv,
        z_send, z_recv, x_send, x_recv, store, x_ref, weight_ref, load, share_send, share_recv,
    ) = refs[10 + experts :]
    loads = [
        pltpu.make_async_copy(x_hbm, x_ref, load.at[0]),
        pltpu.make_async_copy(weight_hbm, weight_ref, load.at[1]),
    ]
    for copy in loads:
        copy.start()
    ex, col = lax.axis_index("ex"), lax.axis_index("col")
    greet(
        grid_peers(columns)
        + [{"ex": (ex + s) % experts} for s in range(1, experts)]
        + [{"half": 1 - lax.axis_index("half")}]
    )
    share = remote(
        shares, share_out, share_send.at[0], share_recv.at[0], {"half": 1 - lax.axis_index("half")}
    )
    share.start()

    def z_copy(s):
        return remote(grad_rows[s], came.at[s], z_send.at[s], z_recv.at[s], {"ex": (ex + s) % experts})

    def x_copy(s, k):
        return remote(
            came.at[s], crossed.at[s, k - 1], x_send.at[s, k - 1], x_recv.at[s, k - 1], {"col": (col + k) % columns}
        )

    far, *near = farthest_first(experts)
    for s in near + [far]:
        z_copy(s).start()
    for copy in loads:
        copy.wait()

    def go_on(s):
        z_copy(s).wait_recv()
        for k in range(1, columns):
            x_copy(s, k).start()

    multiply, cross, rest = project_part(
        columns, experts,
        attended_ref, weight_ref, layer_ref, gain_ref, router_ref, slot_ref,
        second_ref, mixed_ref, gate_ref, column_ref,
        core_out, core_in, keep, col_out, col_in, stat, stat_in,
        core_send, core_recv, col_send, col_recv, stat_send, stat_recv,
    )

    def between(a):
        if a >= 0:
            multiply(a)
        if a > 0:
            cross(a - 1)
        if a == 2:
            for s in near[:-1]:
                go_on(s)

    attention_forward_kernel(
        x_ref, gains_ref, weight_ref, length_ref, vector_ref,
        first_ref, qkv_ref, attended_ref, lse_ref, bias, between,
    )
    cross(PIECES - 1)

    def stored(pairs, first):
        copies = [pltpu.make_async_copy(a, b, store.at[first + i]) for i, (a, b) in enumerate(pairs)]
        for copy in copies:
            copy.start()
        return copies

    stores = stored(
        [(first_ref, first_hbm), (qkv_ref, qkv_hbm), (attended_ref, attended_hbm), (lse_ref, lse_hbm)], 0
    )

    go_on(far)
    rest()
    stores = stores + stored([(second_ref, second_hbm), (column_ref, column_hbm)], 4)
    z_copy(near[-1]).wait_recv()
    for copy in stores:
        copy.wait()
    share.wait()
    for s in [far] + near[:-1]:
        for k in range(1, columns):
            x_copy(s, k).wait()
    for s in near + [far]:
        z_copy(s).wait_send()


def attend(x, gains, weight, lengths, vectors, layer_in, gain, router_rows, slots, shares, grad_rows, columns):
    quarters, tokens, part = x.shape
    experts = len(grad_rows)
    ext = grad_rows[0].shape[0]
    hc = weight.shape[1] // 4
    size = tokens // PIECES
    rows = router_rows.shape[0]
    dma = pltpu.SemaphoreType.DMA
    others = columns - 1
    kept = (
        jax.ShapeDtypeStruct(x.shape, bf16),
        jax.ShapeDtypeStruct((tokens, 3 * hc), bf16),
        jax.ShapeDtypeStruct((tokens, hc), bf16),
        jax.ShapeDtypeStruct((tokens, 128), f32),
        jax.ShapeDtypeStruct((tokens, part), f32),
        jax.ShapeDtypeStruct((tokens, 128), f32),
    )
    return pl.pallas_call(
        functools.partial(attend_kernel, columns, experts),
        out_shape=kept
        + (
            jax.ShapeDtypeStruct((tokens, part), bf16),
            jax.ShapeDtypeStruct((rows, tokens), f32),
            jax.ShapeDtypeStruct((experts, ext, part), bf16),
            jax.ShapeDtypeStruct((experts, others, ext, part), bf16),
            jax.ShapeDtypeStruct(shares.shape, bf16),
        ),
        in_specs=[hbm(), vmem(), hbm(), pl.BlockSpec(memory_space=pltpu.SMEM)]
        + [vmem()] * 5
        + [hbm()] * (1 + experts),
        out_specs=(hbm(),) * 6 + (vmem(),) * 2 + (hbm(),) * 3,
        scratch_shapes=[pltpu.VMEM(each.shape, each.dtype) for each in kept]
        + [
            pltpu.VMEM((vectors.shape[0], TILE, TILE), f32),
            pltpu.VMEM((PIECES, size, columns * part), bf16),
            pltpu.VMEM((PIECES, size, columns * part), bf16),
            pltpu.VMEM((PIECES, size, columns * part), f32),
            pltpu.VMEM((PIECES, others, size, part), bf16),
            pltpu.VMEM((PIECES, others, size, part), bf16),
            pltpu.VMEM((rows, tokens), f32),
            pltpu.VMEM((quarters - 1, rows, tokens), f32),
            dma((PIECES,)), dma((PIECES,)), dma((PIECES, others)), dma((PIECES, others)),
            dma((quarters - 1,)), dma((quarters - 1,)),
            dma((experts,)), dma((experts,)), dma((experts, others)), dma((experts, others)), dma((6,)),
            pltpu.VMEM(x.shape, bf16), pltpu.VMEM(weight.shape, bf16), dma((2,)), dma((1,)), dma((1,)),
        ],
        compiler_params=pltpu.CompilerParams(
            collective_id=1, has_side_effects=True, vmem_limit_bytes=52 * MIB
        ),
        cost_estimate=microseconds(45),
        name="attend",
    )(x, gains, weight, lengths, vectors, layer_in, gain, router_rows, slots, shares, *grad_rows)


def gather_kernel(columns, experts, *refs):
    layer_ref, gain_ref, shard_ref, place_row, route_ref, cotangent_ref = refs[:6]
    x_ref, gains_ref, weight_ref, slot_row_ref, slot_column_ref, crossed_ref, placed_ref, placed_cot = refs[6:14]
    slot_grads = refs[14 : 14 + experts]
    (
        x_send, x_recv, own_send, own_recv, pass_send, pass_recv, gain_send, gain_recv,
        swap_send, swap_recv, z_send, z_recv, y_send, y_recv, place, cross_send, cross_recv,
        stay, slots, slot_store,
    ) = refs[14 + experts :]
    ex, half = lax.axis_index("ex"), lax.axis_index("half")
    row, col = lax.axis_index("row"), lax.axis_index("col")
    mine = row * columns + col
    tokens, part = layer_ref.shape
    greet(
        grid_peers(columns)
        + [{"ex": (ex + s) % experts} for s in range(1, experts)]
        + [{"half": 1 - half}]
    )
    spread = Spread(
        x_ref, placed_ref, columns, x_send, x_recv, own_send, own_recv, pass_send, pass_recv, stay
    )
    member = 2 * ex + half
    swap = remote(
        shard_ref.at[1 - row], weight_ref.at[row, member], swap_send.at[0], swap_recv.at[0], {"row": 1 - row}
    )
    swap.start()
    arrived = remote(
        shard_ref.at[1 - row], weight_ref.at[1 - row, member], swap_send.at[0], swap_recv.at[0], {"row": 1 - row}
    )
    place_shard = pltpu.make_async_copy(shard_ref.at[row], weight_ref.at[row, member], place.at[0])
    place_shard.start()

    def z_copy(s, a):
        block = weight_ref.at[a, member]
        return remote(block, block, z_send.at[s, a], z_recv.at[s, a], {"ex": (ex + s) % experts})

    def z_arrival(s, a):
        block = weight_ref.at[a, 2 * ((ex - s + experts) % experts) + half]
        return remote(block, block, z_send.at[s, a], z_recv.at[s, a], {"ex": (ex + s) % experts})

    def y_copy(s, a):
        block = weight_ref.at[a, 2 * ((ex - s + experts) % experts) + half]
        return remote(block, block, y_send.at[s, a], y_recv.at[s, a], {"half": 1 - half})

    def y_arrival(s, a):
        block = weight_ref.at[a, 2 * ((ex - s + experts) % experts) + 1 - half]
        return remote(block, block, y_send.at[s, a], y_recv.at[s, a], {"half": 1 - half})

    queue = [(s, a) for s in nearest_first(experts) for a in (row, 1 - row)]
    place_shard.wait()
    z_copy(*queue[0]).start()
    y_copy(0, row).start()
    arrived.wait_recv()
    z_copy(*queue[1]).start()
    y_copy(0, 1 - row).start()
    to_given = given_table(place_row, tokens)
    placed_ref[...] = dot_tn(to_given, layer_ref[...]).astype(bf16)
    spread.start()
    gains_ref[mine] = gain_ref[...]
    gain_copies = [
        remote(gain_ref, gains_ref.at[mine], gain_send.at[i], gain_recv.at[i], where)
        for i, where in enumerate(grid_peers(columns))
    ]
    for copy in gain_copies:
        copy.start()

    number = lax.broadcasted_iota(jnp.int32, (128, tokens), 0)
    hits = jnp.where((route_ref[:1] == number) | (route_ref[1:] == number), 1.0, 0.0)
    low_hits = hits.astype(bf16)
    first_at = lax.broadcasted_iota(jnp.int32, (tokens, tokens), 0)
    second_at = lax.broadcasted_iota(jnp.int32, (tokens, tokens), 1)

    def slot_tables():
        from_on = jnp.where(first_at <= second_at, 1.0, 0.0).astype(bf16)
        table = jnp.where(hits > 0.5, dot_nn(low_hits, from_on) - 1.0, -1.0)
        slot_row_ref[...] = table[: slot_row_ref.shape[0]]
        slot_column_ref[...] = table.T

    def place_cotangent():
        placed_cot[...] = dot_tn(to_given, cotangent_ref[...]).astype(bf16)

    def cotangent_slots(s):
        e = (ex + s) % experts
        ext = slot_grads[s].shape[0]
        hit = slot_row_ref[pl.ds(e, 1), :] == lax.broadcasted_iota(jnp.int32, (ext, tokens), 0).astype(f32)
        slots[s] = dot_nn(jnp.where(hit, 1.0, 0.0).astype(bf16), placed_cot[...]).astype(bf16)
        pltpu.make_async_copy(slots.at[s], slot_grads[s], slot_store.at[s]).start()

    crossing = [
        remote(
            slots.at[0], crossed_ref.at[k - 1], cross_send.at[k - 1], cross_recv.at[k - 1],
            {"col": (col + k) % columns},
        )
        for k in range(1, columns)
    ]
    def first_slots():
        cotangent_slots(0)
        for copy in crossing:
            copy.start()

    jobs = [place_cotangent, slot_tables, first_slots] + [functools.partial(cotangent_slots, s) for s in range(1, experts)]
    jobs.pop(0)()
    for i, (s, a) in enumerate(queue):
        z_copy(s, a).wait_send()
        if i + 2 < len(queue):
            z_copy(*queue[i + 2]).start()
        z_arrival(s, a).wait_recv()
        y_copy(s, a).start()
        if i < PIECES:
            spread.hand_on_piece(i)
        if jobs:
            jobs.pop(0)()
    while jobs:
        jobs.pop(0)()
    spread.finish()
    for copy in gain_copies + crossing:
        copy.wait()
    for s in range(experts):
        pltpu.make_async_copy(slots.at[s], slot_grads[s], slot_store.at[s]).wait()
    swap.wait_send()
    for s in range(experts):
        for a in range(2):
            y_arrival(s, a).wait_recv()
            y_copy(s, a).wait_send()


class Spread:
    def __init__(
        self, out, source, columns, x_send, x_recv, own_send, own_recv, pass_send, pass_recv, stay=None
    ):
        self.stay = stay
        row, col = lax.axis_index("row"), lax.axis_index("col")
        mine = row * columns + col
        size = source.shape[0] // PIECES
        self.out, self.source, self.mine = out, source, mine
        self.across, self.own, self.passed = [], [], []
        for i in range(PIECES):
            at = pl.ds(i * size, size)
            for k in range(1, columns):
                self.across.append(
                    remote(
                        source.at[at], out.at[mine, at], x_send.at[i, k - 1], x_recv.at[i, k - 1],
                        {"col": (col + k) % columns},
                    )
                )
                block = out.at[row * columns + (col - k + columns) % columns, at]
                self.passed.append(
                    remote(block, block, pass_send.at[i, k - 1], pass_recv.at[i, k - 1], {"row": 1 - row})
                )
            self.own.append(
                remote(source.at[at], out.at[mine, at], own_send.at[i], own_recv.at[i], {"row": 1 - row})
            )

    def start(self):
        for i in range(PIECES):
            self.start_piece(i)

    def start_piece(self, i):
        others = len(self.across) // PIECES
        for copy in self.across[i * others : (i + 1) * others] + [self.own[i]]:
            copy.start()
        size = self.source.shape[0] // PIECES
        at = pl.ds(i * size, size)
        if self.stay is None:
            self.out[self.mine, at] = self.source[at]
        else:
            pltpu.make_async_copy(self.source.at[at], self.out.at[self.mine, at], self.stay.at[i]).start()

    def hand_on_piece(self, i):
        others = len(self.across) // PIECES
        for n in range(i * others, (i + 1) * others):
            self.across[n].wait_recv()
            self.passed[n].start()

    def wait_piece(self, i):
        others = len(self.across) // PIECES
        for copy in self.passed[i * others : (i + 1) * others] + [self.own[i]]:
            copy.wait_recv()

    def wait_sends(self):
        for copy in self.across + self.own + self.passed:
            copy.wait_send()

    def finish(self):
        if self.stay is not None:
            size = self.source.shape[0] // PIECES
            for i in range(PIECES):
                at = pl.ds(i * size, size)
                pltpu.make_async_copy(self.source.at[at], self.out.at[self.mine, at], self.stay.at[i]).wait()
        for i in range(PIECES):
            self.wait_piece(i)
        self.wait_sends()


def spread_semaphores(columns):
    dma = pltpu.SemaphoreType.DMA
    return [dma((PIECES, columns - 1))] * 2 + [dma((PIECES,))] * 2 + [dma((PIECES, columns - 1))] * 2


def gather(layer_in, gains, shard, place_row, routes, cotangent, stat_rows, ext, experts, columns):
    tokens, part = layer_in.shape
    _, rows, width = shard.shape
    quarters = 2 * columns
    dma = pltpu.SemaphoreType.DMA
    return pl.pallas_call(
        functools.partial(gather_kernel, columns, experts),
        out_shape=(
            jax.ShapeDtypeStruct((quarters, tokens, part), bf16),
            jax.ShapeDtypeStruct((quarters,) + gains.shape, f32),
            jax.ShapeDtypeStruct((2, 2 * experts, rows, width), bf16),
            jax.ShapeDtypeStruct((stat_rows, tokens), f32),
            jax.ShapeDtypeStruct((tokens, 128), f32),
            jax.ShapeDtypeStruct((columns - 1, ext, part), bf16),
            jax.ShapeDtypeStruct((tokens, part), bf16),
            jax.ShapeDtypeStruct((tokens, part), bf16),
        )
        + (jax.ShapeDtypeStruct((ext, part), bf16),) * experts,
        in_specs=[vmem()] * 6,
        out_specs=(hbm(), vmem(), hbm(), vmem(), vmem(), hbm(), vmem(), vmem()) + (hbm(),) * experts,
        scratch_shapes=spread_semaphores(columns)
        + [
            dma((quarters - 1,)), dma((quarters - 1,)), dma((1,)), dma((1,)),
            dma((experts, 2)), dma((experts, 2)), dma((experts, 2)), dma((experts, 2)), dma((1,)),
            dma((columns - 1,)), dma((columns - 1,)), dma((PIECES,)),
            pltpu.VMEM((experts, ext, part), bf16), dma((experts,)),
        ],
        compiler_params=pltpu.CompilerParams(
            collective_id=0, has_side_effects=True, vmem_limit_bytes=52 * MIB
        ),
        cost_estimate=microseconds(30),
        name="gather",
    )(layer_in, gains, shard, place_row, routes, cotangent)


def expert_kernel(
    columns, experts,
    *refs,
):
    mixed_ref, slot_ref, gate_ref, shares, share_came, own_grads, own_crossed, came, crossed = refs[:9]
    (
        home_ref, y_hbm, y_far, keep_up, keep_down, away_up, away_down,
        x, xs, grads, weight, da, db, scaled, core_out, core_in, keep, col_out, col_in,
        load, grad_load, grad_send, grad_recv, z_send, z_recv, own_send, own_recv, col_send, col_recv, pass_send, pass_recv,
        core_send, core_recv, back_send, back_recv, home_send, home_recv, y_send, y_recv, y_sem, store, far_send, far_recv,
        free, last_send, last_recv, on_send, on_recv, y_far_send, y_far_recv,
        hand_send, hand_recv,
    ) = refs[9:]
    ex, half = lax.axis_index("ex"), lax.axis_index("half")
    row, col = lax.axis_index("row"), lax.axis_index("col")
    tokens, part = mixed_ref.shape
    ext = x.shape[2]
    cap = ext - EXTRA
    quarters = 2 * columns
    wide = columns * part
    mine = row * columns + col
    last = experts - 1
    greet(
        [{"ex": (ex + s) % experts} for s in range(1, experts)]
        + [{"col": (col + k) % columns} for k in range(1, columns)]
        + [{"row": 1 - row}]
    )

    own_dims = pl.ds(pl.multiple_of(row * wide, wide), wide)
    other_dims = pl.ds(pl.multiple_of((1 - row) * wide, wide), wide)
    at_home = row == half
    loads, handed = [], []

    def to_row(source, place, i, stays):
        here = pltpu.make_async_copy(source, place, load.at[i])
        there = remote(source, place, hand_send.at[i], hand_recv.at[i], {"row": 1 - row})

        def start():
            pl.when(stays)(here.start)
            pl.when(jnp.logical_not(stays))(there.start)

        def wait():
            pl.when(stays)(here.wait)
            pl.when(jnp.logical_not(stays))(there.wait_send)

        def arrive():
            pl.when(stays)(there.wait_recv)

        return start, wait, arrive

    own_start, own_wait, own_arrive = to_row(shares, weight.at[:, :, own_dims], 0, at_home)
    came_start, came_wait, came_arrive = to_row(
        share_came, weight.at[:, :, own_dims], 1, jnp.logical_not(at_home)
    )
    own_start()
    came_start()
    final_chunk = farthest_first(experts)[-1]
    for s in range(experts):
        for k in range(columns):
            if k and s == final_chunk:
                continue
            at = (s, k)
            place = row * columns + (col - k + columns) % columns
            if s == 0:
                block = own_crossed.at[k - 1] if k else own_grads
            else:
                block = crossed.at[s, k - 1] if k else came.at[s]
            loads.append(pltpu.make_async_copy(block, grads.at[place, s], grad_load.at[at]))
            handed.append(
                remote(block, grads.at[place, s], grad_send.at[at], grad_recv.at[at], {"row": 1 - row})
            )
    for copy in loads + handed:
        copy.start()

    def last_copy(k):
        return remote(
            came.at[final_chunk], grads.at[mine, final_chunk], last_send.at[k - 1], last_recv.at[k - 1],
            {"col": (col + k) % columns},
        )

    def last_on(k):
        block = grads.at[row * columns + (col - k + columns) % columns, final_chunk]
        return remote(block, block, on_send.at[k - 1], on_recv.at[k - 1], {"row": 1 - row})

    def z_copy(s):
        return remote(
            xs.at[s], x.at[mine, s], z_send.at[s], z_recv.at[s], {"ex": (ex + s) % experts}
        )

    def own_copy(s):
        block = x.at[mine, s]
        return remote(block, block, own_send.at[s], own_recv.at[s], {"row": 1 - row})

    def col_copy(s, k):
        block = x.at[mine, s]
        return remote(
            block, block, col_send.at[s, k - 1], col_recv.at[s, k - 1], {"col": (col + k) % columns}
        )

    def pass_copy(s, k):
        block = x.at[row * columns + (col - k + columns) % columns, s]
        return remote(
            block, block, pass_send.at[s, k - 1], pass_recv.at[s, k - 1], {"row": 1 - row}
        )

    def spread(s):
        own_copy(s).start()
        for k in range(1, columns):
            col_copy(s, k).start()

    def hand_on(s):
        for k in range(1, columns):
            col_copy(s, k).wait_recv()
            pass_copy(s, k).start()

    def slots_of(e):
        hit = slot_ref[pl.ds(e, 1), :] == lax.broadcasted_iota(jnp.int32, (cap, tokens), 0).astype(f32)
        values = dot_nn(jnp.where(hit, 1.0, 0.0).astype(bf16), mixed_ref[...]).astype(bf16)
        gate = jnp.sum(jnp.where(hit, gate_ref[pl.ds(e, 1), :], 0.0), axis=1, keepdims=True)
        return values, write_extra(gate, part).astype(bf16)

    def build(s):
        values, extra = slots_of((ex + s) % experts)
        xs[s, :cap] = values
        xs[s, cap:] = extra

    def nth(p):
        far = experts // 2
        return jnp.where(p == 1, far, jnp.where((p > 1) & (p <= far), p - 1, p))

    build(nth(1))
    z_copy(nth(1)).start()
    values, extra = slots_of(ex)
    x[mine, 0, :cap] = values
    x[mine, 0, cap:] = extra
    spread(0)
    for k in range(1, columns):
        last_copy(k).start()

    @pl.loop(2, experts)
    def _(p):
        build(nth(p))

    for copy in loads:
        copy.wait()
    for copy in handed:
        copy.wait()
    hand_on(0)
    z_copy(nth(1)).wait_send()
    z_copy(nth(2)).start()
    z_copy(nth(1)).wait_recv()
    spread(nth(1))
    for wait in (own_wait, own_arrive, came_wait, came_arrive):
        wait()

    def core_copy(s):
        return remote(core_out.at[s], core_in.at[s], core_send.at[s], core_recv.at[s], {"row": 1 - row})

    def back_copy(s, k):
        return remote(
            col_out.at[s, k - 1], col_in.at[s, k - 1], back_send.at[s, k - 1], back_recv.at[s, k - 1],
            {"col": (col + k) % columns},
        )

    def home_copy(s):
        return remote(
            xs.at[s], home_ref.at[s], home_send.at[s], home_recv.at[s], {"ex": (ex - s + experts) % experts}
        )

    def stores(ups, downs):
        parts = [(weight.at[:2], ups, 0), (weight.at[2], downs, 1)]
        return [
            (
                pltpu.make_async_copy(source.at[(slice(None),) * (2 - i) + (own_dims,)], out, store.at[i]),
                remote(
                    source.at[(slice(None),) * (2 - i) + (other_dims,)], out, far_send.at[i], far_recv.at[i],
                    {"row": 1 - row},
                ),
            )
            for source, out, i in parts
        ]

    def store_gradients(i):
        for mine_here, (ups, downs) in ((True, (keep_up, keep_down)), (False, (away_up, away_down))):

            @pl.when((row == half) == mine_here)
            def _():
                for copy in stores(ups, downs)[i]:
                    copy.start()

    def wait_gradients(i):
        for copy in stores(keep_up, keep_down)[i]:
            copy.wait()

    def y_share(s):
        return remote(core_out.at[s], core_in.at[s], y_send.at[s], y_recv.at[s], {"row": 1 - row})

    def y_copy(s):
        return pltpu.make_async_copy(core_in.at[s], y_hbm.at[:, s], y_sem.at[s])

    def after_core(s, slot):
        core_copy(s).wait_recv()
        keep[slot] = keep[slot] + core_in[s].astype(f32)
        for k in range(1, columns):
            to = (col + k) % columns
            col_out[s, k - 1] = keep[slot, to].astype(bf16)
            back_copy(s, k).start()

    def after_columns(s, slot):
        total = keep[slot, col]
        for k in range(1, columns):
            back_copy(s, k).wait_recv()
            total = total + col_in[s, k - 1].astype(f32)
        return total.astype(bf16)

    def send_home(s, slot):
        xs[s] = after_columns(s, slot)
        home_copy(s).start()

    @pl.loop(0, experts)
    def _(p):
        s = nth(p)
        slot = jnp.where(p == 0, 2, p % 2)

        @pl.when(p == 1)
        def _():
            for k in range(1, columns):
                last_copy(k).wait_recv()
                last_on(k).start()

        @pl.when(p == last)
        def _():
            for k in range(1, columns):
                last_on(k).wait_recv()

        grad = jnp.concatenate([grads[q, s] for q in range(quarters)], axis=1)
        d = dot_nt(grad, weight[2])
        own_copy(s).wait_recv()
        for k in range(1, columns):
            pass_copy(s, k).wait_recv()

        @pl.when(p > 1)
        def _():
            after_core(nth(p - 1), (p - 1) % 2)

        @pl.when(p > 2)
        def _():
            send_home(nth(p - 2), p % 2)

        rows = jnp.concatenate([x[q, s] for q in range(quarters)], axis=1)
        gate = read_extra(x[mine, s, cap:], ext)
        a = dot_nt(rows, weight[0])
        b = dot_nt(rows, weight[1])
        d = d * gate
        square = a * a
        t = jnp.tanh(a * (GELU_A + (GELU_A * GELU_B) * square))
        part_on = 0.5 + 0.5 * t
        smooth = a * part_on
        slope = part_on + (a * (0.5 - 0.5 * t * t)) * (GELU_A + (3 * GELU_A * GELU_B) * square)
        active = smooth * b
        da[s] = (d * b * slope).astype(bf16)
        db[s] = (d * smooth).astype(bf16)
        scaled[s] = (active * gate).astype(bf16)
        extra = write_extra(jnp.sum(d * active, axis=1, keepdims=True), part)

        @pl.when((p > 0) & (p + 2 < experts))
        def _():
            z_copy(nth(p + 2)).wait_recv()
            spread(nth(p + 2))

        @pl.when((p > 0) & (p + 1 < experts))
        def _():
            hand_on(nth(p + 1))

        @pl.when((p > 0) & (p + 3 < experts))
        def _():
            z_copy(nth(p + 2)).wait_send()
            z_copy(nth(p + 3)).start()

        for j in range(columns):
            dims = pl.ds(pl.multiple_of(((1 - row) * columns + j) * part, part), part)
            value = dot_nn(da[s], weight[0, :, dims]) + dot_nn(db[s], weight[1, :, dims])
            core_out[s, j] = value.astype(bf16)
            core_out[s, j, cap:] = extra.astype(bf16)
        core_copy(s).start()
        for j in range(columns):
            dims = pl.ds(pl.multiple_of((row * columns + j) * part, part), part)
            keep[slot, j] = dot_nn(da[s], weight[0, :, dims]) + dot_nn(db[s], weight[1, :, dims])
            keep[slot, j, cap:] = extra

        @pl.when(p == 0)
        def _():
            hand_on(nth(1))
            z_copy(nth(2)).wait_send()
            z_copy(nth(3)).start()
            z_copy(nth(2)).wait_recv()
            spread(nth(2))

    def flat(ref, *at):
        block = ref[at] if at else ref[...]
        return block.reshape(experts * ext, block.shape[-1])

    before, final = nth(last - 1), nth(last)
    z_copy(final).wait_send()
    after_core(final, last % 2)
    after_core(0, 2)
    pl.semaphore_signal(free, inc=1, device_id={"row": 1 - row}, device_id_type=MESH)
    send_home(before, (last - 1) % 2)

    pl.semaphore_wait(free, 1)

    @pl.loop(0, experts)
    def _(s):
        core_copy(s).wait_send()
        for j in range(columns):
            dims = pl.ds(pl.multiple_of(((1 - row) * columns + j) * part, part), part)
            core_out[s, j] = dot_nn(scaled[s], weight[2, :, dims]).astype(bf16)
        y_share(s).start()

    def y_far_copy(k):
        return remote(
            core_in.at[nth(1), (col + k) % columns], y_far.at[k - 1], y_far_send.at[k - 1], y_far_recv.at[k - 1],
            {"col": (col + k) % columns},
        )

    @pl.loop(0, experts)
    def _(p):
        s = nth((p + 1) % experts)
        y_share(s).wait_recv()
        for j in range(columns):
            dims = pl.ds(pl.multiple_of((row * columns + j) * part, part), part)
            value = dot_nn(scaled[s], weight[2, :, dims]) + core_in[s, j].astype(f32)
            core_in[s, j] = value.astype(bf16)
        y_copy(s).start()

        @pl.when(p == 0)
        def _():
            for k in range(1, columns):
                y_far_copy(k).start()

    low = flat(scaled)
    for q in range(quarters):
        weight[2, :, q * part : (q + 1) * part] = dot_tn(low, flat(grads, q)).astype(bf16)
    store_gradients(1)
    send_home(final, last % 2)
    for g, hidden in enumerate((da, db)):
        low = flat(hidden)
        for q in range(quarters):
            weight[g, :, q * part : (q + 1) * part] = dot_tn(low, flat(x, q)).astype(bf16)
    store_gradients(0)
    home_ref[0] = after_columns(0, 2)
    wait_gradients(0)
    wait_gradients(1)
    for k in range(1, columns):
        y_far_copy(k).wait()
        last_copy(k).wait_send()
        last_on(k).wait_send()

    @pl.loop(1, experts)
    def _(s):
        home_copy(s).wait_recv()
        home_copy(s).wait_send()

    @pl.loop(0, experts)
    def _(s):
        own_copy(s).wait_send()
        y_share(s).wait_send()
        y_copy(s).wait()
        for k in range(1, columns):
            col_copy(s, k).wait_send()
            pass_copy(s, k).wait_send()
            back_copy(s, k).wait_send()


def expert_block(mixed, slots, gates, shares, share_came, own_grads, own_crossed, came, crossed, columns):
    tokens, part = mixed.shape
    quarters = 2 * columns
    experts, ext, _ = came.shape
    _, ff, wide = shares.shape
    dma = pltpu.SemaphoreType.DMA
    others = columns - 1
    return pl.pallas_call(
        functools.partial(expert_kernel, columns, experts),
        out_shape=(
            jax.ShapeDtypeStruct((experts, ext, part), bf16),
            jax.ShapeDtypeStruct((columns, experts, ext, part), bf16),
            jax.ShapeDtypeStruct((others, ext, part), bf16),
        )
        + (jax.ShapeDtypeStruct((2, ff, wide), bf16), jax.ShapeDtypeStruct((ff, wide), bf16)) * 2,
        in_specs=[vmem()] * 3 + [hbm()] * 6,
        out_specs=(vmem(),) + (hbm(),) * 6,
        scratch_shapes=[
            pltpu.VMEM((quarters, experts, ext, part), bf16),
            pltpu.VMEM((experts, ext, part), bf16),
            pltpu.VMEM((quarters, experts, ext, part), bf16),
            pltpu.VMEM((3, ff, D), bf16),
            pltpu.VMEM((experts, ext, ff), bf16),
            pltpu.VMEM((experts, ext, ff), bf16),
            pltpu.VMEM((experts, ext, ff), bf16),
            pltpu.VMEM((experts, columns, ext, part), bf16),
            pltpu.VMEM((experts, columns, ext, part), bf16),
            pltpu.VMEM((3, columns, ext, part), f32),
            pltpu.VMEM((experts, others, ext, part), bf16),
            pltpu.VMEM((experts, others, ext, part), bf16),
            dma((2,)), dma((experts, columns)), dma((experts, columns)), dma((experts, columns)),
            dma((experts,)), dma((experts,)), dma((experts,)), dma((experts,)),
            dma((experts, others)), dma((experts, others)), dma((experts, others)), dma((experts, others)),
            dma((experts,)), dma((experts,)), dma((experts, others)), dma((experts, others)),
            dma((experts,)), dma((experts,)), dma((experts,)), dma((experts,)), dma((experts,)),
            dma((2,)), dma((2,)), dma((2,)), pltpu.SemaphoreType.REGULAR,
            dma((others,)), dma((others,)), dma((others,)), dma((others,)), dma((others,)), dma((others,)),
            dma((2,)), dma((2,)),
        ],
        compiler_params=pltpu.CompilerParams(
            collective_id=2, has_side_effects=True, vmem_limit_bytes=56 * MIB
        ),
        cost_estimate=microseconds(80),
        name="expert_block",
    )(mixed, slots, gates, shares, share_came, own_grads, own_crossed, came, crossed)


def settle_part(
    columns, experts,
    home_ref, slot_ref, column_ref, second_ref, mixed_ref, cotangent_ref, gain_ref, router_ref,
    branch_ref, two_ref, drouter_ref, dgain_ref,
    low, dmixed_ref, dlogit_ref, stat, stat_in, stat_send, stat_recv, *rest,
):
    *spread_sems, after_spread = rest
    ex = lax.axis_index("ex")
    tokens, part = second_ref.shape
    ext = home_ref.shape[1]
    cap = ext - EXTRA
    size = tokens // PIECES
    lane = lax.broadcasted_iota(jnp.int32, (size, 128), 1)
    extras = []
    for s in range(experts):
        values = read_extra(home_ref[s, cap:], ext)
        near = values.astype(bf16)
        left = (values - near.astype(f32)).astype(bf16)
        extras.append(
            jnp.concatenate([jnp.broadcast_to(near, (ext, 128)), jnp.broadcast_to(left, (ext, 128))], axis=1)
        )
    peers = grid_peers(columns)
    spread = Spread(branch_ref, low, columns, *spread_sems)

    def stat_copy(i, n):
        at = pl.ds(i * size, size)
        return remote(
            stat.at[:, at], stat_in.at[n, :, at], stat_send.at[i, n], stat_recv.at[i, n], peers[n]
        )

    def combine(i):
        at = slice(i * size, (i + 1) * size)
        dmixed = jnp.zeros((size, part), f32)
        gate_grads = jnp.zeros((size, 128), f32)
        for s in range(experts):
            e = (ex + s) % experts
            place = jnp.sum(jnp.where(lane == e, slot_ref[at, :], 0.0), axis=1, keepdims=True)
            hit = place == lax.broadcasted_iota(jnp.int32, (size, ext), 1).astype(f32)
            pick_rows = jnp.where(hit, 1.0, 0.0).astype(bf16)
            dmixed = dmixed + dot_nn(pick_rows, home_ref[s])
            found = dot_nn(pick_rows, extras[s])
            gate_grads = jnp.where(lane == e, found[:, :128] + found[:, 128:], gate_grads)
        gates = jnp.where(lane < experts, column_ref[at, :], 0.0)
        dlogits = gate_grads - gates * jnp.sum(gate_grads, axis=1, keepdims=True)
        dlogit_ref[at, :] = dlogits
        dmixed = dmixed + dot_exact(dlogits[:, : router_ref.shape[0]], router_ref[...], ((1,), (0,)))
        dmixed_ref[at, :] = dmixed
        stat[:, at] = dot_exact(
            jnp.ones((8, part), f32), second_ref[at, :] * dmixed * gain_ref[1:2], ((1,), (1,))
        )
        for n in range(len(peers)):
            stat_copy(i, n).start()

    first_row = jnp.where(lax.broadcasted_iota(jnp.int32, (8, 128), 0) == 0, 1.0, 0.0)

    def close(i):
        at = slice(i * size, (i + 1) * size)
        total = stat[:, at]
        for n in range(len(peers)):
            stat_copy(i, n).wait_recv()
            total = total + stat_in[n, :, at]
        row_total = dot_exact(total, first_row, ((0,), (0,)))[:, :1]
        inverse = column_ref[at, experts : experts + 1]
        two = cotangent_ref[at, :].astype(f32) + inverse * (
            dmixed_ref[at, :] * gain_ref[1:2] - second_ref[at, :] * (inverse * inverse * row_total / D)
        )
        two_ref[at, :] = two
        low[at, :] = two.astype(bf16)
        spread.start_piece(i)

    for i in reversed(range(PIECES)):
        combine(i)
        if i + 1 < PIECES:
            close(i + 1)
            if i + 2 < PIECES:
                spread.hand_on_piece(i + 2)
    close(0)
    after_spread()

    def sums():
        rows = drouter_ref.shape[0]
        drouter_ref[...] = dot_exact(dlogit_ref[...], mixed_ref[...].astype(f32), ((0,), (0,)))[:rows]
        normed = second_ref[...] * column_ref[:, experts : experts + 1]
        dgain_ref[...] = jnp.broadcast_to(
            jnp.sum(dmixed_ref[...] * normed, axis=0, keepdims=True), dgain_ref.shape
        )

    for i in range(PIECES):
        for n in range(len(peers)):
            stat_copy(i, n).wait_send()
    return spread, sums


def finish_part(
    columns, experts,
    dfirst_ref, dweight_ref, small, layer_ref, two_ref, gain_ref, inverse_ref,
    placed_grad, qkv_grad_ref, proj_grad_ref, sums_ref,
    core_in, keep, col_out, col_in, stat, stat_in, y_in, z_out, z_in, held, row_out, row_in, small_in,
    core_send, core_recv, col_send, col_recv, stat_send, stat_recv,
    y_send, y_recv, z_send, z_recv, row_send, row_recv, small_send, small_recv, others_meanwhile, while_waiting,
):
    ex, half = lax.axis_index("ex"), lax.axis_index("half")
    row, col = lax.axis_index("row"), lax.axis_index("col")
    tokens, part = layer_ref.shape
    size = tokens // PIECES
    members = 2 * experts
    rows = held.shape[1]
    hc = held.shape[2] // 4

    def core_copy(i):
        at = pl.ds(i * size, size)
        return remote(
            dfirst_ref.at[pl.ds((1 - row) * columns, columns), at], core_in.at[:, at],
            core_send.at[i], core_recv.at[i], {"row": 1 - row},
        )

    def block_of(member, a):
        return pl.ds(pl.multiple_of((a * members + member) * rows, rows), rows)

    def y_copy(s, a):
        to = 2 * ((ex + s) % experts) + 1 - half
        return remote(
            dweight_ref.at[block_of(to, a)], y_in.at[s, a], y_send.at[s, a], y_recv.at[s, a], {"half": 1 - half}
        )

    def z_copy(s, a):
        return remote(
            z_out.at[s, a], z_in.at[s, a], z_send.at[s, a], z_recv.at[s, a], {"ex": (ex + s) % experts}
        )

    queue = [(s, a) for s in nearest_first(experts)[::-1] + [0] for a in range(2)]

    def col_copy(i, k):
        at = pl.ds(i * size, size)
        return remote(
            col_out.at[k - 1, at], col_in.at[k - 1, at], col_send.at[i, k - 1], col_recv.at[i, k - 1],
            {"col": (col + k) % columns},
        )

    def start(i):
        core_copy(i).start()

    def cross(i):
        at = slice(i * size, (i + 1) * size)
        core_copy(i).wait_recv()
        for j in range(columns):
            keep[j, at] = dfirst_ref[row * columns + j, at].astype(f32) + core_in[j, at].astype(f32)
        for k in range(1, columns):
            col_out[k - 1, at] = keep[(col + k) % columns, at].astype(bf16)
            col_copy(i, k).start()

    def normed():
        return layer_ref[...].astype(f32) * inverse_ref[:, 127:128]

    peers = grid_peers(columns)

    def stat_copy(n):
        return remote(stat, stat_in.at[n], stat_send.at[n], stat_recv.at[n], peers[n])

    def arrive():
        for i in range(PIECES):
            for k in range(1, columns):
                col_copy(i, k).wait_recv()
        dnorm = keep[col]
        for k in range(1, columns):
            dnorm = dnorm + col_in[k - 1].astype(f32)
        keep[col] = dnorm
        stat[...] = dot_exact(
            jnp.ones((8, part), f32), layer_ref[...].astype(f32) * (dnorm * gain_ref[:1]), ((1,), (1,))
        )
        for n in range(len(peers)):
            stat_copy(n).start()
        small[:8] = jnp.broadcast_to(jnp.sum(dnorm * normed(), axis=0, keepdims=True), (8, part))
        small_over_y.start()

    small_over_y = remote(small, small_in.at[0], small_send.at[0], small_recv.at[0], {"half": 1 - half})
    pair = small_in.at[experts]

    def small_over_z(s):
        return remote(pair, small_in.at[s], small_send.at[s], small_recv.at[s], {"ex": (ex + s) % experts})

    def close():
        small_over_y.wait_recv()
        small_in[experts] = small[...] + small_in[0]
        for s in range(1, experts):
            small_over_z(s).start()
        total = stat[...]
        for n in range(len(peers)):
            stat_copy(n).wait_recv()
            total = total + stat_in[n]
        first_row = jnp.where(lax.broadcasted_iota(jnp.int32, (8, 128), 0) == 0, 1.0, 0.0)
        row_total = dot_exact(total, first_row, ((0,), (0,)))[:, :1]
        inverse = inverse_ref[:, 127:128]
        placed_grad[...] = (
            two_ref[...] + inverse * (keep[col] * gain_ref[:1] - normed() * (inverse * row_total / D))
        ).astype(bf16)

    def rest():
        for at in queue[:2]:
            y_copy(*at).start()
        cross(0)
        others_meanwhile()
        for n, (s, a) in enumerate(queue):
            y_copy(s, a).wait_send()
            if n + 2 < len(queue):
                y_copy(*queue[n + 2]).start()
            y_copy(s, a).wait_recv()
            own = dweight_ref[block_of(2 * ((ex + s) % experts) + half, a), :]
            total = own.astype(f32) + y_in[s, a].astype(f32)
            if s > 0:
                z_out[s, a] = total.astype(bf16)
                z_copy(s, a).start()
            else:
                held[a] = total
            if n == 2:
                arrive()
            if n == 4:
                close()
        while_waiting()
        for s in nearest_first(experts)[::-1]:
            for a in range(2):
                z_copy(s, a).wait_recv()
                held[a] = held[a] + z_in[s, a].astype(f32)
        row_out[...] = held[1 - row].astype(bf16)
        swap = remote(row_out, row_in, row_send.at[0], row_recv.at[0], {"row": 1 - row})
        swap.start()
        sums = small_in[experts]
        for s in range(1, experts):
            small_over_z(s).wait_recv()
            sums = sums + small_in[s]
        sums_ref[...] = sums
        swap.wait_recv()
        for at_row, values in ((row, held[row]), (1 - row, row_in[...].astype(f32))):
            proj_grad_ref[at_row] = values[:, 3 * hc :]
            for k in range(3):
                qkv_grad_ref[:, k, at_row, :] = values[:, k * hc : (k + 1) * hc]
        swap.wait_send()
        small_over_y.wait_send()
        for s in range(1, experts):
            small_over_z(s).wait_send()
        for n in range(len(peers)):
            stat_copy(n).wait_send()
        for i in range(PIECES):
            core_copy(i).wait_send()
            for k in range(1, columns):
                col_copy(i, k).wait_send()
        for s, a in queue:
            if s > 0:
                z_copy(s, a).wait_send()

    return start, cross, rest


def tail_kernel(columns, experts, *refs):
    (
        home_ref, slot_ref, column_ref, second_ref, mixed_ref, cotangent_ref, gain_two, router_ref,
        qkv_ref, lse_ref, attended_ref, first_ref, weight_ref, place_row, length_ref, vector_ref,
        layer_ref, gain_one, y_hbm, y_far, away_up, away_down,
    ) = refs[:22]
    layer_out_ref, input_grad_ref, qkv_grad_ref, proj_grad_ref, sums_ref, came_up, came_down = refs[22:29]
    scratch = list(refs[29:])

    def take(count):
        taken = scratch[:count]
        del scratch[:count]
        return taken

    branch_ref, two_ref, drouter_ref, dgain_ref, dfirst_ref, dweight_ref, dvector_ref, small = take(8)
    y_own, y_in, y_home = take(3)
    y_load, y_send, y_recv, y_away, y_came, half_send, half_recv = take(7)
    y_far_in, placed_out, placed_grad = take(3)
    settle_scratch = take(7 + 6)
    attention_scratch = take(5)
    finish_scratch = take(13 + 14)
    ex, half, col = lax.axis_index("ex"), lax.axis_index("half"), lax.axis_index("col")
    greet(
        grid_peers(columns)
        + [{"ex": (ex + s) % experts} for s in range(1, experts)]
        + [{"half": 1 - half}]
    )

    halves = [
        remote(source, out, half_send.at[i], half_recv.at[i], {"half": 1 - half})
        for i, (source, out) in enumerate(((away_up, came_up), (away_down, came_down)))
    ]
    for copy in halves:
        copy.start()

    far, *near = farthest_first(experts)
    y_stay = pltpu.make_async_copy(y_hbm.at[col], y_own, y_load.at[0])
    y_stay.start()
    y_far_load = pltpu.make_async_copy(y_far, y_far_in, y_load.at[1])
    y_far_load.start()

    def y_cross(s, k):
        to = (col + k) % columns
        return remote(
            y_hbm.at[to, s], y_in.at[s, k - 1], y_send.at[s, k - 1], y_recv.at[s, k - 1], {"col": to}
        )

    def y_copy(s):
        return remote(
            y_own.at[s], y_home.at[s], y_away.at[s], y_came.at[s], {"ex": (ex - s + experts) % experts}
        )

    def y_sum(s, others):
        total = y_own[s].astype(f32)
        for other in others:
            total = total + other.astype(f32)
        if s > 0:
            y_own[s] = total.astype(bf16)
            y_copy(s).start()
        else:
            y_home[0] = total.astype(bf16)

    def y_homeward(s):
        for k in range(1, columns):
            y_cross(s, k).wait_recv()
        y_sum(s, [y_in[s, k - 1] for k in range(1, columns)])

    def after_spread():
        for s in near + [0]:
            for k in range(1, columns):
                y_cross(s, k).start()

    y_stay.wait()
    y_far_load.wait()
    y_sum(far, [y_far_in[k - 1] for k in range(1, columns)])
    spread, settle_sums = settle_part(
        columns, experts,
        home_ref, slot_ref, column_ref, second_ref, mixed_ref, cotangent_ref, gain_two, router_ref,
        branch_ref, two_ref, drouter_ref, dgain_ref, *settle_scratch, after_spread,
    )
    ways = near + [0]
    tokens, part = second_ref.shape
    stat_rows = drouter_ref.shape[0]

    def others_meanwhile():
        settle_sums()
        bias_sums(attention_scratch[1], dvector_ref)
        small[8:16] = dgain_ref[...]
        small[16 : 16 + stat_rows] = drouter_ref[...]
        pieces = 2 * TILE // part
        for i in range(dvector_ref.shape[0]):
            for n in range(pieces):
                at = 16 + stat_rows + i * pieces + n
                small[at : at + 1] = dvector_ref[i : i + 1, n * part : (n + 1) * part]

    def while_waiting():
        for s in range(1, experts):
            y_copy(s).wait_recv()
        ext = y_own.shape[1]
        size = tokens // PIECES
        lane = lax.broadcasted_iota(jnp.int32, (size, 128), 1)
        for i in range(PIECES):
            at = slice(i * size, (i + 1) * size)
            total = second_ref[at, :]
            for s in range(experts):
                place = jnp.sum(jnp.where(lane == (ex + s) % experts, slot_ref[at, :], 0.0), axis=1, keepdims=True)
                hit = place == lax.broadcasted_iota(jnp.int32, (size, ext), 1).astype(f32)
                total = total + dot_nn(jnp.where(hit, 1.0, 0.0).astype(bf16), y_home[s])
            placed_out[at, :] = total.astype(bf16)
        to_given = given_table(place_row, tokens)
        layer_out_ref[...] = dot_nn(to_given, placed_out[...]).astype(bf16)
        input_grad_ref[...] = dot_nn(to_given, placed_grad[...]).astype(bf16)

    start, cross, rest = finish_part(
        columns, experts,
        dfirst_ref, dweight_ref, small, layer_ref, two_ref, gain_one, lse_ref,
        placed_grad, qkv_grad_ref, proj_grad_ref, sums_ref, *finish_scratch, others_meanwhile, while_waiting,
    )

    def before(a):
        if a + 1 == PIECES:
            spread.hand_on_piece(1)
        elif a == 2:
            spread.hand_on_piece(0)
        spread.wait_piece(a)

    def after(a):
        start(a)
        if a + 1 < PIECES:
            cross(a + 1)
        if a == 0:
            while ways:
                y_homeward(ways.pop(0))
        elif a + 2 < PIECES and len(ways) > 1:
            y_homeward(ways.pop(0))

    attention_backward_kernel(
        branch_ref, qkv_ref, lse_ref, attended_ref, first_ref, weight_ref, length_ref, vector_ref,
        dfirst_ref, dweight_ref, dvector_ref, *attention_scratch, before, after,
    )
    rest()
    spread.wait_sends()
    for copy in halves:
        copy.wait()
    for s in near + [0]:
        for k in range(1, columns):
            y_cross(s, k).wait_send()
    for s in range(1, experts):
        y_copy(s).wait_send()


def tail(
    home, slots, table, second, mixed, cotangent, gain_two, router_rows,
    qkv, lse, attended, first, weight, placing, lengths, vectors, layer_in, gain_one, y, y_far, away_up, away_down,
    stat_rows, experts, columns,
):
    tokens, part = second.shape
    quarters, others = 2 * columns, columns - 1
    hc = weight.shape[1] // 4
    ext = home.shape[1]
    rows, width = D // (4 * experts), 4 * hc
    small = (16 + stat_rows + vectors.size // part, part)
    dma = pltpu.SemaphoreType.DMA
    return pl.pallas_call(
        functools.partial(tail_kernel, columns, experts),
        out_shape=(
            jax.ShapeDtypeStruct((tokens, part), bf16),
            jax.ShapeDtypeStruct((tokens, part), bf16),
            jax.ShapeDtypeStruct((rows, 3, 2, hc), f32),
            jax.ShapeDtypeStruct((2, rows, hc), f32),
            jax.ShapeDtypeStruct(small, f32),
            jax.ShapeDtypeStruct(away_up.shape, bf16),
            jax.ShapeDtypeStruct(away_down.shape, bf16),
        ),
        in_specs=[vmem()] * 14 + [pl.BlockSpec(memory_space=pltpu.SMEM)] + [vmem()] * 3 + [hbm()] * 4,
        out_specs=(vmem(),) * 5 + (hbm(),) * 2,
        scratch_shapes=[
            pltpu.VMEM((quarters, tokens, part), bf16),
            pltpu.VMEM((tokens, part), f32),
            pltpu.VMEM((stat_rows, part), f32),
            pltpu.VMEM((8, part), f32),
            pltpu.VMEM((quarters, tokens, part), bf16),
            pltpu.VMEM((D, width), bf16),
            pltpu.VMEM(vectors.shape, f32),
            pltpu.VMEM(small, f32),
            pltpu.VMEM((experts, ext, part), bf16),
            pltpu.VMEM((experts, others, ext, part), bf16),
            pltpu.VMEM((experts, ext, part), bf16),
            dma((2,)), dma((experts, others)), dma((experts, others)), dma((experts,)), dma((experts,)), dma((2,)), dma((2,)),
            pltpu.VMEM((others, ext, part), bf16),
            pltpu.VMEM((tokens, part), bf16),
            pltpu.VMEM((tokens, part), bf16),
            pltpu.VMEM((tokens, part), bf16),
            pltpu.VMEM((tokens, part), f32),
            pltpu.VMEM((tokens, 128), f32),
            pltpu.VMEM((8, tokens), f32),
            pltpu.VMEM((quarters - 1, 8, tokens), f32),
            dma((PIECES, quarters - 1)), dma((PIECES, quarters - 1)),
        ]
        + spread_semaphores(columns)
        + [
            pltpu.VMEM((vectors.shape[0], TILE, TILE), f32),
            pltpu.VMEM((vectors.shape[0], TILE, TILE), f32),
            pltpu.VMEM((tokens, hc), bf16),
            pltpu.VMEM((tokens, 3 * hc), bf16),
            pltpu.VMEM((tokens, 2 * hc), f32),
            pltpu.VMEM((columns, tokens, part), bf16),
            pltpu.VMEM((columns, tokens, part), f32),
            pltpu.VMEM((others, tokens, part), bf16),
            pltpu.VMEM((others, tokens, part), bf16),
            pltpu.VMEM((8, tokens), f32),
            pltpu.VMEM((quarters - 1, 8, tokens), f32),
            pltpu.VMEM((experts, 2, rows, width), bf16),
            pltpu.VMEM((experts, 2, rows, width), bf16),
            pltpu.VMEM((experts, 2, rows, width), bf16),
            pltpu.VMEM((2, rows, width), f32),
            pltpu.VMEM((rows, width), bf16),
            pltpu.VMEM((rows, width), bf16),
            pltpu.VMEM((experts + 1,) + small, f32),
            dma((PIECES,)), dma((PIECES,)), dma((PIECES, others)), dma((PIECES, others)),
            dma((quarters - 1,)), dma((quarters - 1,)),
            dma((experts, 2)), dma((experts, 2)), dma((experts, 2)), dma((experts, 2)),
            dma((1,)), dma((1,)), dma((experts,)), dma((experts,)),
        ],
        compiler_params=pltpu.CompilerParams(
            collective_id=3, has_side_effects=True, vmem_limit_bytes=47 * MIB
        ),
        cost_estimate=microseconds(90),
        name="tail",
    )(
        home, slots, table, second, mixed, cotangent, gain_two, router_rows,
        qkv, lse, attended, first, weight, placing, lengths, vectors, layer_in, gain_one, y, y_far, away_up, away_down,
    )


def adamw_step(weight, grad, first, second, rate):
    first_new = beta_first * first + (1.0 - beta_first) * grad
    second_new = beta_second * second + (1.0 - beta_second) * grad * grad
    moment = first_new / (1.0 - beta_first**STEP)
    spread = second_new / (1.0 - beta_second**STEP)
    weight_new = weight - rate * (
        moment / (jnp.sqrt(spread) + adam_epsilon) + weight_decay * weight
    )
    return (weight_new, first_new, second_new)


def local(
    layer_in, lengths, placing, routes, cotangent,
    norm_gains, gain_first, gain_second, rel_bias, bias_first, bias_second,
    router, router_first, router_second, qkv_weight, qkv_first, qkv_second,
    proj_weight, proj_first, proj_second, expert_up, up_first, up_second,
    expert_down, down_first, down_second,
):
    tokens, part = layer_in.shape
    experts, columns = lax.axis_size("ex"), lax.axis_size("col")
    quarters = 2 * columns
    cap = min(tokens, 5 * TOP * tokens // (4 * experts))
    ext = cap + EXTRA
    hc = qkv_weight.shape[5]
    head_count = hc // HD
    wide = D // 2

    qkv_low = jnp.moveaxis(qkv_weight[0, 0].astype(bf16), 1, 0).reshape(2, -1, 3 * hc)
    proj_low = jnp.swapaxes(proj_weight[:, :, 0, 0].astype(bf16), 1, 2)
    shard = jnp.concatenate([qkv_low, proj_low], axis=2)
    stat_rows = (experts + 8) // 8 * 8
    ff = expert_down.shape[1]
    shares = jnp.concatenate(
        [jnp.transpose(expert_up[0], (1, 2, 0)).reshape(2 * ff, wide).astype(bf16), expert_down[0].astype(bf16)]
    ).reshape(3, ff, wide)
    vectors = bias_vectors(rel_bias, tokens)
    router_rows = jnp.pad(router.T, ((0, stat_rows - experts), (0, 0)))
    x_all, gains_all, weight, slot_rows, slot_columns, own_crossed, placed, placed_cot, *grad_rows = gather(
        layer_in, norm_gains, shard, placing, routes.T, cotangent, stat_rows, ext, experts, columns
    )
    weight = weight.reshape(D, 4 * hc)
    first, qkv, attended, lse, second, table, mixed, gates, came, crossed, share_came = attend(
        x_all, gains_all, weight, lengths, vectors, placed, norm_gains, router_rows, slot_rows, shares,
        grad_rows, columns,
    )
    home, y, y_far, keep_up, keep_down, away_up, away_down = expert_block(
        mixed, slot_rows, gates, shares, share_came, grad_rows[0], own_crossed, came, crossed, columns
    )
    layer_out, input_grad, grad_qkv, grad_proj, sums, came_up, came_down = tail(
        home, slot_columns, table, second, mixed, placed_cot, norm_gains,
        router_rows, qkv, lse, attended, first, weight, placing, lengths, vectors, placed, norm_gains,
        y, y_far, away_up, away_down, stat_rows, experts, columns,
    )
    grad_gains = jnp.stack([sums[0], sums[8]])
    grad_router = sums[16 : 16 + experts].T
    grad_bias = bias_gradient(sums[16 + stat_rows :].reshape(vectors.shape), head_count, tokens)
    grad_qkv = jnp.swapaxes(grad_qkv, 1, 2).reshape(qkv_weight.shape)
    grad_proj = jnp.swapaxes(grad_proj, 1, 2).reshape(proj_weight.shape)
    grad_up = jnp.transpose(keep_up.astype(f32) + came_up.astype(f32), (2, 0, 1))[None]
    grad_down = (keep_down.astype(f32) + came_down.astype(f32))[None]
    ups = adamw_step(expert_up, grad_up, up_first, up_second, 2.0 * D ** (-0.5))
    downs = adamw_step(expert_down, grad_down, down_first, down_second, 2.0 * (FF / 2) ** (-0.5))
    gains = adamw_step(norm_gains, grad_gains, gain_first, gain_second, 0.5)
    bias = adamw_step(rel_bias, grad_bias, bias_first, bias_second, 1.0)
    routers = adamw_step(router, grad_router, router_first, router_second, 2.0 * (2 * D) ** (-0.5))
    qkvs = adamw_step(qkv_weight, grad_qkv, qkv_first, qkv_second, 2.0 * D ** (-0.5))
    projs = adamw_step(proj_weight, grad_proj, proj_first, proj_second, 2.0 * (HEADS * HD / 8) ** (-0.5))
    out = (layer_out, input_grad) + gains + bias + routers
    for group in (qkvs, projs, ups, downs):
        out = out + group + (group[0].astype(bf16),)
    return out


def solution(mesh):
    shape = mesh.devices.shape
    fine = Mesh(
        mesh.devices.reshape((shape[0] // 2, 2) + shape[1:]), ("ex", "half", "row", "col")
    )
    dp, grid = ("ex", "half"), ("row", "col")
    tokens, own = P(dp, grid), P(dp, None)
    gain, router = P(None, grid), P(grid, None)
    qkv, proj = P("row", dp, None, None, None, "col"), P(None, "col", "row", dp, None)
    up, down = P(dp, "row", None, "col"), P(dp, "col", "row")
    in_specs = (
        (tokens, own, own, own, tokens) + (gain,) * 6 + (router,) * 3
        + (qkv,) * 3 + (proj,) * 3 + (up,) * 3 + (down,) * 3
    )
    out_specs = (
        (tokens, tokens) + (gain,) * 6 + (router,) * 3
        + (qkv,) * 4 + (proj,) * 4 + (up,) * 4 + (down,) * 4
    )
    return jax.shard_map(local, mesh=fine, in_specs=in_specs, out_specs=out_specs, check_vma=False)
```
